32 devices in a mesh: ctx: 4 (over z), exp: 8 (over y, x, core).
Axes of the slice: x: 2, y: 2, z: 4, core: 2. Of those that a mesh axis runs over, the one named last changes fastest.
Arguments:
- block_input: bfloat16 [2, 4096, 2048], P(None, ('ctx', 'exp')), may hold values from -16 to 16
- attend_gain: float32 [2048], replicated, may hold values from 0.5 to 1.5
- w_query: bfloat16 [2048, 2048], P(None, 'exp'), may hold values from -0.125 to 0.125
- w_key: bfloat16 [2048, 2048], P(None, 'exp'), may hold values from -0.125 to 0.125
- w_value: bfloat16 [2048, 2048], P(None, 'exp'), may hold values from -0.125 to 0.125
- w_out: bfloat16 [2048, 2048], P('exp'), may hold values from -1.5 to 1.5
- query_gain: float32 [2048], P('exp'), may hold values from 0.5 to 1.5
- key_gain: float32 [2048], P('exp'), may hold values from 0.5 to 1.5
- expert_gain: float32 [2048], replicated, may hold values from 0.5 to 1.5
- router: bfloat16 [2048, 16], replicated, may hold values from -1 to 1
- expert_weights: bfloat16 [2048, 16, 3, 1024], P(None, 'exp'), may hold values from -0.375 to 0.375
- routes: int32 [4096, 2, 8], P(('ctx', 'exp')), may hold values from 0 to 15, all different within a row; in each aligned block of 256 rows (0 to 255, 256 to 511, ..., all dimensions but the last counted through in order) at most 256 rows name the same one
- cotangent: bfloat16 [2, 4096, 2048], P(None, ('ctx', 'exp')), may hold values from -6 to 6
Outputs:
- block_output: bfloat16 [2, 4096, 2048], P(None, ('ctx', 'exp'))
- input_grad: float32 [2, 4096, 2048], P(None, ('ctx', 'exp'))
- attend_grad: float32 [2048], P('exp')
- query_grad: float32 [2048, 2048], P(None, 'exp')
- key_grad: float32 [2048, 2048], P(None, 'exp')
- value_grad: float32 [2048, 2048], P(None, 'exp')
- out_grad: float32 [2048, 2048], P('exp')
- qgain_grad: float32 [2048], P('exp')
- kgain_grad: float32 [2048], P('exp')
- egain_grad: float32 [2048], P('exp')
- router_grad: float32 [2048, 16], P('exp')
- expert_grad: float32 [2048, 16, 3, 1024], P('ctx', 'exp')
The draws below stay inside these ranges and needn't reach their ends.
Inputs may be any that keep to these rules, and one draw needn't show every extreme that they name: `routes`: each token names 8 different experts; the tokens of one device (an aligned block of 256 rows, row first) name each expert at most 256 times.
All inputs are finite; a program needn't handle non-finite values.
Results may differ from the reference program's by a relative error of at most 0.02.
Values may be sent and summed in bfloat16 or wider, within the bound.
No kernel may reach another device: no remote copies, remote signals or barrier semaphores. Data moves between devices by JAX's collectives and lax.ppermute only.
A program may use at most 384 MiB of HBM per device.

```python
import math
from functools import partial
import jax
import jax.numpy as jnp
import numpy as np
from jax import lax

D = 2048
HEADS = 16
HD = 128
FFE = 1024
TOP = 8
SEQS = 2
SEQ_DEV = 1024
EXPERTS = 16
SEQ_LEN = 4096
TOK_DEV = 256
CAP = 256
N_CTX = 4
N_EXP = 8


def draw_block_input(key, part):
    noise_key = jax.random.fold_in(jax.random.fold_in(key, 1), 0)
    full_shape = (SEQS, SEQ_LEN, D)
    values = jax.random.normal(noise_key, full_shape, jnp.float32)
    return jnp.clip(values, -16.0, 16.0).astype(jnp.bfloat16)


def draw_router(key, part):
    base_key = jax.random.fold_in(key, 2)
    spread = 0.5 / math.sqrt(D)
    base_vals = jnp.clip(jax.random.normal(base_key, (D, EXPERTS), jnp.float32), -6.0, 6.0) * spread
    return jnp.clip(base_vals, -1.0, 1.0).astype(jnp.bfloat16)


def draw_query_gain(key, part):
    gain_key = jax.random.fold_in(key, 3)
    gain_vals = jax.random.uniform(gain_key, (D,), jnp.float32, 0.6, 1.4)
    return gain_vals


def draw_key_gain(key, part):
    gain_key = jax.random.fold_in(key, 4)
    gain_vals = jax.random.uniform(gain_key, (D,), jnp.float32, 0.6, 1.4)
    return gain_vals


def steps_of(key, extent, shards, smallest, largest):
    def one(axis_at, parts):
        heights = jax.random.uniform(jax.random.fold_in(jax.random.fold_in(key, 6), axis_at), (parts,), jnp.float32, smallest / len(shards), largest / len(shards))
        return jnp.repeat(jnp.exp(heights), extent[axis_at] // parts).reshape((-1,) + (1,) * (len(extent) - axis_at - 1))

    loudness = one(*shards[0])
    for cut in shards[1:]:
        loudness = loudness * one(*cut)
    return loudness


def shared_out(own_key, own, number, rows, count, top, bound, lean):
    order = jax.random.permutation(own_key, count)
    heavy_load, common = portions_of(count, rows * top, bound, lean, True), portions_of(count, rows * top, bound, lean, False)
    places = jnp.arange(count)

    def named(sizes, turn):
        used = int((sizes > 0).sum())
        fixed = max(1, used // 4)
        shifted = fixed + (places - fixed + turn * (used - fixed)) % max(1, count - fixed)
        return jnp.zeros((count,), jnp.int32).at[order[jnp.where(places < fixed, places, shifted)]].set(jnp.asarray(sizes, jnp.int32))

    sizes = jnp.where(number % 4 == 0, named(heavy_load, number // 4), named(common, number - number // 4 - 1))
    mixed = jax.random.permutation(jax.random.fold_in(own, 3), count)
    donor, taker = mixed[0:count // 2 * 2:2], mixed[1:count // 2 * 2:2]
    margin = jnp.minimum(sizes[donor] - 1, bound - sizes[taker]) // 2
    margin = jnp.where((donor == order[0]) | (taker == order[0]) | (sizes[taker] == 0), 0, jnp.maximum(margin, 0))
    shifted = jax.random.randint(jax.random.fold_in(own, 4), (count // 2,), 0, 1 << 20) % (margin + 1)
    sizes = sizes.at[donor].add(-shifted).at[taker].add(shifted)
    labels = jnp.searchsorted(jnp.cumsum(sizes), jnp.arange(rows * top), side="right").astype(jnp.int32)
    table = labels.reshape(top, rows).T
    table = table[jax.random.permutation(jax.random.fold_in(own, 1), rows)]
    turn = jax.random.randint(jax.random.fold_in(own, 2), (rows, 1), 0, top)
    return jnp.take_along_axis(table, (jnp.arange(top)[None, :] + turn) % top, axis=1)


def portions_of(number_of, total, most, skew, full):
    weights = [(1 << 20) // math.isqrt(grade ** skew) + 1 for grade in range(1, number_of + 1)]
    largest = most if full else min(most, max(-(-total // number_of), total * weights[0] // sum(weights)))
    least = 1 if total - largest >= number_of - 1 else 0
    counts, surplus = [largest] + [least] * (number_of - 1), total - largest - least * (number_of - 1)
    while surplus > 0:
        movable = [i for i in range(1, number_of) if counts[i] < largest] or [i for i in range(1, number_of) if counts[i] < most]
        whole, left = sum([weights[i] for i in movable]), surplus
        for i in movable:
            more = min(most - counts[i], max(1, left * weights[i] // whole), surplus)
            counts[i] = counts[i] + more
            surplus = surplus - more
    return np.array(counts)


def normal_values(rng, shape, scale, most, pieces=(), kind=jnp.bfloat16):
    drawn = jax.random.normal(rng, shape, jnp.float32) * scale
    if len(pieces) > 0:
        drawn = steps_of(rng, shape, pieces, -0.22, 0.18) * drawn
    return jnp.clip(drawn, min=-most, max=most).astype(kind)


def setup_inputs(seed: int = 0) -> dict:
    key_of = jax.random.split(jax.random.key(seed), 14)
    block_input = draw_block_input(jax.random.fold_in(key_of[13], 71), 0)
    attend_gain = jnp.clip(1.0 + 0.1 * jax.random.normal(key_of[1], (D,), jnp.float32), 0.5, 1.5)
    w_query = normal_values(key_of[2], (D, D), D ** -0.5, 0.125, ((1, 8),))
    w_key = normal_values(key_of[3], (D, D), D ** -0.5, 0.125, ((1, 8),))
    w_value = normal_values(key_of[4], (D, D), D ** -0.5, 0.125, ((1, 8),))
    w_out = normal_values(key_of[5], (D, D), 16 ** -0.5, 1.5, ((0, 8),))
    query_gain = draw_query_gain(jax.random.fold_in(key_of[13], 71), 0)
    key_gain = draw_key_gain(jax.random.fold_in(key_of[13], 71), 0)
    expert_gain = jnp.clip(1.0 + 0.1 * jax.random.normal(key_of[8], (D,), jnp.float32), 0.5, 1.5)
    router = draw_router(jax.random.fold_in(key_of[13], 71), 0)
    expert_weights = normal_values(key_of[10], (D, EXPERTS, 3, FFE), (D // 8) ** -0.5, 0.375, ((1, 8),))
    routes_keys = jax.random.split(jax.random.fold_in(key_of[11], 1), SEQ_LEN * SEQS // TOK_DEV)
    routes_turns = jax.random.permutation(jax.random.fold_in(key_of[11], 3), SEQ_LEN * SEQS // TOK_DEV)
    routes = jax.vmap(lambda own, number: shared_out(jax.random.fold_in(key_of[11], 2), own, number, TOK_DEV, EXPERTS, TOP, CAP, 2))(routes_keys, routes_turns).reshape((SEQ_LEN, SEQS, TOP))
    cotangent = normal_values(key_of[12], (SEQS, SEQ_LEN, D), 1.0, 6.0, ((1, 32),))
    return {"block_input": block_input, "attend_gain": attend_gain, "w_query": w_query, "w_key": w_key, "w_value": w_value, "w_out": w_out, "query_gain": query_gain, "key_gain": key_gain, "expert_gain": expert_gain, "router": router, "expert_weights": expert_weights, "routes": routes, "cotangent": cotangent}


@jax.custom_vjp
def low(v):
    return lax.optimization_barrier(v.astype(jnp.bfloat16)).astype(jnp.float32)

@jax.custom_vjp
def low_back(v):
    return v

def low_keep(v):
    return (low(v), None)

def low_pass(kept, grad):
    return (grad,)

def back_keep(v):
    return (v, None)

def back_low(kept, grad):
    return (low(grad),)
low.defvjp(low_keep, low_pass)
low_back.defvjp(back_keep, back_low)
norm_eps = 1e-05
rope_base = 10000.0
masked_score = -1e+30

def matmul(operand, other):
    return jnp.dot(operand, other, precision=lax.Precision.HIGHEST, preferred_element_type=jnp.float32)

def rms_factor(values):
    return lax.rsqrt(lax.optimization_barrier(jnp.mean(values * values, axis=-1, keepdims=True)) + norm_eps)

def position_map(length):
    row_ids = jnp.arange(length, dtype=jnp.int32)
    share = length // N_CTX
    half_rows = share // 2
    owner = row_ids // share
    within = row_ids % share
    return jnp.where(within < half_rows, owner * half_rows + within, (2 * N_CTX - 1 - owner) * half_rows + within - half_rows).astype(jnp.int32)

def rotary_tables(positions, head_size):
    half_size = head_size // 2
    inverse_freq = rope_base ** (-(jnp.arange(half_size, dtype=jnp.float32) * 2.0) / head_size)
    angles = positions.astype(jnp.float32)[:, None] * inverse_freq[None, :]
    angles = jnp.concatenate([angles, angles], axis=1)
    return (jnp.cos(angles), jnp.sin(angles))

def rotate(values, cosine, sines):
    half_size = values.shape[-1] // 2
    turned = jnp.concatenate([-values[..., half_size:], values[..., :half_size]], axis=-1)
    return values * cosine[:, None, :] + turned * sines[:, None, :]

def attend(rows, attend_gain, w_query, w_key, w_value, w_out, query_gain, key_gain):
    length = rows.shape[0]
    unit_rows = rows * rms_factor(rows)
    normed = low(unit_rows * attend_gain)
    queries = low_back(matmul(normed, w_query))
    keys_proj = low_back(matmul(normed, w_key))
    values_low = low_back(low(matmul(normed, w_value)))
    query_unit = queries * rms_factor(queries)
    key_unit = keys_proj * rms_factor(keys_proj)
    positions = position_map(length)
    cosine, sines = rotary_tables(positions, HD)
    query_rot = low(rotate((query_unit * query_gain).reshape(length, HEADS, HD), cosine, sines))
    key_rot = low(rotate((key_unit * key_gain).reshape(length, HEADS, HD), cosine, sines))
    value_heads = values_low.reshape(length, HEADS, HD)
    block_len = math.gcd(length, 512)

    def one_block(first_row):
        query_block = lax.dynamic_slice_in_dim(query_rot, first_row, block_len, 0)
        scores = jnp.einsum('qhd,khd->hqk', query_block, key_rot, precision=lax.Precision.HIGHEST) * (1.0 / math.sqrt(HD))
        scores = low_back(scores)
        query_pos = lax.dynamic_slice_in_dim(positions, first_row, block_len, 0)
        scores = jnp.where(positions[None, None, :] <= query_pos[None, :, None], scores, masked_score)
        soft_probs = low(jax.nn.softmax(scores, axis=-1))
        return jnp.einsum('hqk,khd->qhd', soft_probs, value_heads, precision=lax.Precision.HIGHEST)
    starts = jnp.arange(length // block_len, dtype=jnp.int32) * block_len
    blocks = lax.map(jax.checkpoint(one_block), starts)
    attended = low_back(low(blocks.reshape(length, HEADS * HD)))
    return low_back(matmul(attended, w_out))

def forward(block_input, attend_gain, w_query, w_key, w_value, w_out, query_gain, key_gain, expert_gain, router, expert_weights, routes, slot_table):

    def sequence_branch(rows):
        return attend(rows, attend_gain, w_query, w_key, w_value, w_out, query_gain, key_gain)
    branch = lax.map(sequence_branch, block_input)
    hidden = block_input + branch
    unit_second = hidden * rms_factor(hidden)
    mixed_in = low(unit_second * expert_gain).reshape(-1, D)
    logits = low_back(matmul(mixed_in, router))
    choice_prob = jax.nn.softmax(logits, axis=-1)
    gate_vals = jnp.take_along_axis(choice_prob, routes.reshape(-1, TOP), axis=1).reshape(-1)
    sentinel = gate_vals.shape[0]

    def expert_step(totals, inputs):
        index_row, weights = inputs
        usable = (index_row < sentinel).astype(jnp.float32)
        safe_index = jnp.minimum(index_row, sentinel - 1)
        token_row = safe_index // TOP
        row_data = low_back(mixed_in[token_row] * usable[:, None])
        pre_gate = low_back(matmul(row_data, weights[:, 0, :]))
        pre_up = low_back(matmul(row_data, weights[:, 1, :]))
        middle = low(jax.nn.silu(pre_gate) * pre_up)
        produced = low_back(low(matmul(middle, weights[:, 2, :].T)))
        return (totals.at[token_row].add(produced * (gate_vals[safe_index] * usable)[:, None]), None)
    mixture, unused = lax.scan(jax.checkpoint(expert_step), jnp.zeros(mixed_in.shape, jnp.float32), (slot_table, jnp.moveaxis(expert_weights, 1, 0)))
    return hidden + mixture.reshape(hidden.shape)

def reference(block_input, attend_gain, w_query, w_key, w_value, w_out, query_gain, key_gain, expert_gain, router, expert_weights, routes, cotangent):
    shard_len = SEQ_DEV // N_EXP
    devices_all = N_CTX * N_EXP
    per_device = routes.reshape(devices_all, shard_len * SEQS * TOP).astype(jnp.int32)
    hot = (per_device[:, :, None] == jnp.arange(EXPERTS, dtype=jnp.int32)[None, None, :]).astype(jnp.int32)
    earlier = jnp.cumsum(hot, axis=1) - hot
    slot_flat = lax.optimization_barrier(jnp.sum(earlier * hot, axis=-1)).astype(jnp.int32)
    slots_seq = jnp.transpose(slot_flat.reshape(SEQ_LEN, SEQS, TOP), (1, 0, 2))
    routes_seq = jnp.transpose(routes, (1, 0, 2)).astype(jnp.int32)
    flat_routes = routes_seq.reshape(-1)
    device_of = jnp.broadcast_to((jnp.arange(SEQ_LEN, dtype=jnp.int32) // shard_len)[None, :, None], routes_seq.shape).reshape(-1)
    buffer_pos = (device_of * CAP + slots_seq.reshape(-1)).astype(jnp.int32)
    count_all = flat_routes.shape[0]
    slot_table = jnp.full((EXPERTS, devices_all * CAP), count_all, jnp.int32).at[flat_routes, buffer_pos].set(jnp.arange(count_all, dtype=jnp.int32))
    primal = (block_input.astype(jnp.float32), attend_gain, w_query.astype(jnp.float32), w_key.astype(jnp.float32), w_value.astype(jnp.float32), w_out.astype(jnp.float32), query_gain, key_gain, expert_gain, router.astype(jnp.float32), expert_weights.astype(jnp.float32))
    result, pullback = jax.vjp(partial(forward, routes=routes_seq, slot_table=slot_table), *primal)
    gradients = pullback(cotangent.astype(jnp.float32))
    return (result.astype(jnp.bfloat16), gradients[0], gradients[1], gradients[2], gradients[3], gradients[4], gradients[5], gradients[6], gradients[7], gradients[8], gradients[9], gradients[10])
```

```python
import functools
import math

import jax
import jax.numpy as jnp
from jax import lax
from jax.experimental import pallas as pl
from jax.experimental.pallas import tpu as pltpu
from jax.sharding import PartitionSpec as P

HD = 128
TOP = 8


norm_eps = 1e-05
rope_base = 10000.0
masked_score = -1e30
LOG2E = 1.4426950408889634
F32 = jnp.float32
BF16 = jnp.bfloat16


def rms_factor(values):
    return lax.rsqrt(jnp.mean(values * values, axis=-1, keepdims=True) + norm_eps)


def rotary_tables(positions, head_size):
    half_size = head_size // 2
    inverse_freq = rope_base ** (-(jnp.arange(half_size, dtype=F32) * 2.0) / head_size)
    angles = positions.astype(F32)[:, None] * inverse_freq[None, :]
    angles = jnp.concatenate([angles, angles], axis=1)
    return (jnp.cos(angles), jnp.sin(angles))


def turn(values):
    half_size = values.shape[-1] // 2
    return jnp.concatenate([-values[..., half_size:], values[..., :half_size]], axis=-1)


def turn_back(values):
    half_size = values.shape[-1] // 2
    return jnp.concatenate([values[..., half_size:], -values[..., :half_size]], axis=-1)


def dot32(a, b):
    return jnp.dot(a, b, preferred_element_type=F32)


def flip(values, axis, mask):
    return lax.ppermute(values, axis, [(i, i ^ mask) for i in range(lax.axis_size(axis))])


def pick(values, index, axis=0):
    return lax.dynamic_index_in_dim(values, index, axis, keepdims=False)


def butterfly_sum(values, axis):
    mask = 1
    while mask < lax.axis_size(axis):
        values = jax.tree.map(lambda v: v + flip(v, axis, mask), values)
        mask *= 2
    return values


def reduce_rows(partial, own=None):
    count = partial.shape[0]
    me = lax.axis_index("exp")
    core, chip = me % 2, me // 2
    pairs = partial.reshape((count // 2, 2) + partial.shape[1:])
    got = flip(pick(pairs, 1 - core, 1), "exp", 1)
    mine = pick(pairs, core, 1)
    both = (mine.astype(F32) + got.astype(F32)).astype(BF16)
    parts = [flip(pick(both, chip ^ m), "exp", 2 * m) for m in range(1, count // 2)]
    total = pick(mine, chip).astype(F32) + pick(got, chip).astype(F32)
    for part in parts:
        total = total + part.astype(F32)
    return total


def block_place(block, ctx_count, place):
    late = block >= ctx_count
    owner = jnp.where(late, 2 * ctx_count - 1 - block, block)
    return owner ^ place, jnp.where(late, 1, 0)


def causal_mask(rows):
    key_line = lax.broadcasted_iota(jnp.int32, (rows, rows), 0)
    query_line = lax.broadcasted_iota(jnp.int32, (rows, rows), 1)
    return key_line <= query_line


def attend_kernel(place_ref, qk_ref, v_ref, o_ref, ot_ref, lse_ref, qt_ref, vt_ref):
    ctx_count, rows = v_ref.shape[0], v_ref.shape[1] // 2
    blocks = 2 * ctx_count
    place = place_ref[0]
    scale = LOG2E / math.sqrt(HD)

    def lay(block, unused):
        slab, half = block_place(block, ctx_count, place)
        at = pl.ds(pl.multiple_of(half * rows, rows), rows)
        to = pl.ds(pl.multiple_of(block * rows, rows), rows)
        qt_ref[:, to] = qk_ref[slab, 0, at, :].T
        vt_ref[:, to] = v_ref[slab, at, :].T
        return unused

    lax.fori_loop(0, blocks, lay, 0)

    def query_block(block, unused):
        cols = pl.ds(pl.multiple_of(block * rows, rows), rows)
        query = qt_ref[:, cols]

        def part(key_block, carried, masked):
            high, total, acc = carried
            slab, half = block_place(key_block, ctx_count, place)
            at = pl.ds(pl.multiple_of(half * rows, rows), rows)
            scores = dot32(qk_ref[slab, 1, at, :], query) * scale
            if masked:
                scores = jnp.where(causal_mask(rows), scores, masked_score)
            new_high = jnp.maximum(high, jnp.max(scores, axis=0, keepdims=True))
            probs = jnp.exp2(scores - new_high)
            fade = jnp.exp2(high - new_high)
            total = total * fade + jnp.sum(probs, axis=0, keepdims=True)
            keys = pl.ds(pl.multiple_of(key_block * rows, rows), rows)
            acc = acc * fade + dot32(vt_ref[:, keys], probs.astype(BF16))
            return new_high, total, acc

        start = (
            jnp.full((1, rows), masked_score, F32),
            jnp.zeros((1, rows), F32),
            jnp.zeros((HD, rows), F32),
        )
        state = part(block, start, True)
        high, total, acc = lax.fori_loop(0, block, lambda j, c: part(j, c, False), state)
        out = acc / total
        ot_ref[:, cols] = out
        slab, half = block_place(block, ctx_count, place)
        o_ref[slab, pl.ds(pl.multiple_of(half * rows, rows), rows), :] = out.T.astype(BF16)
        lse_ref[block] = high + jnp.log2(total)
        return unused

    lax.fori_loop(0, blocks, query_block, 0)


def attend_back_kernel(
    place_ref, qk_ref, v_ref, do_ref, ot_ref, lse_ref, d_ref, qt_ref, kt_ref, dot_ref, dk_ref, dv_ref
):
    ctx_count, rows = v_ref.shape[0], v_ref.shape[1] // 2
    blocks = 2 * ctx_count
    place = place_ref[0]
    score_scale = 1.0 / math.sqrt(HD)
    scale = LOG2E * score_scale

    def lay(block, unused):
        slab, half = block_place(block, ctx_count, place)
        at = pl.ds(pl.multiple_of(half * rows, rows), rows)
        to = pl.ds(pl.multiple_of(block * rows, rows), rows)
        qt_ref[:, to] = qk_ref[slab, 0, at, :].T
        kt_ref[:, to] = qk_ref[slab, 1, at, :].T
        dot_ref[:, to] = do_ref[slab, at, :].T
        dk_ref[to, :] = jnp.zeros((rows, HD), F32)
        dv_ref[to, :] = jnp.zeros((rows, HD), F32)
        return unused

    lax.fori_loop(0, blocks, lay, 0)

    def query_block(block, unused):
        cols = pl.ds(pl.multiple_of(block * rows, rows), rows)
        slab_q, half_q = block_place(block, ctx_count, place)
        at_q = pl.ds(pl.multiple_of(half_q * rows, rows), rows)
        query_t, grad_t = qt_ref[:, cols], dot_ref[:, cols]
        delta = jnp.sum(grad_t.astype(F32) * ot_ref[:, cols], axis=0, keepdims=True)
        lse = lse_ref[block]

        def part(key_block, dq, masked):
            slab, half = block_place(key_block, ctx_count, place)
            at = pl.ds(pl.multiple_of(half * rows, rows), rows)
            keys = pl.ds(pl.multiple_of(key_block * rows, rows), rows)
            probs = jnp.exp2(dot32(qk_ref[slab, 1, at, :], query_t) * scale - lse)
            if masked:
                probs = jnp.where(causal_mask(rows), probs, 0.0)
            grad_probs = dot32(v_ref[slab, at, :], grad_t)
            grad_scores = (probs * (grad_probs - delta)).astype(BF16)
            dv_ref[keys, :] += dot32(probs.astype(BF16), do_ref[slab_q, at_q, :])
            dk_ref[keys, :] += dot32(grad_scores, qk_ref[slab_q, 0, at_q, :])
            return dq + dot32(kt_ref[:, keys], grad_scores)

        dq = part(block, jnp.zeros((HD, rows), F32), True)
        dq = lax.fori_loop(0, block, lambda j, c: part(j, c, False), dq)
        d_ref[slab_q, 0, at_q, :] = (dq * score_scale).T.astype(BF16)
        return unused

    lax.fori_loop(0, blocks, query_block, 0)

    def give(block, unused):
        slab, half = block_place(block, ctx_count, place)
        at = pl.ds(pl.multiple_of(half * rows, rows), rows)
        to = pl.ds(pl.multiple_of(block * rows, rows), rows)
        d_ref[slab, 1, at, :] = (dk_ref[to, :] * score_scale).astype(BF16)
        d_ref[slab, 2, at, :] = dv_ref[to, :].astype(BF16)
        return unused

    lax.fori_loop(0, blocks, give, 0)


VMEM = pl.BlockSpec(memory_space=pltpu.VMEM)
SMEM = pl.BlockSpec(memory_space=pltpu.SMEM)


def attend_call(place, qk, v):
    ctx_count, ctx_rows = v.shape[0], v.shape[1]
    length, rows = ctx_count * ctx_rows, ctx_rows // 2
    pairs = length * length // 2
    return pl.pallas_call(
        attend_kernel,
        out_shape=(
            jax.ShapeDtypeStruct(v.shape, BF16),
            jax.ShapeDtypeStruct((HD, length), F32),
            jax.ShapeDtypeStruct((2 * ctx_count, 1, rows), F32),
        ),
        in_specs=[SMEM, VMEM, VMEM],
        out_specs=(VMEM, VMEM, VMEM),
        scratch_shapes=[pltpu.VMEM((HD, length), BF16), pltpu.VMEM((HD, length), BF16)],
        compiler_params=pltpu.CompilerParams(vmem_limit_bytes=50 * 2**20),
        cost_estimate=pl.CostEstimate(
            flops=8 * pairs * HD, bytes_accessed=12 * length * HD, transcendentals=pairs
        ),
        name="attend",
    )(place, qk, v)


def attend_back_call(place, qk, v, grads, out_t, lse):
    ctx_count, ctx_rows = v.shape[0], v.shape[1]
    length = ctx_count * ctx_rows
    pairs = length * length // 2
    return pl.pallas_call(
        attend_back_kernel,
        out_shape=jax.ShapeDtypeStruct((ctx_count, 3, ctx_rows, HD), BF16),
        in_specs=[SMEM] + [VMEM] * 5,
        out_specs=VMEM,
        scratch_shapes=[pltpu.VMEM((HD, length), BF16)] * 3 + [pltpu.VMEM((length, HD), F32)] * 2,
        compiler_params=pltpu.CompilerParams(vmem_limit_bytes=50 * 2**20),
        cost_estimate=pl.CostEstimate(
            flops=20 * pairs * HD, bytes_accessed=18 * length * HD, transcendentals=pairs
        ),
        name="attend_back",
    )(place, qk, v, grads, out_t, lse)


def spread_pairs(values):
    count = values.shape[0]
    place = lax.axis_index("ctx")
    parts = [pick(values, place ^ m) for m in range(count)]
    return jnp.stack([parts[0]] + [flip(parts[m], "ctx", m) for m in range(1, count)])


def return_pairs(values):
    count = values.shape[0]
    place = lax.axis_index("ctx")
    parts = jnp.stack([values[0]] + [flip(values[m], "ctx", m) for m in range(1, count)])
    return jnp.stack([pick(parts, place ^ p) for p in range(count)])


def paired_forward(queries, keys_proj, values_low, query_gain, key_gain, cosine, sines, model_width):
    exp_count, seq_count, shard_len, local_width = queries.shape
    local_heads = local_width // HD
    ctx_rows = exp_count * shard_len

    def by_pair(values):
        values = values.reshape(exp_count, seq_count, shard_len, local_heads, HD)
        return jnp.transpose(values, (1, 3, 0, 2, 4)).reshape(-1, ctx_rows, HD)

    v_all = spread_pairs(by_pair(values_low))
    squares = jnp.stack(
        [jnp.sum(queries * queries, axis=-1), jnp.sum(keys_proj * keys_proj, axis=-1)]
    )
    squares = butterfly_sum(squares, "exp")
    factors = lax.rsqrt(squares[..., None] / model_width + norm_eps)
    query_unit = queries * factors[0]
    key_unit = keys_proj * factors[1]

    def rotated(values):
        pairs = by_pair(values)
        return (pairs * cosine + turn(pairs) * sines).astype(BF16)

    rotated_qk = jnp.stack([rotated(query_unit * query_gain), rotated(key_unit * key_gain)], axis=1)
    qk_all = spread_pairs(rotated_qk)
    place = lax.axis_index("ctx").astype(jnp.int32).reshape(1)
    out, out_t, lse = attend_call(place, qk_all, v_all)
    attended = return_pairs(out)
    return attended, (place, qk_all, v_all, out_t, lse, query_unit, key_unit, factors)


def paired_backward(kept, grads, query_gain, key_gain, cosine, sines, model_width):
    place, qk_all, v_all, out_t, lse, query_unit, key_unit, factors = kept
    exp_count, seq_count, shard_len, local_width = query_unit.shape
    local_heads = local_width // HD
    back = attend_back_call(place, qk_all, v_all, spread_pairs(grads), out_t, lse)
    back = return_pairs(back)

    def by_row(values):
        values = values.reshape(seq_count, local_heads, exp_count, shard_len, HD)
        return jnp.transpose(values, (2, 0, 3, 1, 4)).reshape(query_unit.shape)

    def unrotated(values):
        values = values.astype(F32)
        return by_row(values * cosine + turn_back(values) * sines)

    qnorm_grad, knorm_grad = unrotated(back[:, 0]), unrotated(back[:, 1])
    grad_values = by_row(back[:, 2])
    qgain_part = jnp.sum(qnorm_grad * query_unit, axis=(0, 1, 2))
    kgain_part = jnp.sum(knorm_grad * key_unit, axis=(0, 1, 2))
    qunit_grad = qnorm_grad * query_gain
    kunit_grad = knorm_grad * key_gain
    dots = jnp.stack(
        [jnp.sum(qunit_grad * query_unit, axis=-1), jnp.sum(kunit_grad * key_unit, axis=-1)]
    )
    dots = butterfly_sum(dots, "exp")[..., None] / model_width
    grad_queries = (factors[0] * (qunit_grad - query_unit * dots[0])).astype(BF16)
    grad_keys = (factors[1] * (kunit_grad - key_unit * dots[1])).astype(BF16)
    return jnp.concatenate([grad_queries, grad_keys, grad_values], axis=-1), qgain_part, kgain_part


def gathered_forward(queries, keys_proj, values_low, query_gain, key_gain, cosine, sines, model_width):
    exp_count, seq_count, shard_len, local_width = queries.shape
    ctx_count, ctx_place = lax.axis_size("ctx"), lax.axis_index("ctx")
    local_heads = local_width // HD
    ctx_rows = exp_count * shard_len
    half_rows = ctx_rows // 2
    squares = jnp.stack(
        [jnp.sum(queries * queries, axis=-1), jnp.sum(keys_proj * keys_proj, axis=-1)]
    )
    squares = lax.psum(squares, "exp")
    factors = lax.rsqrt(squares[..., None] / model_width + norm_eps)
    query_unit = queries * factors[0]
    key_unit = keys_proj * factors[1]

    def heads(values):
        values = values.reshape(exp_count, seq_count, shard_len, local_heads, HD)
        return jnp.transpose(values, (1, 0, 2, 3, 4)).reshape(seq_count, ctx_rows, local_heads, HD)

    def rotated(values):
        values = heads(values)
        return (values * cosine[:, None, :] + turn(values) * sines[:, None, :]).astype(BF16)

    query_rot = rotated(query_unit * query_gain)
    keys_all = lax.all_gather(rotated(key_unit * key_gain), "ctx", axis=1, tiled=True)
    values_all = lax.all_gather(heads(values_low), "ctx", axis=1, tiled=True)
    tools = block_tools(half_rows, ctx_count, ctx_place)
    block_len, half_firsts, row_start, block_scores = tools
    attended_halves = []
    log_halves = []
    for half_index in range(2):
        query_half = query_rot[:, half_index * half_rows : (half_index + 1) * half_rows]
        query_first = half_firsts[half_index]
        needed_blocks = (query_first + half_rows) // block_len

        def step(counter, carried):
            running_max, running_sum, acc = carried
            key_first = counter * block_len
            start_row = row_start(key_first)
            key_block = lax.dynamic_slice_in_dim(keys_all, start_row, block_len, 1)
            value_block = lax.dynamic_slice_in_dim(values_all, start_row, block_len, 1)
            scores = block_scores(query_half, query_first, key_block, key_first)
            new_max = jnp.maximum(running_max, jnp.max(scores, axis=-1))
            fade = jnp.exp(running_max - new_max)
            probs = jnp.exp(scores - new_max[..., None])
            running_sum = running_sum * fade + jnp.sum(probs, axis=-1)
            acc = acc * jnp.transpose(fade, (0, 2, 1))[..., None] + jnp.einsum(
                "shqk,skhd->sqhd", probs.astype(BF16), value_block, preferred_element_type=F32
            )
            return (new_max, running_sum, acc)

        stat_shape = (seq_count, local_heads, half_rows)
        running_max, running_sum, acc = lax.fori_loop(
            0,
            needed_blocks,
            step,
            (
                jnp.full(stat_shape, masked_score, F32),
                jnp.zeros(stat_shape, F32),
                jnp.zeros((seq_count, half_rows, local_heads, HD), F32),
            ),
        )
        attended_halves.append(acc / jnp.transpose(running_sum, (0, 2, 1))[..., None])
        log_halves.append(running_max + jnp.log(running_sum))
    attended_float = jnp.concatenate(attended_halves, axis=1)
    attended = jnp.transpose(attended_float.astype(BF16), (0, 2, 1, 3)).reshape(-1, ctx_rows, HD)
    kept = (
        query_rot, keys_all, values_all, attended_float, log_halves, query_unit, key_unit, factors
    )
    return attended, kept


def block_tools(half_rows, ctx_count, ctx_place):
    block_len = math.gcd(half_rows, 512)
    far_first = (2 * ctx_count - 1 - ctx_place) * half_rows
    half_firsts = (ctx_place * half_rows, far_first)

    def row_start(first_pos):
        segment = first_pos // half_rows
        offset = first_pos % half_rows
        return jnp.where(
            segment < ctx_count,
            segment * 2 * half_rows + offset,
            (2 * ctx_count - 1 - segment) * 2 * half_rows + half_rows + offset,
        )

    def block_scores(query_block, query_first, key_block, key_first):
        scores = jnp.einsum("sqhd,skhd->shqk", query_block, key_block, preferred_element_type=F32)
        scores = scores * (1.0 / math.sqrt(HD))
        query_line = query_first + jnp.arange(query_block.shape[1], dtype=jnp.int32)
        key_line = key_first + jnp.arange(key_block.shape[1], dtype=jnp.int32)
        return jnp.where(key_line[None, :] <= query_line[:, None], scores, masked_score)

    return block_len, half_firsts, row_start, block_scores


def gathered_backward(kept, grads, query_gain, key_gain, cosine, sines, model_width):
    query_rot, keys_all, values_all, attended_float, log_halves, query_unit, key_unit, factors = kept
    exp_count, seq_count, shard_len, local_width = query_unit.shape
    ctx_count, ctx_place = lax.axis_size("ctx"), lax.axis_index("ctx")
    local_heads = local_width // HD
    ctx_rows = exp_count * shard_len
    half_rows = ctx_rows // 2
    seq_len = keys_all.shape[1]
    score_scale = 1.0 / math.sqrt(HD)
    block_len, half_firsts, row_start, block_scores = block_tools(half_rows, ctx_count, ctx_place)
    grad_heads = jnp.transpose(
        grads.reshape(seq_count, local_heads, ctx_rows, HD), (0, 2, 1, 3)
    )
    delta_rows = jnp.transpose(jnp.sum(grad_heads.astype(F32) * attended_float, axis=-1), (0, 2, 1))
    keyval_grads = jnp.zeros((seq_count, seq_len, 2 * local_width), F32)
    query_halves = []
    for half_index in range(2):
        row_slice = slice(half_index * half_rows, (half_index + 1) * half_rows)
        query_half = query_rot[:, row_slice]
        grad_half = grad_heads[:, row_slice]
        delta_half = delta_rows[:, :, row_slice]
        log_total = log_halves[half_index]
        query_first = half_firsts[half_index]
        needed_blocks = (query_first + half_rows) // block_len

        def one_block(counter, inner):
            query_acc, keyval_acc = inner
            key_first = counter * block_len
            start_row = row_start(key_first)
            key_block = lax.dynamic_slice_in_dim(keys_all, start_row, block_len, 1)
            value_block = lax.dynamic_slice_in_dim(values_all, start_row, block_len, 1)
            scores = block_scores(query_half, query_first, key_block, key_first)
            soft_probs = jnp.exp(scores - log_total[..., None])
            grad_probs = jnp.einsum(
                "sqhd,skhd->shqk", grad_half, value_block, preferred_element_type=F32
            )
            grad_scores = (soft_probs * (grad_probs - delta_half[..., None])).astype(BF16)
            query_acc = query_acc + score_scale * jnp.einsum(
                "shqk,skhd->sqhd", grad_scores, key_block, preferred_element_type=F32
            )
            kblock_grad = score_scale * jnp.einsum(
                "shqk,sqhd->skhd", grad_scores, query_half, preferred_element_type=F32
            )
            vblock_grad = jnp.einsum(
                "shqk,sqhd->skhd", soft_probs.astype(BF16), grad_half, preferred_element_type=F32
            )
            flat = (seq_count, block_len, local_width)
            combined = jnp.concatenate([kblock_grad.reshape(flat), vblock_grad.reshape(flat)], -1)
            keyval_acc = lax.dynamic_update_slice_in_dim(
                keyval_acc,
                lax.dynamic_slice_in_dim(keyval_acc, start_row, block_len, 1) + combined,
                start_row,
                1,
            )
            return (query_acc, keyval_acc)

        query_acc, keyval_grads = lax.fori_loop(
            0,
            needed_blocks,
            one_block,
            (jnp.zeros((seq_count, half_rows, local_heads, HD), F32), keyval_grads),
        )
        query_halves.append(query_acc)
    query_back = jnp.concatenate(query_halves, axis=1)
    keyval_local = lax.psum_scatter(keyval_grads, "ctx", scatter_dimension=1, tiled=True)

    def by_row(values):
        values = values.reshape(seq_count, exp_count, shard_len, local_width)
        return jnp.transpose(values, (1, 0, 2, 3))

    def unrotated(values):
        values = values.reshape(seq_count, ctx_rows, local_heads, HD)
        return by_row(values * cosine[:, None, :] + turn_back(values) * sines[:, None, :])

    qnorm_grad = unrotated(query_back)
    knorm_grad = unrotated(keyval_local[..., :local_width])
    grad_values = by_row(keyval_local[..., local_width:].astype(BF16))
    qgain_part = jnp.sum(qnorm_grad * query_unit, axis=(0, 1, 2))
    kgain_part = jnp.sum(knorm_grad * key_unit, axis=(0, 1, 2))
    qunit_grad = qnorm_grad * query_gain
    kunit_grad = knorm_grad * key_gain
    dots = jnp.stack(
        [jnp.sum(qunit_grad * query_unit, axis=-1), jnp.sum(kunit_grad * key_unit, axis=-1)]
    )
    dots = lax.psum(dots, "exp")[..., None] / model_width
    grad_queries = (factors[0] * (qunit_grad - query_unit * dots[0])).astype(BF16)
    grad_keys = (factors[1] * (kunit_grad - key_unit * dots[1])).astype(BF16)
    return jnp.concatenate([grad_queries, grad_keys, grad_values], axis=-1), qgain_part, kgain_part


def body(
    block_input,
    attend_gain,
    w_query,
    w_key,
    w_value,
    w_out,
    query_gain,
    key_gain,
    expert_gain,
    router,
    expert_weights,
    routes,
    cotangent,
):
    exp_count, ctx_count = lax.axis_size("exp"), lax.axis_size("ctx")
    ctx_place, exp_place = lax.axis_index("ctx"), lax.axis_index("exp")
    seq_count, shard_len, model_width = block_input.shape
    local_width = w_query.shape[1]
    local_heads = local_width // HD
    experts_all = router.shape[1]
    experts_here = expert_weights.shape[1]
    hidden_units = expert_weights.shape[3]
    rows_dev = seq_count * shard_len
    rows_all = exp_count * rows_dev
    ctx_rows = exp_count * shard_len
    half_rows = ctx_rows // 2
    pair_count = seq_count * local_heads
    paired = pair_count == ctx_count and half_rows % 128 == 0

    def gather(values):
        return lax.all_gather(values, "exp", axis=0, tiled=False)

    local_float = block_input.astype(F32).reshape(rows_dev, model_width)
    local_factor = rms_factor(local_float)
    local_unit = local_float * local_factor
    normed = gather((local_unit * attend_gain).astype(BF16)).reshape(rows_all, model_width)
    all_routes = gather(jnp.transpose(routes, (1, 0, 2)).reshape(rows_dev, TOP))
    all_routes = all_routes.reshape(rows_all, TOP)
    grad_low = gather(cotangent.reshape(rows_dev, model_width)).reshape(rows_all, model_width)
    full_out = gather(w_out).reshape(exp_count * local_width, model_width)
    w_qkv = jnp.concatenate([w_query, w_key, w_value], axis=1)
    full_qkv = gather(w_qkv.T).reshape(exp_count * 3 * local_width, model_width)
    w_gate, w_up, w_down = (
        jnp.concatenate([expert_weights[:, e, k, :] for e in range(experts_here)], axis=1)
        for k in range(3)
    )

    projected = dot32(normed, w_qkv).reshape(exp_count, seq_count, shard_len, 3 * local_width)
    row_ids = jnp.arange(ctx_rows, dtype=jnp.int32)
    far_first = (2 * ctx_count - 1 - ctx_place) * half_rows
    query_pos = jnp.where(
        row_ids < half_rows, ctx_place * half_rows + row_ids, far_first + row_ids - half_rows
    )
    cosine, sines = rotary_tables(query_pos, HD)
    forward, backward = (
        (paired_forward, paired_backward) if paired else (gathered_forward, gathered_backward)
    )
    attended, kept = forward(
        projected[..., :local_width],
        projected[..., local_width : 2 * local_width],
        projected[..., 2 * local_width :].astype(BF16),
        query_gain,
        key_gain,
        cosine,
        sines,
        model_width,
    )

    def exchange(values):
        return lax.all_to_all(values, "exp", split_axis=0, concat_axis=0, tiled=True)

    sent = jnp.transpose(attended.reshape(pair_count, exp_count, shard_len, HD), (1, 0, 2, 3))
    own = exchange(sent).reshape(exp_count, seq_count, local_heads, shard_len, HD)
    own_attended = jnp.transpose(own, (1, 3, 0, 2, 4)).reshape(rows_dev, exp_count * local_width)
    hidden = local_float + dot32(own_attended, full_out)
    hidden_factor = rms_factor(hidden)
    unit_second = hidden * hidden_factor
    own_mixed = (unit_second * expert_gain).astype(BF16)

    expert_ids = jnp.arange(experts_all, dtype=jnp.int32)

    def chosen(table):
        return jnp.any(table[:, :, None] == expert_ids[None, None, :], axis=1)

    own_prob = jax.nn.softmax(dot32(own_mixed, router), axis=-1)
    own_routes = jnp.transpose(routes, (1, 0, 2)).reshape(rows_dev, TOP)
    own_chosen = chosen(own_routes)

    mixed = gather(own_mixed).reshape(rows_all, model_width)
    all_prob = jax.nn.softmax(dot32(mixed, router), axis=-1)
    all_gates = jnp.where(chosen(all_routes), all_prob, 0.0)
    gates = lax.dynamic_slice_in_dim(all_gates, exp_place * experts_here, experts_here, 1)
    gates = gates[:, :, None]

    wide = (rows_all, experts_here, hidden_units)
    grad_down = dot32(grad_low, w_down).reshape(wide)
    pre_gate = dot32(mixed, w_gate).reshape(wide)
    pre_up = dot32(mixed, w_up).reshape(wide)
    sigmoid_vals = jax.nn.sigmoid(pre_gate)
    activated = pre_gate * sigmoid_vals
    middle = activated * pre_up
    gate_grads = jnp.sum(middle * grad_down, axis=-1)
    grad_middle = gates * grad_down
    flat = (rows_all, experts_here * hidden_units)
    gated_middle = (gates * middle).astype(BF16).reshape(flat)
    grad_gate = grad_middle * pre_up * sigmoid_vals * (1.0 + pre_gate * (1.0 - sigmoid_vals))
    grad_gate = grad_gate.astype(BF16).reshape(flat)
    grad_up = (grad_middle * activated).astype(BF16).reshape(flat)

    def weight_term(rows, grads):
        term = jnp.einsum("rd,rf->df", rows, grads, preferred_element_type=F32).astype(BF16)
        return lax.psum_scatter(term, "ctx", scatter_dimension=0, tiled=True)

    down_term = weight_term(grad_low, gated_middle)
    gate_term = weight_term(mixed, grad_gate)
    up_term = weight_term(mixed, grad_up)
    expert_grad = jnp.stack(
        [
            t.astype(F32).reshape(t.shape[0], experts_here, hidden_units)
            for t in (gate_term, up_term, down_term)
        ],
        axis=2,
    )

    slot_rows = jnp.einsum("rf,df->rd", grad_gate, w_gate, preferred_element_type=F32)
    slot_rows = slot_rows + jnp.einsum("rf,df->rd", grad_up, w_up, preferred_element_type=F32)
    slot_sum = reduce_rows(slot_rows.astype(BF16).reshape(exp_count, rows_dev, model_width))
    expert_out = jnp.einsum("rf,df->rd", gated_middle, w_down, preferred_element_type=F32)
    mixture = reduce_rows(expert_out.astype(BF16).reshape(exp_count, rows_dev, model_width))
    block_output = (hidden + mixture).astype(BF16).reshape(block_input.shape)

    choice_grad = exchange(gate_grads.reshape(exp_count, rows_dev, experts_here))
    choice_grad = jnp.transpose(choice_grad, (1, 0, 2)).reshape(rows_dev, experts_all)
    choice_grad = jnp.where(own_chosen, choice_grad, 0.0)
    logit_grad = (
        own_prob * (choice_grad - jnp.sum(own_prob * choice_grad, axis=-1, keepdims=True))
    ).astype(BF16)
    router_part = jnp.einsum("td,te->de", own_mixed, logit_grad, preferred_element_type=F32)
    mixed_grad = slot_sum + jnp.einsum(
        "te,de->td", logit_grad, router, preferred_element_type=F32
    )
    egain_part = jnp.sum(mixed_grad * unit_second, axis=0)
    usecond_grad = mixed_grad * expert_gain
    grad_rows = cotangent.astype(F32).reshape(rows_dev, model_width)
    grad_hidden = (
        hidden_factor
        * (usecond_grad - unit_second * jnp.mean(usecond_grad * unit_second, axis=-1, keepdims=True))
        + grad_rows
    )
    own_branch = grad_hidden.astype(BF16)

    grad_attended = jnp.einsum(
        "rd,hd->rh", own_branch, full_out, preferred_element_type=F32
    ).astype(BF16)
    sent = grad_attended.reshape(seq_count, shard_len, exp_count, local_heads, HD)
    sent = jnp.transpose(sent, (2, 0, 3, 1, 4)).reshape(exp_count, pair_count, shard_len, HD)
    grads = jnp.transpose(exchange(sent), (1, 0, 2, 3)).reshape(pair_count, ctx_rows, HD)
    grad_qkv, qgain_part, kgain_part = backward(
        kept, grads, query_gain, key_gain, cosine, sines, model_width
    )
    own_qkv = exchange(grad_qkv.reshape(exp_count, rows_dev, 3 * local_width))
    own_qkv = jnp.transpose(own_qkv, (1, 0, 2)).reshape(rows_dev, exp_count * 3 * local_width)
    grad_normed = dot32(own_qkv, full_qkv)
    attend_part = jnp.sum(grad_normed * local_unit, axis=0)
    lunit_grad = grad_normed * attend_gain
    input_grad = grad_hidden + local_factor * (
        lunit_grad - local_unit * jnp.mean(lunit_grad * local_unit, axis=-1, keepdims=True)
    )

    branch_rows = gather(own_branch).reshape(exp_count, seq_count, shard_len, model_width)
    attended_rows = attended.reshape(seq_count, local_heads, exp_count, shard_len, HD)
    outw_part = jnp.einsum(
        "shetc,estd->hcd", attended_rows, branch_rows, preferred_element_type=F32
    ).reshape(local_width, model_width)
    out_grad = lax.psum(outw_part.astype(BF16), "ctx").astype(F32)
    qkv_part = jnp.einsum(
        "rd,rh->dh", normed, grad_qkv.reshape(rows_all, -1), preferred_element_type=F32
    )
    qkv_grad = lax.psum(qkv_part.astype(BF16), "ctx").astype(F32)
    attend_sum, egain_sum, router_sum = (
        lax.psum_scatter(part, "exp", scatter_dimension=0, tiled=True)
        for part in (attend_part, egain_part, router_part)
    )
    attend_sum, egain_sum, router_sum, qgain_grad, kgain_grad = lax.psum(
        (attend_sum, egain_sum, router_sum, qgain_part, kgain_part), "ctx"
    )
    return (
        block_output,
        input_grad.reshape(block_input.shape),
        attend_sum,
        qkv_grad[:, :local_width],
        qkv_grad[:, local_width : 2 * local_width],
        qkv_grad[:, 2 * local_width :],
        out_grad,
        qgain_grad,
        kgain_grad,
        egain_sum,
        router_sum,
        expert_grad,
    )


def solution(mesh):
    placed = (
        P(None, ("ctx", "exp"), None),
        P(),
        P(None, "exp"),
        P(None, "exp"),
        P(None, "exp"),
        P("exp", None),
        P("exp"),
        P("exp"),
        P(),
        P(),
        P(None, "exp", None, None),
        P(("ctx", "exp"), None, None),
        P(None, ("ctx", "exp"), None),
    )
    return jax.shard_map(
        body,
        mesh=mesh,
        in_specs=placed,
        out_specs=(
            P(None, ("ctx", "exp"), None),
            P(None, ("ctx", "exp"), None),
            P("exp"),
            P(None, "exp"),
            P(None, "exp"),
            P(None, "exp"),
            P("exp", None),
            P("exp"),
            P("exp"),
            P("exp"),
            P("exp", None),
            P("ctx", "exp", None, None),
        ),
        check_vma=False,
    )
```

```python
import functools
import math

import jax
import jax.numpy as jnp
from jax import lax
from jax.experimental import pallas as pl
from jax.experimental.pallas import tpu as pltpu
from jax.sharding import PartitionSpec as P

HD = 128
TOP = 8


norm_eps = 1e-05
rope_base = 10000.0
masked_score = -1e30
LOG2E = 1.4426950408889634
F32 = jnp.float32
SMALL = pl.CostEstimate(flops=0, bytes_accessed=0, transcendentals=0)
BF16 = jnp.bfloat16


def rms_factor(values):
    return lax.rsqrt(jnp.mean(values * values, axis=-1, keepdims=True) + norm_eps)


def rotary_tables(positions, head_size):
    half_size = head_size // 2
    inverse_freq = rope_base ** (-(jnp.arange(half_size, dtype=F32) * 2.0) / head_size)
    angles = positions.astype(F32)[:, None] * inverse_freq[None, :]
    angles = jnp.concatenate([angles, angles], axis=1)
    return (jnp.cos(angles), jnp.sin(angles))


def turn(values):
    half_size = values.shape[-1] // 2
    return jnp.concatenate([-values[..., half_size:], values[..., :half_size]], axis=-1)


def turn_back(values):
    half_size = values.shape[-1] // 2
    return jnp.concatenate([values[..., half_size:], -values[..., :half_size]], axis=-1)


def dot32(a, b):
    return jnp.dot(a, b, preferred_element_type=F32)


def flip(values, axis, mask):
    return lax.ppermute(values, axis, [(i, i ^ mask) for i in range(lax.axis_size(axis))])


def pick(values, index, axis=0):
    return lax.dynamic_index_in_dim(values, index, axis, keepdims=False)


def hold_kernel(*refs):
    del refs


def hold(value, *after):
    return pl.pallas_call(
        hold_kernel,
        out_shape=jax.ShapeDtypeStruct(value.shape, value.dtype),
        in_specs=[pl.BlockSpec(memory_space=pl.ANY)] * (1 + len(after)),
        out_specs=pl.BlockSpec(memory_space=pl.ANY),
        input_output_aliases={0: 0},
        cost_estimate=SMALL,
        name="hold",
    )(value, *after)


def butterfly_sum(values, axis):
    mask = 1
    while mask < lax.axis_size(axis):
        values = jax.tree.map(lambda v: v + flip(v, axis, mask), values)
        mask *= 2
    return values


def reduce_rows(partial, *after):
    count = partial.shape[0]
    me = lax.axis_index("exp")
    core, chip = me % 2, me // 2
    pairs = partial.reshape((count // 2, 2) + partial.shape[1:])
    got = flip(pick(pairs, 1 - core, 1), "exp", 1)
    mine = pick(pairs, core, 1)
    both = (mine.astype(F32) + got.astype(F32)).astype(BF16)
    parts = [flip(pick(both, chip ^ m), "exp", 2 * m) for m in range(1, count // 2)]
    parts = [hold(part, *after) for part in parts]
    total = pick(mine, chip).astype(F32) + pick(got, chip).astype(F32)
    for part in parts:
        total = total + part.astype(F32)
    return total


def block_place(block, ctx_count, place):
    late = block >= ctx_count
    owner = jnp.where(late, 2 * ctx_count - 1 - block, block)
    return owner ^ place, jnp.where(late, 1, 0)


def causal_mask(rows):
    key_line = lax.broadcasted_iota(jnp.int32, (rows, rows), 0)
    query_line = lax.broadcasted_iota(jnp.int32, (rows, rows), 1)
    return key_line <= query_line


def attend_kernel(place_ref, qk_ref, v_ref, o_ref, ot_ref, lse_ref, qt_ref, vt_ref):
    ctx_count, rows = v_ref.shape[0], v_ref.shape[1] // 2
    blocks = 2 * ctx_count
    place = place_ref[0]
    scale = LOG2E / math.sqrt(HD)

    def lay(block, unused):
        slab, half = block_place(block, ctx_count, place)
        at = pl.ds(pl.multiple_of(half * rows, rows), rows)
        to = pl.ds(pl.multiple_of(block * rows, rows), rows)
        qt_ref[:, to] = qk_ref[slab, 0, at, :].T
        vt_ref[:, to] = v_ref[slab, at, :].T
        return unused

    lax.fori_loop(0, blocks, lay, 0)

    def query_block(block, unused):
        cols = pl.ds(pl.multiple_of(block * rows, rows), rows)
        query = qt_ref[:, cols]

        def part(key_block, carried, masked):
            high, total, acc = carried
            slab, half = block_place(key_block, ctx_count, place)
            at = pl.ds(pl.multiple_of(half * rows, rows), rows)
            scores = dot32(qk_ref[slab, 1, at, :], query) * scale
            if masked:
                scores = jnp.where(causal_mask(rows), scores, masked_score)
            new_high = jnp.maximum(high, jnp.max(scores, axis=0, keepdims=True))
            probs = jnp.exp2(scores - new_high)
            fade = jnp.exp2(high - new_high)
            total = total * fade + jnp.sum(probs, axis=0, keepdims=True)
            keys = pl.ds(pl.multiple_of(key_block * rows, rows), rows)
            acc = acc * fade + dot32(vt_ref[:, keys], probs.astype(BF16))
            return new_high, total, acc

        start = (
            jnp.full((1, rows), masked_score, F32),
            jnp.zeros((1, rows), F32),
            jnp.zeros((HD, rows), F32),
        )
        state = part(block, start, True)
        high, total, acc = lax.fori_loop(0, block, lambda j, c: part(j, c, False), state)
        out = acc / total
        ot_ref[:, cols] = out
        slab, half = block_place(block, ctx_count, place)
        o_ref[slab, pl.ds(pl.multiple_of(half * rows, rows), rows), :] = out.T.astype(BF16)
        lse_ref[block] = high + jnp.log2(total)
        return unused

    lax.fori_loop(0, blocks, query_block, 0)


def attend_back_kernel(
    place_ref,
    qk_ref,
    v_ref,
    do_ref,
    ot_ref,
    lse_ref,
    d_ref,
    sums_ref,
    qt_ref,
    kt_ref,
    dot_ref,
    dk_ref,
    dv_ref,
):
    ctx_count, rows = v_ref.shape[0], v_ref.shape[1] // 2
    blocks = 2 * ctx_count
    place = place_ref[0]
    score_scale = 1.0 / math.sqrt(HD)
    scale = LOG2E * score_scale

    def lay(block, unused):
        slab, half = block_place(block, ctx_count, place)
        at = pl.ds(pl.multiple_of(half * rows, rows), rows)
        to = pl.ds(pl.multiple_of(block * rows, rows), rows)
        qt_ref[:, to] = qk_ref[slab, 0, at, :].T
        kt_ref[:, to] = qk_ref[slab, 1, at, :].T
        dot_ref[:, to] = do_ref[slab, at, :].T
        dk_ref[to, :] = jnp.zeros((rows, HD), F32)
        dv_ref[to, :] = jnp.zeros((rows, HD), F32)
        return unused

    lax.fori_loop(0, blocks, lay, 0)

    def query_block(block, unused):
        cols = pl.ds(pl.multiple_of(block * rows, rows), rows)
        slab_q, half_q = block_place(block, ctx_count, place)
        at_q = pl.ds(pl.multiple_of(half_q * rows, rows), rows)
        query_t, grad_t = qt_ref[:, cols], dot_ref[:, cols]
        delta = jnp.sum(grad_t.astype(F32) * ot_ref[:, cols], axis=0, keepdims=True)
        lse = lse_ref[block]

        def part(key_block, dq, masked):
            slab, half = block_place(key_block, ctx_count, place)
            at = pl.ds(pl.multiple_of(half * rows, rows), rows)
            keys = pl.ds(pl.multiple_of(key_block * rows, rows), rows)
            probs = jnp.exp2(dot32(qk_ref[slab, 1, at, :], query_t) * scale - lse)
            if masked:
                probs = jnp.where(causal_mask(rows), probs, 0.0)
            grad_probs = dot32(v_ref[slab, at, :], grad_t)
            grad_scores = (probs * (grad_probs - delta)).astype(BF16)
            dv_ref[keys, :] += dot32(probs.astype(BF16), do_ref[slab_q, at_q, :])
            dk_ref[keys, :] += dot32(grad_scores, qk_ref[slab_q, 0, at_q, :])
            return dq + dot32(kt_ref[:, keys], grad_scores)

        dq = part(block, jnp.zeros((HD, rows), F32), True)
        dq = lax.fori_loop(0, block, lambda j, c: part(j, c, False), dq)
        dq = dq * score_scale
        d_ref[slab_q, 0, at_q, :] = dq.T.astype(BF16)
        sums = jnp.sum(dq * query_t.astype(F32), axis=0, keepdims=True)
        sums_ref[slab_q, pl.ds(half_q, 1), :] = sums
        return unused

    lax.fori_loop(0, blocks, query_block, 0)

    def give(block, unused):
        slab, half = block_place(block, ctx_count, place)
        at = pl.ds(pl.multiple_of(half * rows, rows), rows)
        to = pl.ds(pl.multiple_of(block * rows, rows), rows)
        dk = dk_ref[to, :] * score_scale
        d_ref[slab, 1, at, :] = dk.astype(BF16)
        sums = jnp.sum(dk.T * kt_ref[:, to].astype(F32), axis=0, keepdims=True)
        sums_ref[slab, pl.ds(2 + half, 1), :] = sums
        d_ref[slab, 2, at, :] = dv_ref[to, :].astype(BF16)
        return unused

    lax.fori_loop(0, blocks, give, 0)


VMEM = pl.BlockSpec(memory_space=pltpu.VMEM)
SMEM = pl.BlockSpec(memory_space=pltpu.SMEM)


def attend_call(place, qk, v):
    ctx_count, ctx_rows = v.shape[0], v.shape[1]
    length, rows = ctx_count * ctx_rows, ctx_rows // 2
    pairs = length * length // 2
    return pl.pallas_call(
        attend_kernel,
        out_shape=(
            jax.ShapeDtypeStruct(v.shape, BF16),
            jax.ShapeDtypeStruct((HD, length), F32),
            jax.ShapeDtypeStruct((2 * ctx_count, 1, rows), F32),
        ),
        in_specs=[SMEM, VMEM, VMEM],
        out_specs=(VMEM, VMEM, VMEM),
        scratch_shapes=[pltpu.VMEM((HD, length), BF16), pltpu.VMEM((HD, length), BF16)],
        compiler_params=pltpu.CompilerParams(vmem_limit_bytes=50 * 2**20),
        cost_estimate=SMALL,
        name="attend",
    )(place, qk, v)


def attend_back_call(place, qk, v, grads, out_t, lse):
    ctx_count, ctx_rows = v.shape[0], v.shape[1]
    length = ctx_count * ctx_rows
    pairs = length * length // 2
    return pl.pallas_call(
        attend_back_kernel,
        out_shape=(
            jax.ShapeDtypeStruct((ctx_count, 3, ctx_rows, HD), BF16),
            jax.ShapeDtypeStruct((ctx_count, 4, ctx_rows // 2), F32),
        ),
        in_specs=[SMEM] + [VMEM] * 5,
        out_specs=(VMEM, VMEM),
        scratch_shapes=[pltpu.VMEM((HD, length), BF16)] * 3 + [pltpu.VMEM((length, HD), F32)] * 2,
        compiler_params=pltpu.CompilerParams(vmem_limit_bytes=50 * 2**20),
        cost_estimate=SMALL,
        name="attend_back",
    )(place, qk, v, grads, out_t, lse)


def spread_pairs(values):
    count = values.shape[0]
    place = lax.axis_index("ctx")
    parts = [pick(values, place ^ m) for m in range(count)]
    return jnp.stack([parts[0]] + [flip(parts[m], "ctx", m) for m in range(1, count)])


def return_pairs(values):
    count = values.shape[0]
    place = lax.axis_index("ctx")
    parts = jnp.stack([values[0]] + [flip(values[m], "ctx", m) for m in range(1, count)])
    return jnp.stack([pick(parts, place ^ p) for p in range(count)])


def rotate_kernel(proj_ref, stat_ref, gain_ref, cos_ref, sin_ref, out_ref):
    heads, rows = out_ref.shape[1], proj_ref.shape[2]
    for group in range(proj_ref.shape[0]):
        line = slice(group * rows, (group + 1) * rows)
        cosine, sines = cos_ref[line, :], sin_ref[line, :]
        for which in range(2):
            factor = stat_ref[group, 0, :, which : which + 1]
            for head in range(heads):
                at = slice((which * heads + head) * HD, (which * heads + head + 1) * HD)
                unit = proj_ref[group, 0, :, at] * factor * gain_ref[:, at]
                turned = pltpu.roll(unit, HD // 2, 1)
                out_ref[0, head, which, line, :] = (unit * cosine + turned * sines).astype(BF16)


def rotate_call(projected, stats, gains, cosine, turn_sines):
    exp_count, seq_count, shard_len, width = projected.shape
    local_heads = width // 3 // HD
    group = math.gcd(exp_count, 4)
    shape = (seq_count, local_heads, 2, exp_count * shard_len, HD)
    line_spec = pl.BlockSpec((group * shard_len, HD), lambda s, e: (e, 0))
    out = pl.pallas_call(
        rotate_kernel,
        grid=(seq_count, exp_count // group),
        in_specs=[
            pl.BlockSpec((group, 1, shard_len, width), lambda s, e: (e, s, 0, 0)),
            pl.BlockSpec((group, 1, shard_len, stats.shape[-1]), lambda s, e: (e, s, 0, 0)),
            pl.BlockSpec((1, gains.shape[1]), lambda s, e: (0, 0)),
            line_spec,
            line_spec,
        ],
        out_specs=pl.BlockSpec(
            (1, local_heads, 2, group * shard_len, HD), lambda s, e: (s, 0, 0, e, 0)
        ),
        out_shape=jax.ShapeDtypeStruct(shape, BF16),
        cost_estimate=SMALL,
        name="rotate",
    )(projected, stats, gains, cosine, turn_sines)
    return out.reshape((-1,) + shape[2:])


def norm_back_kernel(place_ref, proj_ref, stat_ref, gain_ref, cos_ref, sin_ref, *refs):
    heads = len(refs) - 2
    back_refs, out_ref, sum_ref = refs[:heads], refs[heads], refs[heads + 1]
    rows = proj_ref.shape[2]

    @pl.when((pl.program_id(0) == 0) & (pl.program_id(1) == 0))
    def start():
        sum_ref[...] = jnp.zeros_like(sum_ref)

    for group in range(proj_ref.shape[0]):
        line = slice(group * rows, (group + 1) * rows)
        cosine, sines = cos_ref[line, :], sin_ref[line, :]
        for which in range(2):
            factor = stat_ref[group, 0, :, which : which + 1]
            mean = stat_ref[group, 0, :, 2 + which : 3 + which]
            for head in range(heads):
                at = slice((which * heads + head) * HD, (which * heads + head + 1) * HD)
                grad = back_refs[head][0, which, line, :].astype(F32)
                grad = grad * cosine + pltpu.roll(grad, HD // 2, 1) * sines
                unit = proj_ref[group, 0, :, at] * factor
                sum_ref[:, at] += jnp.sum(grad * unit, axis=0, keepdims=True)
                grad = factor * (grad * gain_ref[:, at] - unit * mean)
                out_ref[group, 0, :, at] = grad.astype(BF16)
        for head in range(heads):
            at = slice((2 * heads + head) * HD, (2 * heads + head + 1) * HD)
            out_ref[group, 0, :, at] = back_refs[head][0, 2, line, :]


def norm_back_call(place, projected, stats, gains, cosine, back_sines, back):
    exp_count, seq_count, shard_len, width = projected.shape
    local_heads = width // 3 // HD
    group = math.gcd(exp_count, 4)

    def back_spec(head):
        return pl.BlockSpec(
            (1, 3, group * shard_len, HD),
            lambda s, e, p: ((s * local_heads + head) ^ p[0], 0, e, 0),
        )

    wide_spec = pl.BlockSpec((group, 1, shard_len, width), lambda s, e, p: (e, s, 0, 0))
    line_spec = pl.BlockSpec((group * shard_len, HD), lambda s, e, p: (e, 0))
    gain_spec = pl.BlockSpec((1, gains.shape[1]), lambda s, e, p: (0, 0))
    return pl.pallas_call(
        norm_back_kernel,
        grid_spec=pltpu.PrefetchScalarGridSpec(
            num_scalar_prefetch=1,
            grid=(seq_count, exp_count // group),
            in_specs=[
                wide_spec,
                pl.BlockSpec(
                    (group, 1, shard_len, stats.shape[-1]), lambda s, e, p: (e, s, 0, 0)
                ),
                gain_spec,
                line_spec,
                line_spec,
            ]
            + [back_spec(head) for head in range(local_heads)],
            out_specs=(wide_spec, gain_spec),
        ),
        out_shape=(
            jax.ShapeDtypeStruct(projected.shape, BF16),
            jax.ShapeDtypeStruct(gains.shape, F32),
        ),
        cost_estimate=SMALL,
        name="norm_back",
    )(place, projected, stats, gains, cosine, back_sines, *([back] * local_heads))


def half_signs(sines, first, second):
    half_size = sines.shape[1] // 2
    return jnp.concatenate([first * sines[:, :half_size], second * sines[:, half_size:]], axis=1)


def paired_forward(projected, query_gain, key_gain, cosine, sines, model_width, early):
    exp_count, seq_count, shard_len, width = projected.shape
    local_width = width // 3
    local_heads = local_width // HD
    ctx_rows = exp_count * shard_len
    values = projected[..., 2 * local_width :].astype(BF16)
    values = values.reshape(exp_count, seq_count, shard_len, local_heads, HD)
    v_all = spread_pairs(jnp.transpose(values, (1, 3, 0, 2, 4)).reshape(-1, ctx_rows, HD))
    squares = jnp.stack(
        [
            jnp.sum(jnp.square(projected[..., i * local_width : (i + 1) * local_width]), axis=-1)
            for i in range(2)
        ]
    )
    squares = butterfly_sum(squares, "exp")
    factors = lax.rsqrt(squares / model_width + norm_eps)
    gains = jnp.concatenate([query_gain, key_gain])[None]
    stats = jnp.stack([factors[0], factors[1]], axis=-1)
    rotated_qk = rotate_call(projected, stats, gains, cosine, half_signs(sines, -1.0, 1.0))
    qk_all = hold(spread_pairs(rotated_qk), early)
    place = lax.axis_index("ctx").astype(jnp.int32).reshape(1)
    out, out_t, lse = attend_call(place, qk_all, v_all)
    natural = jnp.stack([pick(out, place[0] ^ p) for p in range(out.shape[0])])
    natural = natural.reshape(-1, shard_len, HD)
    own = lax.all_to_all(natural, ("ctx", "exp"), split_axis=0, concat_axis=0, tiled=True)
    own = own.reshape(seq_count, local_heads, exp_count, shard_len, HD)
    own = jnp.transpose(own, (0, 3, 2, 1, 4)).reshape(seq_count * shard_len, -1)
    return (own, out), (place, qk_all, v_all, out_t, lse, projected, factors, gains)


def paired_backward(kept, grads, query_gain, key_gain, cosine, sines, model_width, early, later):
    place, qk_all, v_all, out_t, lse, projected, factors, gains = kept
    exp_count, seq_count, shard_len, width = projected.shape
    local_heads = width // 3 // HD
    grads = hold(spread_pairs(grads), *early)
    back, sums = attend_back_call(place, qk_all, v_all, grads, out_t, lse)
    count = back.shape[0]
    parts = jnp.stack([back[0]] + [flip(back[m], "ctx", m) for m in range(1, count)])
    parts = hold(parts, *later)
    sums = butterfly_sum(return_pairs(sums), "exp")
    sums = sums.reshape(seq_count, local_heads, 2, exp_count, shard_len).sum(axis=1) / model_width
    sums = jnp.transpose(sums, (1, 2, 0, 3))
    stats = jnp.stack([factors[0], factors[1], sums[0], sums[1]], axis=-1)
    grad_qkv, gain_parts = norm_back_call(
        place, projected, stats, gains, cosine, half_signs(sines, 1.0, -1.0), parts
    )
    qgain_part, kgain_part = jnp.split(gain_parts[0], 2)
    return grad_qkv, qgain_part, kgain_part, sums


def gathered_forward(projected, query_gain, key_gain, cosine, sines, model_width, early):
    queries, keys_proj, values_low = jnp.split(projected, 3, axis=-1)
    values_low = values_low.astype(BF16)
    exp_count, seq_count, shard_len, local_width = queries.shape
    ctx_count, ctx_place = lax.axis_size("ctx"), lax.axis_index("ctx")
    local_heads = local_width // HD
    ctx_rows = exp_count * shard_len
    half_rows = ctx_rows // 2
    squares = jnp.stack(
        [jnp.sum(queries * queries, axis=-1), jnp.sum(keys_proj * keys_proj, axis=-1)]
    )
    squares = lax.psum(squares, "exp")
    factors = lax.rsqrt(squares[..., None] / model_width + norm_eps)
    query_unit = queries * factors[0]
    key_unit = keys_proj * factors[1]

    def heads(values):
        values = values.reshape(exp_count, seq_count, shard_len, local_heads, HD)
        return jnp.transpose(values, (1, 0, 2, 3, 4)).reshape(seq_count, ctx_rows, local_heads, HD)

    def rotated(values):
        values = heads(values)
        return (values * cosine[:, None, :] + turn(values) * sines[:, None, :]).astype(BF16)

    query_rot = rotated(query_unit * query_gain)
    keys_all = lax.all_gather(rotated(key_unit * key_gain), "ctx", axis=1, tiled=True)
    values_all = lax.all_gather(heads(values_low), "ctx", axis=1, tiled=True)
    tools = block_tools(half_rows, ctx_count, ctx_place)
    block_len, half_firsts, row_start, block_scores = tools
    attended_halves = []
    log_halves = []
    for half_index in range(2):
        query_half = query_rot[:, half_index * half_rows : (half_index + 1) * half_rows]
        query_first = half_firsts[half_index]
        needed_blocks = (query_first + half_rows) // block_len

        def step(counter, carried):
            running_max, running_sum, acc = carried
            key_first = counter * block_len
            start_row = row_start(key_first)
            key_block = lax.dynamic_slice_in_dim(keys_all, start_row, block_len, 1)
            value_block = lax.dynamic_slice_in_dim(values_all, start_row, block_len, 1)
            scores = block_scores(query_half, query_first, key_block, key_first)
            new_max = jnp.maximum(running_max, jnp.max(scores, axis=-1))
            fade = jnp.exp(running_max - new_max)
            probs = jnp.exp(scores - new_max[..., None])
            running_sum = running_sum * fade + jnp.sum(probs, axis=-1)
            acc = acc * jnp.transpose(fade, (0, 2, 1))[..., None] + jnp.einsum(
                "shqk,skhd->sqhd", probs.astype(BF16), value_block, preferred_element_type=F32
            )
            return (new_max, running_sum, acc)

        stat_shape = (seq_count, local_heads, half_rows)
        running_max, running_sum, acc = lax.fori_loop(
            0,
            needed_blocks,
            step,
            (
                jnp.full(stat_shape, masked_score, F32),
                jnp.zeros(stat_shape, F32),
                jnp.zeros((seq_count, half_rows, local_heads, HD), F32),
            ),
        )
        attended_halves.append(acc / jnp.transpose(running_sum, (0, 2, 1))[..., None])
        log_halves.append(running_max + jnp.log(running_sum))
    attended_float = jnp.concatenate(attended_halves, axis=1)
    attended = jnp.transpose(attended_float.astype(BF16), (0, 2, 1, 3)).reshape(-1, ctx_rows, HD)
    kept = (
        query_rot, keys_all, values_all, attended_float, log_halves, query_unit, key_unit, factors
    )
    sent = jnp.transpose(attended.reshape(-1, exp_count, shard_len, HD), (1, 0, 2, 3))
    own = lax.all_to_all(sent, "exp", split_axis=0, concat_axis=0, tiled=True)
    own = own.reshape(exp_count, seq_count, local_heads, shard_len, HD)
    own = jnp.transpose(own, (1, 3, 0, 2, 4)).reshape(seq_count * shard_len, -1)
    return (own, attended), kept


def block_tools(half_rows, ctx_count, ctx_place):
    block_len = math.gcd(half_rows, 512)
    far_first = (2 * ctx_count - 1 - ctx_place) * half_rows
    half_firsts = (ctx_place * half_rows, far_first)

    def row_start(first_pos):
        segment = first_pos // half_rows
        offset = first_pos % half_rows
        return jnp.where(
            segment < ctx_count,
            segment * 2 * half_rows + offset,
            (2 * ctx_count - 1 - segment) * 2 * half_rows + half_rows + offset,
        )

    def block_scores(query_block, query_first, key_block, key_first):
        scores = jnp.einsum("sqhd,skhd->shqk", query_block, key_block, preferred_element_type=F32)
        scores = scores * (1.0 / math.sqrt(HD))
        query_line = query_first + jnp.arange(query_block.shape[1], dtype=jnp.int32)
        key_line = key_first + jnp.arange(key_block.shape[1], dtype=jnp.int32)
        return jnp.where(key_line[None, :] <= query_line[:, None], scores, masked_score)

    return block_len, half_firsts, row_start, block_scores


def gathered_backward(
    kept, grads, query_gain, key_gain, cosine, sines, model_width, early, later
):
    query_rot, keys_all, values_all, attended_float, log_halves, query_unit, key_unit, factors = kept
    exp_count, seq_count, shard_len, local_width = query_unit.shape
    ctx_count, ctx_place = lax.axis_size("ctx"), lax.axis_index("ctx")
    local_heads = local_width // HD
    ctx_rows = exp_count * shard_len
    half_rows = ctx_rows // 2
    seq_len = keys_all.shape[1]
    score_scale = 1.0 / math.sqrt(HD)
    block_len, half_firsts, row_start, block_scores = block_tools(half_rows, ctx_count, ctx_place)
    grad_heads = jnp.transpose(
        grads.reshape(seq_count, local_heads, ctx_rows, HD), (0, 2, 1, 3)
    )
    delta_rows = jnp.transpose(jnp.sum(grad_heads.astype(F32) * attended_float, axis=-1), (0, 2, 1))
    keyval_grads = jnp.zeros((seq_count, seq_len, 2 * local_width), F32)
    query_halves = []
    for half_index in range(2):
        row_slice = slice(half_index * half_rows, (half_index + 1) * half_rows)
        query_half = query_rot[:, row_slice]
        grad_half = grad_heads[:, row_slice]
        delta_half = delta_rows[:, :, row_slice]
        log_total = log_halves[half_index]
        query_first = half_firsts[half_index]
        needed_blocks = (query_first + half_rows) // block_len

        def one_block(counter, inner):
            query_acc, keyval_acc = inner
            key_first = counter * block_len
            start_row = row_start(key_first)
            key_block = lax.dynamic_slice_in_dim(keys_all, start_row, block_len, 1)
            value_block = lax.dynamic_slice_in_dim(values_all, start_row, block_len, 1)
            scores = block_scores(query_half, query_first, key_block, key_first)
            soft_probs = jnp.exp(scores - log_total[..., None])
            grad_probs = jnp.einsum(
                "sqhd,skhd->shqk", grad_half, value_block, preferred_element_type=F32
            )
            grad_scores = (soft_probs * (grad_probs - delta_half[..., None])).astype(BF16)
            query_acc = query_acc + score_scale * jnp.einsum(
                "shqk,skhd->sqhd", grad_scores, key_block, preferred_element_type=F32
            )
            kblock_grad = score_scale * jnp.einsum(
                "shqk,sqhd->skhd", grad_scores, query_half, preferred_element_type=F32
            )
            vblock_grad = jnp.einsum(
                "shqk,sqhd->skhd", soft_probs.astype(BF16), grad_half, preferred_element_type=F32
            )
            flat = (seq_count, block_len, local_width)
            combined = jnp.concatenate([kblock_grad.reshape(flat), vblock_grad.reshape(flat)], -1)
            keyval_acc = lax.dynamic_update_slice_in_dim(
                keyval_acc,
                lax.dynamic_slice_in_dim(keyval_acc, start_row, block_len, 1) + combined,
                start_row,
                1,
            )
            return (query_acc, keyval_acc)

        query_acc, keyval_grads = lax.fori_loop(
            0,
            needed_blocks,
            one_block,
            (jnp.zeros((seq_count, half_rows, local_heads, HD), F32), keyval_grads),
        )
        query_halves.append(query_acc)
    query_back = jnp.concatenate(query_halves, axis=1)
    keyval_local = lax.psum_scatter(keyval_grads, "ctx", scatter_dimension=1, tiled=True)

    def by_row(values):
        values = values.reshape(seq_count, exp_count, shard_len, local_width)
        return jnp.transpose(values, (1, 0, 2, 3))

    def unrotated(values):
        values = values.reshape(seq_count, ctx_rows, local_heads, HD)
        return by_row(values * cosine[:, None, :] + turn_back(values) * sines[:, None, :])

    qnorm_grad = unrotated(query_back)
    knorm_grad = unrotated(keyval_local[..., :local_width])
    grad_values = by_row(keyval_local[..., local_width:].astype(BF16))
    qgain_part = jnp.sum(qnorm_grad * query_unit, axis=(0, 1, 2))
    kgain_part = jnp.sum(knorm_grad * key_unit, axis=(0, 1, 2))
    qunit_grad = qnorm_grad * query_gain
    kunit_grad = knorm_grad * key_gain
    dots = jnp.stack(
        [jnp.sum(qunit_grad * query_unit, axis=-1), jnp.sum(kunit_grad * key_unit, axis=-1)]
    )
    dots = lax.psum(dots, "exp")[..., None] / model_width
    grad_queries = (factors[0] * (qunit_grad - query_unit * dots[0])).astype(BF16)
    grad_keys = (factors[1] * (kunit_grad - key_unit * dots[1])).astype(BF16)
    grad_qkv = jnp.concatenate([grad_queries, grad_keys, grad_values], axis=-1)
    return grad_qkv, qgain_part, kgain_part, dots


NT = (((1,), (1,)), ((), ()))
TN = (((0,), (0,)), ((), ()))
EXPERT_PARAMS = pltpu.CompilerParams(vmem_limit_bytes=58 * 2**20)


def down_kernel(half_ref, rows_ref, weight_ref, out_ref):
    out_ref[0] = dot32(rows_ref[...], weight_ref[0, 0])


def down_call(rows, weights, half, width):
    count, model_width = rows.shape
    experts = weights.shape[0]
    tile, cols = math.gcd(count, 1024), math.gcd(width, 1024)
    parts = width // cols
    return pl.pallas_call(
        down_kernel,
        grid_spec=pltpu.PrefetchScalarGridSpec(
            num_scalar_prefetch=1,
            grid=(experts, parts, count // tile),
            in_specs=[
                pl.BlockSpec((tile, model_width), lambda e, f, r, h: (r, 0)),
                pl.BlockSpec(
                    (1, 1, model_width, cols), lambda e, f, r, h: (e, 2, 0, h[0] * parts + f)
                ),
            ],
            out_specs=pl.BlockSpec((1, tile, cols), lambda e, f, r, h: (e, r, f)),
        ),
        out_shape=jax.ShapeDtypeStruct((experts, count, width), F32),
        compiler_params=EXPERT_PARAMS,
        cost_estimate=SMALL,
        name="down",
    )(half, rows, weights)


def hidden_kernel(
    half_ref, rows_ref, wg_ref, wu_ref, down_ref, gate_ref, gm_ref, gg_ref, gu_ref, *dots, chunk
):
    width = wg_ref.shape[-1]

    def step(i, unused):
        at = pl.ds(pl.multiple_of(i * chunk, chunk), chunk)
        rows = rows_ref[at, :]
        pre_gate = dot32(rows, wg_ref[0, 0])
        pre_up = dot32(rows, wu_ref[0, 0])
        down, gate = down_ref[0, at, :], gate_ref[0, at, :]
        sigmoid_vals = 1.0 / (1.0 + jnp.exp(-pre_gate))
        activated = pre_gate * sigmoid_vals
        middle = activated * pre_up
        for dot_ref in dots:
            products = middle * down
            acc = products[:, :128]
            for c in range(1, width // 128):
                acc = acc + products[:, c * 128 : (c + 1) * 128]
            dot_ref[0, 0, at, :] = acc
        gm_ref[0, at, :] = (gate * middle).astype(BF16)
        grad = gate * down
        gu_ref[0, at, :] = (grad * activated).astype(BF16)
        slope = sigmoid_vals * (1.0 + pre_gate * (1.0 - sigmoid_vals))
        gg_ref[0, at, :] = (grad * pre_up * slope).astype(BF16)
        return unused

    lax.fori_loop(0, rows_ref.shape[0] // chunk, step, 0)


def hidden_call(rows, weights, down, gates, half, with_dots):
    count, model_width = rows.shape
    experts, width = weights.shape[0], down.shape[-1]
    tile, cols = math.gcd(count, 1024), math.gcd(width, 512)
    parts = width // cols
    wide = pl.BlockSpec((1, tile, cols), lambda e, f, r, h: (e, r, f))
    shape = jax.ShapeDtypeStruct((experts, count, width), BF16)
    out_specs, out_shape = [wide] * 3, [shape] * 3
    if with_dots:
        out_specs.append(pl.BlockSpec((1, 1, tile, 128), lambda e, f, r, h: (e, f, r, 0)))
        out_shape.append(jax.ShapeDtypeStruct((experts, parts, count, 128), F32))

    def weight_spec(which):
        return pl.BlockSpec(
            (1, 1, model_width, cols), lambda e, f, r, h: (e, which, 0, h[0] * parts + f)
        )

    return pl.pallas_call(
        functools.partial(hidden_kernel, chunk=math.gcd(tile, 256)),
        grid_spec=pltpu.PrefetchScalarGridSpec(
            num_scalar_prefetch=1,
            grid=(experts, parts, count // tile),
            in_specs=[
                pl.BlockSpec((tile, model_width), lambda e, f, r, h: (r, 0)),
                weight_spec(0),
                weight_spec(1),
                wide,
                pl.BlockSpec((1, tile, 1), lambda e, f, r, h: (e, r, 0)),
            ],
            out_specs=out_specs,
        ),
        out_shape=out_shape,
        compiler_params=EXPERT_PARAMS,
        cost_estimate=SMALL,
        name="hidden",
    )(half, rows, weights, weights, down, gates)


def back_kernel(*refs, count, chunk):
    a_refs, b_refs, out_ref, acc_ref = refs[:count], refs[count : 2 * count], refs[-2], refs[-1]
    turn_at = pl.program_id(2)

    def step(i, unused):
        at = pl.ds(pl.multiple_of(i * chunk, chunk), chunk)
        total = None
        for a, b in zip(a_refs, b_refs):
            term = lax.dot_general(a[0, at, :], b[0, 0], NT, preferred_element_type=F32)
            total = term if total is None else total + term

        @pl.when(turn_at == 0)
        def first():
            acc_ref[at, :] = total

        @pl.when(turn_at > 0)
        def later():
            acc_ref[at, :] += total

        return unused

    lax.fori_loop(0, out_ref.shape[0] // chunk, step, 0)

    @pl.when(turn_at == pl.num_programs(2) - 1)
    def last():
        out_ref[...] = acc_ref[...].astype(out_ref.dtype)


def back_call(parts, weights, which, kind=BF16, *after):
    experts, count, width = parts[0].shape
    model_width = weights.shape[2]
    tile, cols = math.gcd(count, 512), math.gcd(model_width, 2048)

    def weight_spec(k):
        return pl.BlockSpec((1, 1, cols, width), lambda d, r, e: (e, k, d, 0))

    return pl.pallas_call(
        functools.partial(back_kernel, count=len(parts), chunk=math.gcd(tile, 256)),
        grid=(model_width // cols, count // tile, experts),
        in_specs=[pl.BlockSpec((1, tile, width), lambda d, r, e: (e, r, 0))] * len(parts)
        + [weight_spec(k) for k in which]
        + [pl.BlockSpec(memory_space=pl.ANY)] * len(after),
        out_specs=pl.BlockSpec((tile, cols), lambda d, r, e: (r, d)),
        out_shape=jax.ShapeDtypeStruct((count, model_width), kind),
        scratch_shapes=[pltpu.VMEM((tile, cols), F32)],
        compiler_params=EXPERT_PARAMS,
        cost_estimate=SMALL,
        name="back",
    )(*parts, *([weights] * len(parts)), *after)


def grad_kernel(half_ref, own_rows, own_grads, near_rows, near_grads, out_ref):
    total = lax.dot_general(own_rows[...], own_grads[0], TN, preferred_element_type=F32)
    total += lax.dot_general(near_rows[...], near_grads[0], TN, preferred_element_type=F32)
    out_ref[...] = total.astype(BF16)


def grad_call(own_rows, own_grads, near_rows, near_grads, half):
    count, model_width = own_rows.shape
    experts, _, width = near_grads.shape
    cols = math.gcd(model_width, 512)
    row_spec = pl.BlockSpec((count, cols), lambda e, d, h: (0, d))
    return pl.pallas_call(
        grad_kernel,
        grid_spec=pltpu.PrefetchScalarGridSpec(
            num_scalar_prefetch=1,
            grid=(experts, model_width // cols),
            in_specs=[
                row_spec,
                pl.BlockSpec((1, count, width), lambda e, d, h: (e, 0, h[0])),
                row_spec,
                pl.BlockSpec((1, count, width), lambda e, d, h: (e, 0, 0)),
            ],
            out_specs=pl.BlockSpec((cols, width), lambda e, d, h: (d, e)),
        ),
        out_shape=jax.ShapeDtypeStruct((model_width, experts * width), BF16),
        compiler_params=EXPERT_PARAMS,
        cost_estimate=SMALL,
        name="grad",
    )(half, own_rows, own_grads, near_rows, near_grads)


def scatter_rows(term):
    count = lax.axis_size("ctx")
    groups = [[i for i in range(count) if i % 2 == parity] for parity in range(2)]
    return lax.psum_scatter(
        term, "ctx", scatter_dimension=0, axis_index_groups=groups, tiled=True
    )


def swap_rows(term):
    size = term.shape[0] // 2
    odd = lax.axis_index("ctx") % 2
    sent = flip(lax.dynamic_slice_in_dim(term, (1 - odd) * size, size, 0), "ctx", 1)
    kept = lax.dynamic_slice_in_dim(term, odd * size, size, 0)
    return sent, kept


def body(
    block_input,
    attend_gain,
    w_query,
    w_key,
    w_value,
    w_out,
    query_gain,
    key_gain,
    expert_gain,
    router,
    expert_weights,
    routes,
    cotangent,
):
    exp_count, ctx_count = lax.axis_size("exp"), lax.axis_size("ctx")
    ctx_place, exp_place = lax.axis_index("ctx"), lax.axis_index("exp")
    seq_count, shard_len, model_width = block_input.shape
    local_width = w_query.shape[1]
    local_heads = local_width // HD
    experts_all = router.shape[1]
    experts_here = expert_weights.shape[1]
    hidden_units = expert_weights.shape[3]
    rows_dev = seq_count * shard_len
    rows_all = exp_count * rows_dev
    ctx_rows = exp_count * shard_len
    half_rows = ctx_rows // 2
    pair_count = seq_count * local_heads
    paired = pair_count == ctx_count and half_rows % 128 == 0

    def gather(values):
        return lax.all_gather(values, "exp", axis=0, tiled=False)

    half = (ctx_place % 2).astype(jnp.int32).reshape(1)
    whole = jnp.zeros((1,), jnp.int32)
    local_float = block_input.astype(F32).reshape(rows_dev, model_width)
    local_factor = rms_factor(local_float)
    local_unit = local_float * local_factor
    normed = gather((local_unit * attend_gain).astype(BF16)).reshape(rows_all, model_width)
    weights = jnp.transpose(expert_weights, (1, 2, 0, 3))
    w_qkv = jnp.concatenate([w_query, w_key, w_value], axis=1)
    own_routes = jnp.transpose(routes, (1, 0, 2)).reshape(rows_dev, TOP)
    own_grads = cotangent.reshape(rows_dev, model_width)
    grad_low = gather(own_grads).reshape(rows_all, model_width)
    full_out = gather(w_out).reshape(exp_count * local_width, model_width)
    near_low = gather(hold(flip(own_grads, "ctx", 1), weights)).reshape(rows_all, model_width)
    all_routes = gather(own_routes).reshape(rows_all, TOP)
    near_routes = flip(all_routes, "ctx", 1)
    w_qkv = hold(w_qkv, weights, near_routes)
    grad_down = down_call(grad_low, weights, whole, hidden_units)
    near_down = down_call(near_low, weights, half, hidden_units // 2)

    projected = dot32(normed, w_qkv).reshape(exp_count, seq_count, shard_len, 3 * local_width)
    row_ids = jnp.arange(ctx_rows, dtype=jnp.int32)
    far_first = (2 * ctx_count - 1 - ctx_place) * half_rows
    query_pos = jnp.where(
        row_ids < half_rows, ctx_place * half_rows + row_ids, far_first + row_ids - half_rows
    )
    cosine, sines = rotary_tables(query_pos, HD)
    forward, backward = (
        (paired_forward, paired_backward) if paired else (gathered_forward, gathered_backward)
    )
    (own_attended, attended), kept = forward(
        projected, query_gain, key_gain, cosine, sines, model_width, grad_down
    )

    def exchange(values):
        return lax.all_to_all(values, "exp", split_axis=0, concat_axis=0, tiled=True)

    hidden = local_float + dot32(own_attended, full_out)
    hidden_factor = rms_factor(hidden)
    unit_second = hidden * hidden_factor
    own_mixed = (unit_second * expert_gain).astype(BF16)

    expert_ids = jnp.arange(experts_all, dtype=jnp.int32)

    def chosen(table):
        return jnp.any(table[:, :, None] == expert_ids[None, None, :], axis=1)

    own_prob = jax.nn.softmax(dot32(own_mixed, router), axis=-1)

    def local_gates(rows, table):
        prob = jax.nn.softmax(dot32(rows, router), axis=-1)
        gates = jnp.where(chosen(table), prob, 0.0)
        gates = lax.dynamic_slice_in_dim(gates, exp_place * experts_here, experts_here, 1)
        return jnp.transpose(gates)[:, :, None]

    if paired:
        attended = return_pairs(hold(attended, own_mixed))
    mixed = hold(gather(own_mixed).reshape(rows_all, model_width), near_down, attended)
    near_mixed = gather(hold(flip(own_mixed, "ctx", 1), near_down))
    gates = local_gates(mixed, all_routes)

    gated_middle, grad_gate, grad_up, dots = hidden_call(
        mixed, weights, grad_down, gates, whole, True
    )
    gate_grads = jnp.sum(dots, axis=(1, 3))
    choice_grad = exchange(
        jnp.transpose(gate_grads.reshape(experts_here, exp_count, rows_dev), (1, 0, 2))
    )
    near_mixed = hold(near_mixed.reshape(rows_all, model_width), gated_middle)
    near_gates = local_gates(near_mixed, near_routes)
    near_middle, near_grad_gate, near_grad_up = hidden_call(
        near_mixed, weights, near_down, near_gates, half, False
    )

    down_term = grad_call(grad_low, gated_middle, near_low, near_middle, half)
    slot_rows = back_call([grad_gate, grad_up], weights, (0, 1), BF16, down_term, choice_grad)
    gate_term = grad_call(mixed, grad_gate, near_mixed, near_grad_gate, half)
    up_term = grad_call(mixed, grad_up, near_mixed, near_grad_up, half)
    down_sum, gate_sum, up_sum = (scatter_rows(t) for t in (down_term, gate_term, up_term))
    slot_sum = reduce_rows(
        slot_rows.reshape(exp_count, rows_dev, model_width), gate_term, up_term
    )
    choice_grad = jnp.transpose(choice_grad, (2, 0, 1)).reshape(rows_dev, experts_all)
    choice_grad = jnp.where(chosen(own_routes), choice_grad, 0.0)
    logit_grad = (
        own_prob * (choice_grad - jnp.sum(own_prob * choice_grad, axis=-1, keepdims=True))
    ).astype(BF16)
    router_part = jnp.einsum("td,te->de", own_mixed, logit_grad, preferred_element_type=F32)
    mixed_grad = slot_sum + jnp.einsum(
        "te,de->td", logit_grad, router, preferred_element_type=F32
    )
    egain_part = jnp.sum(mixed_grad * unit_second, axis=0)
    usecond_grad = mixed_grad * expert_gain
    grad_rows = cotangent.astype(F32).reshape(rows_dev, model_width)
    grad_hidden = (
        hidden_factor
        * (usecond_grad - unit_second * jnp.mean(usecond_grad * unit_second, axis=-1, keepdims=True))
        + grad_rows
    )
    own_branch = grad_hidden.astype(BF16)
    early_part = jnp.concatenate([router_part, egain_part[:, None]], axis=1)
    early_part = exchange(early_part.reshape(exp_count, -1, experts_all + 1))
    branch_rows = gather(hold(own_branch, up_sum)).reshape(exp_count, seq_count, shard_len, model_width)

    grad_attended = jnp.einsum(
        "rd,hd->rh", own_branch, full_out, preferred_element_type=F32
    ).astype(BF16)
    expert_out = back_call([gated_middle], weights, (2,), BF16, grad_attended)
    sent = grad_attended.reshape(seq_count, shard_len, exp_count, local_heads, HD)
    sent = jnp.transpose(sent, (2, 0, 3, 1, 4)).reshape(exp_count, pair_count, shard_len, HD)
    grads = jnp.transpose(exchange(sent), (1, 0, 2, 3)).reshape(pair_count, ctx_rows, HD)
    swapped = [swap_rows(term) for term in (gate_sum, hold(up_sum, grads), down_sum)]
    grad_qkv, qgain_part, kgain_part, ended = backward(
        kept, grads, query_gain, key_gain, cosine, sines, model_width, (expert_out, swapped[2][0]), (swapped[0][0], swapped[1][0])
    )
    attended_rows = attended.reshape(seq_count, local_heads, exp_count, shard_len, HD)
    branch_rows = hold(branch_rows, ended)
    outw_part = jnp.einsum(
        "shetc,estd->hcd", attended_rows, branch_rows, preferred_element_type=F32
    ).reshape(local_width, model_width)
    qkv_part = jnp.einsum(
        "rd,rh->dh", normed, grad_qkv.reshape(rows_all, -1), preferred_element_type=F32
    )
    qkv_part, outw_part = qkv_part.astype(BF16), outw_part.astype(BF16)
    qkv_grad, out_grad = lax.psum((qkv_part, outw_part), "ctx")

    w_qkv = jnp.concatenate([w_query, w_key, w_value], axis=1)
    grad_rows_qkv = grad_qkv.reshape(1, rows_all, -1)
    normed_back = back_call(
        [grad_rows_qkv], w_qkv[None, None], (0,), BF16, qkv_part, outw_part
    )
    grad_normed = reduce_rows(normed_back.reshape(exp_count, rows_dev, model_width))
    attend_part = jnp.sum(grad_normed * local_unit, axis=0)
    lunit_grad = grad_normed * attend_gain
    input_grad = grad_hidden + local_factor * (
        lunit_grad - local_unit * jnp.mean(lunit_grad * local_unit, axis=-1, keepdims=True)
    )
    halves = []
    even = ctx_place % 2 == 0
    for sent_rows, kept_rows in swapped:
        sent_rows = hold(sent_rows, grad_normed)
        lower = jnp.where(even, kept_rows, sent_rows)
        upper = jnp.where(even, sent_rows, kept_rows)
        parts = [
            v.astype(F32).reshape(-1, experts_here, hidden_units // 2) for v in (lower, upper)
        ]
        halves.append(jnp.concatenate(parts, axis=-1))
    expert_grad = jnp.stack(halves, axis=2)
    expert_out = hold(expert_out, normed_back)
    mixture = reduce_rows(expert_out.reshape(exp_count, rows_dev, model_width), grad_normed)
    block_output = (hidden + mixture).astype(BF16).reshape(block_input.shape)

    attend_sum = jnp.sum(exchange(attend_part.reshape(exp_count, -1)), axis=0)
    early_sum = jnp.sum(hold(early_part, grad_qkv), axis=0)
    late = [v[:, None] for v in (attend_sum, qgain_part, kgain_part)]
    sums = butterfly_sum(jnp.concatenate([early_sum] + late, axis=1), "ctx")
    last = (sums, input_grad, block_output, expert_grad)
    qkv_grad = hold(qkv_grad, *last).astype(F32)
    out_grad = hold(out_grad, *last).astype(F32)
    return (
        block_output,
        input_grad.reshape(block_input.shape),
        sums[:, experts_all + 1],
        qkv_grad[:, :local_width],
        qkv_grad[:, local_width : 2 * local_width],
        qkv_grad[:, 2 * local_width :],
        out_grad,
        sums[:, experts_all + 2],
        sums[:, experts_all + 3],
        sums[:, experts_all],
        sums[:, :experts_all],
        expert_grad,
    )


def solution(mesh):
    placed = (
        P(None, ("ctx", "exp"), None),
        P(),
        P(None, "exp"),
        P(None, "exp"),
        P(None, "exp"),
        P("exp", None),
        P("exp"),
        P("exp"),
        P(),
        P(),
        P(None, "exp", None, None),
        P(("ctx", "exp"), None, None),
        P(None, ("ctx", "exp"), None),
    )
    return jax.shard_map(
        body,
        mesh=mesh,
        in_specs=placed,
        out_specs=(
            P(None, ("ctx", "exp"), None),
            P(None, ("ctx", "exp"), None),
            P("exp"),
            P(None, "exp"),
            P(None, "exp"),
            P(None, "exp"),
            P("exp", None),
            P("exp"),
            P("exp"),
            P("exp"),
            P("exp", None),
            P("ctx", "exp", None, None),
        ),
        check_vma=False,
    )
```

```python
import functools
import math

import jax
import jax.numpy as jnp
from jax import lax
from jax.experimental import pallas as pl
from jax.experimental.pallas import tpu as pltpu
from jax.sharding import PartitionSpec as P

HD = 128
TOP = 8


norm_eps = 1e-05
rope_base = 10000.0
masked_score = -1e30
LOG2E = 1.4426950408889634
F32 = jnp.float32
SMALL = pl.CostEstimate(flops=0, bytes_accessed=0, transcendentals=0)
BF16 = jnp.bfloat16


def rms_factor(values):
    return lax.rsqrt(jnp.mean(values * values, axis=-1, keepdims=True) + norm_eps)


def rotary_tables(positions, head_size):
    half_size = head_size // 2
    inverse_freq = rope_base ** (-(jnp.arange(half_size, dtype=F32) * 2.0) / head_size)
    angles = positions.astype(F32)[:, None] * inverse_freq[None, :]
    angles = jnp.concatenate([angles, angles], axis=1)
    return (jnp.cos(angles), jnp.sin(angles))


def turn(values):
    half_size = values.shape[-1] // 2
    return jnp.concatenate([-values[..., half_size:], values[..., :half_size]], axis=-1)


def turn_back(values):
    half_size = values.shape[-1] // 2
    return jnp.concatenate([values[..., half_size:], -values[..., :half_size]], axis=-1)


def dot32(a, b):
    return jnp.dot(a, b, preferred_element_type=F32)


def flip(values, axis, mask):
    return lax.ppermute(values, axis, [(i, i ^ mask) for i in range(lax.axis_size(axis))])


def pick(values, index, axis=0):
    return lax.dynamic_index_in_dim(values, index, axis, keepdims=False)


def hold_kernel(*refs):
    del refs


def hold(value, *after):
    return pl.pallas_call(
        hold_kernel,
        out_shape=jax.ShapeDtypeStruct(value.shape, value.dtype),
        in_specs=[pl.BlockSpec(memory_space=pl.ANY)] * (1 + len(after)),
        out_specs=pl.BlockSpec(memory_space=pl.ANY),
        input_output_aliases={0: 0},
        cost_estimate=SMALL,
        name="hold",
    )(value, *after)


def butterfly_sum(values, axis):
    mask = 1
    while mask < lax.axis_size(axis):
        values = jax.tree.map(lambda v: v + flip(v, axis, mask), values)
        mask *= 2
    return values


def reduce_start(partial):
    count = partial.shape[0]
    me = lax.axis_index("exp")
    core, chip = me % 2, me // 2
    pairs = partial.reshape((count // 2, 2) + partial.shape[1:])
    got = flip(pick(pairs, 1 - core, 1), "exp", 1)
    mine = pick(pairs, core, 1)
    both = (mine.astype(F32) + got.astype(F32)).astype(BF16)
    return both, (pick(mine, chip), pick(got, chip))


def reduce_send(both):
    chip = lax.axis_index("exp") // 2
    return [flip(pick(both, chip ^ m), "exp", 2 * m) for m in range(1, both.shape[0])]


def reduce_total(parts, own, *after):
    parts = [hold(part, *after) for part in parts] if after else parts
    total = own[0].astype(F32) + own[1].astype(F32)
    for part in parts:
        total = total + part.astype(F32)
    return total


def reduce_finish(both, own, *after):
    return reduce_total(reduce_send(both), own, *after)


def reduce_rows(partial, *after):
    return reduce_finish(*reduce_start(partial), *after)


def block_place(block, ctx_count, place):
    late = block >= ctx_count
    owner = jnp.where(late, 2 * ctx_count - 1 - block, block)
    return owner ^ place, jnp.where(late, 1, 0)


def causal_mask(rows):
    key_line = lax.broadcasted_iota(jnp.int32, (rows, rows), 0)
    query_line = lax.broadcasted_iota(jnp.int32, (rows, rows), 1)
    return key_line <= query_line


def attend_kernel(place_ref, qk_ref, v_ref, o_ref, ot_ref, lse_ref, qt_ref, vt_ref):
    ctx_count, rows = v_ref.shape[0], v_ref.shape[1] // 2
    blocks = 2 * ctx_count
    place = place_ref[0]
    scale = LOG2E / math.sqrt(HD)

    def lay(block, unused):
        slab, half = block_place(block, ctx_count, place)
        at = pl.ds(pl.multiple_of(half * rows, rows), rows)
        to = pl.ds(pl.multiple_of(block * rows, rows), rows)
        qt_ref[:, to] = qk_ref[slab, 0, at, :].T
        vt_ref[:, to] = v_ref[slab, at, :].T
        return unused

    lax.fori_loop(0, blocks, lay, 0)

    def query_block(block, unused):
        cols = pl.ds(pl.multiple_of(block * rows, rows), rows)
        query = qt_ref[:, cols]

        def part(key_block, carried, masked):
            high, total, acc = carried
            slab, half = block_place(key_block, ctx_count, place)
            at = pl.ds(pl.multiple_of(half * rows, rows), rows)
            scores = dot32(qk_ref[slab, 1, at, :], query) * scale
            if masked:
                scores = jnp.where(causal_mask(rows), scores, masked_score)
            new_high = jnp.maximum(high, jnp.max(scores, axis=0, keepdims=True))
            probs = jnp.exp2(scores - new_high)
            fade = jnp.exp2(high - new_high)
            total = total * fade + jnp.sum(probs, axis=0, keepdims=True)
            keys = pl.ds(pl.multiple_of(key_block * rows, rows), rows)
            acc = acc * fade + dot32(vt_ref[:, keys], probs.astype(BF16))
            return new_high, total, acc

        start = (
            jnp.full((1, rows), masked_score, F32),
            jnp.zeros((1, rows), F32),
            jnp.zeros((HD, rows), F32),
        )
        state = part(block, start, True)
        high, total, acc = lax.fori_loop(0, block, lambda j, c: part(j, c, False), state)
        out = acc / total
        ot_ref[:, cols] = out
        slab, half = block_place(block, ctx_count, place)
        o_ref[slab, pl.ds(pl.multiple_of(half * rows, rows), rows), :] = out.T.astype(BF16)
        lse_ref[block] = high + jnp.log2(total)
        return unused

    lax.fori_loop(0, blocks, query_block, 0)


def attend_back_kernel(
    place_ref,
    qk_ref,
    v_ref,
    do_ref,
    ot_ref,
    lse_ref,
    d_ref,
    sums_ref,
    qt_ref,
    kt_ref,
    dot_ref,
    dk_ref,
    dv_ref,
):
    ctx_count, rows = v_ref.shape[0], v_ref.shape[1] // 2
    blocks = 2 * ctx_count
    place = place_ref[0]
    score_scale = 1.0 / math.sqrt(HD)
    scale = LOG2E * score_scale

    def lay(block, unused):
        slab, half = block_place(block, ctx_count, place)
        at = pl.ds(pl.multiple_of(half * rows, rows), rows)
        to = pl.ds(pl.multiple_of(block * rows, rows), rows)
        qt_ref[:, to] = qk_ref[slab, 0, at, :].T
        kt_ref[:, to] = qk_ref[slab, 1, at, :].T
        dot_ref[:, to] = do_ref[slab, at, :].T
        dk_ref[to, :] = jnp.zeros((rows, HD), F32)
        dv_ref[to, :] = jnp.zeros((rows, HD), F32)
        return unused

    lax.fori_loop(0, blocks, lay, 0)

    def query_block(block, unused):
        cols = pl.ds(pl.multiple_of(block * rows, rows), rows)
        slab_q, half_q = block_place(block, ctx_count, place)
        at_q = pl.ds(pl.multiple_of(half_q * rows, rows), rows)
        query_t, grad_t = qt_ref[:, cols], dot_ref[:, cols]
        delta = jnp.sum(grad_t.astype(F32) * ot_ref[:, cols], axis=0, keepdims=True)
        lse = lse_ref[block]

        def part(key_block, dq, masked):
            slab, half = block_place(key_block, ctx_count, place)
            at = pl.ds(pl.multiple_of(half * rows, rows), rows)
            keys = pl.ds(pl.multiple_of(key_block * rows, rows), rows)
            probs = jnp.exp2(dot32(qk_ref[slab, 1, at, :], query_t) * scale - lse)
            if masked:
                probs = jnp.where(causal_mask(rows), probs, 0.0)
            grad_probs = dot32(v_ref[slab, at, :], grad_t)
            grad_scores = (probs * (grad_probs - delta)).astype(BF16)
            dv_ref[keys, :] += dot32(probs.astype(BF16), do_ref[slab_q, at_q, :])
            dk_ref[keys, :] += dot32(grad_scores, qk_ref[slab_q, 0, at_q, :])
            return dq + dot32(kt_ref[:, keys], grad_scores)

        dq = part(block, jnp.zeros((HD, rows), F32), True)
        dq = lax.fori_loop(0, block, lambda j, c: part(j, c, False), dq)
        dq = dq * score_scale
        d_ref[slab_q, 0, at_q, :] = dq.T.astype(BF16)
        sums = jnp.sum(dq * query_t.astype(F32), axis=0, keepdims=True)
        sums_ref[slab_q, pl.ds(half_q, 1), :] = sums
        return unused

    lax.fori_loop(0, blocks, query_block, 0)

    def give(block, unused):
        slab, half = block_place(block, ctx_count, place)
        at = pl.ds(pl.multiple_of(half * rows, rows), rows)
        to = pl.ds(pl.multiple_of(block * rows, rows), rows)
        dk = dk_ref[to, :] * score_scale
        d_ref[slab, 1, at, :] = dk.astype(BF16)
        sums = jnp.sum(dk.T * kt_ref[:, to].astype(F32), axis=0, keepdims=True)
        sums_ref[slab, pl.ds(2 + half, 1), :] = sums
        d_ref[slab, 2, at, :] = dv_ref[to, :].astype(BF16)
        return unused

    lax.fori_loop(0, blocks, give, 0)


VMEM = pl.BlockSpec(memory_space=pltpu.VMEM)
SMEM = pl.BlockSpec(memory_space=pltpu.SMEM)


def attend_call(place, qk, v):
    ctx_count, ctx_rows = v.shape[0], v.shape[1]
    length, rows = ctx_count * ctx_rows, ctx_rows // 2
    pairs = length * length // 2
    return pl.pallas_call(
        attend_kernel,
        out_shape=(
            jax.ShapeDtypeStruct(v.shape, BF16),
            jax.ShapeDtypeStruct((HD, length), F32),
            jax.ShapeDtypeStruct((2 * ctx_count, 1, rows), F32),
        ),
        in_specs=[SMEM, VMEM, VMEM],
        out_specs=(VMEM, VMEM, VMEM),
        scratch_shapes=[pltpu.VMEM((HD, length), BF16), pltpu.VMEM((HD, length), BF16)],
        compiler_params=pltpu.CompilerParams(vmem_limit_bytes=50 * 2**20),
        cost_estimate=SMALL,
        name="attend",
    )(place, qk, v)


def attend_back_call(place, qk, v, grads, out_t, lse):
    ctx_count, ctx_rows = v.shape[0], v.shape[1]
    length = ctx_count * ctx_rows
    pairs = length * length // 2
    return pl.pallas_call(
        attend_back_kernel,
        out_shape=(
            jax.ShapeDtypeStruct((ctx_count, 3, ctx_rows, HD), BF16),
            jax.ShapeDtypeStruct((ctx_count, 4, ctx_rows // 2), F32),
        ),
        in_specs=[SMEM] + [VMEM] * 5,
        out_specs=(VMEM, VMEM),
        scratch_shapes=[pltpu.VMEM((HD, length), BF16)] * 3 + [pltpu.VMEM((length, HD), F32)] * 2,
        compiler_params=pltpu.CompilerParams(vmem_limit_bytes=50 * 2**20),
        cost_estimate=pl.CostEstimate(
            flops=160 * length * length // 2 * HD, bytes_accessed=0, transcendentals=0
        ),
        name="attend_back",
    )(place, qk, v, grads, out_t, lse)


def spread_pairs(values, *after):
    count = values.shape[0]
    place = lax.axis_index("ctx")
    parts = [pick(values, place ^ m) for m in range(count)]
    parts[1:] = [flip(parts[m], "ctx", m) for m in range(1, count)]
    if after:
        parts[1:] = [hold(part, *after) for part in parts[1:]]
    return jnp.stack(parts)


def return_pairs(values):
    count = values.shape[0]
    place = lax.axis_index("ctx")
    parts = jnp.stack([values[0]] + [flip(values[m], "ctx", m) for m in range(1, count)])
    return jnp.stack([pick(parts, place ^ p) for p in range(count)])


def rotate_kernel(proj_ref, stat_ref, gain_ref, cos_ref, sin_ref, out_ref):
    heads, rows = out_ref.shape[1], proj_ref.shape[2]
    for group in range(proj_ref.shape[0]):
        line = slice(group * rows, (group + 1) * rows)
        cosine, sines = cos_ref[line, :], sin_ref[line, :]
        for which in range(2):
            factor = stat_ref[group, 0, :, which : which + 1]
            for head in range(heads):
                at = slice((which * heads + head) * HD, (which * heads + head + 1) * HD)
                unit = proj_ref[group, 0, :, at] * factor * gain_ref[:, at]
                turned = pltpu.roll(unit, HD // 2, 1)
                out_ref[0, head, which, line, :] = (unit * cosine + turned * sines).astype(BF16)


def rotate_call(projected, stats, gains, cosine, turn_sines):
    exp_count, seq_count, shard_len, width = projected.shape
    local_heads = width // 3 // HD
    group = math.gcd(exp_count, 4)
    shape = (seq_count, local_heads, 2, exp_count * shard_len, HD)
    line_spec = pl.BlockSpec((group * shard_len, HD), lambda s, e: (e, 0))
    out = pl.pallas_call(
        rotate_kernel,
        grid=(seq_count, exp_count // group),
        in_specs=[
            pl.BlockSpec((group, 1, shard_len, width), lambda s, e: (e, s, 0, 0)),
            pl.BlockSpec((group, 1, shard_len, stats.shape[-1]), lambda s, e: (e, s, 0, 0)),
            pl.BlockSpec((1, gains.shape[1]), lambda s, e: (0, 0)),
            line_spec,
            line_spec,
        ],
        out_specs=pl.BlockSpec(
            (1, local_heads, 2, group * shard_len, HD), lambda s, e: (s, 0, 0, e, 0)
        ),
        out_shape=jax.ShapeDtypeStruct(shape, BF16),
        cost_estimate=SMALL,
        name="rotate",
    )(projected, stats, gains, cosine, turn_sines)
    return out.reshape((-1,) + shape[2:])


def norm_back_kernel(place_ref, proj_ref, stat_ref, gain_ref, cos_ref, sin_ref, *refs):
    heads = len(refs) - 2
    back_refs, out_ref, sum_ref = refs[:heads], refs[heads], refs[heads + 1]
    rows = proj_ref.shape[2]

    @pl.when((pl.program_id(0) == 0) & (pl.program_id(1) == 0))
    def start():
        sum_ref[...] = jnp.zeros_like(sum_ref)

    for group in range(proj_ref.shape[0]):
        line = slice(group * rows, (group + 1) * rows)
        cosine, sines = cos_ref[line, :], sin_ref[line, :]
        for which in range(2):
            factor = stat_ref[group, 0, :, which : which + 1]
            mean = stat_ref[group, 0, :, 2 + which : 3 + which]
            for head in range(heads):
                at = slice((which * heads + head) * HD, (which * heads + head + 1) * HD)
                grad = back_refs[head][0, which, line, :].astype(F32)
                grad = grad * cosine + pltpu.roll(grad, HD // 2, 1) * sines
                unit = proj_ref[group, 0, :, at] * factor
                sum_ref[:, at] += jnp.sum(grad * unit, axis=0, keepdims=True)
                grad = factor * (grad * gain_ref[:, at] - unit * mean)
                out_ref[group, 0, :, at] = grad.astype(BF16)
        for head in range(heads):
            at = slice((2 * heads + head) * HD, (2 * heads + head + 1) * HD)
            out_ref[group, 0, :, at] = back_refs[head][0, 2, line, :]


def norm_back_call(place, projected, stats, gains, cosine, back_sines, back):
    exp_count, seq_count, shard_len, width = projected.shape
    local_heads = width // 3 // HD
    group = math.gcd(exp_count, 4)

    def back_spec(head):
        return pl.BlockSpec(
            (1, 3, group * shard_len, HD),
            lambda s, e, p: ((s * local_heads + head) ^ p[0], 0, e, 0),
        )

    wide_spec = pl.BlockSpec((group, 1, shard_len, width), lambda s, e, p: (e, s, 0, 0))
    line_spec = pl.BlockSpec((group * shard_len, HD), lambda s, e, p: (e, 0))
    gain_spec = pl.BlockSpec((1, gains.shape[1]), lambda s, e, p: (0, 0))
    return pl.pallas_call(
        norm_back_kernel,
        grid_spec=pltpu.PrefetchScalarGridSpec(
            num_scalar_prefetch=1,
            grid=(seq_count, exp_count // group),
            in_specs=[
                wide_spec,
                pl.BlockSpec(
                    (group, 1, shard_len, stats.shape[-1]), lambda s, e, p: (e, s, 0, 0)
                ),
                gain_spec,
                line_spec,
                line_spec,
            ]
            + [back_spec(head) for head in range(local_heads)],
            out_specs=(wide_spec, gain_spec),
        ),
        out_shape=(
            jax.ShapeDtypeStruct(projected.shape, BF16),
            jax.ShapeDtypeStruct(gains.shape, F32),
        ),
        cost_estimate=SMALL,
        name="norm_back",
    )(place, projected, stats, gains, cosine, back_sines, *([back] * local_heads))


def half_signs(sines, first, second):
    half_size = sines.shape[1] // 2
    return jnp.concatenate([first * sines[:, :half_size], second * sines[:, half_size:]], axis=1)


def paired_forward(projected, query_gain, key_gain, cosine, sines, model_width, early):
    exp_count, seq_count, shard_len, width = projected.shape
    local_width = width // 3
    local_heads = local_width // HD
    ctx_rows = exp_count * shard_len
    values = projected[..., 2 * local_width :].astype(BF16)
    values = values.reshape(exp_count, seq_count, shard_len, local_heads, HD)
    v_all = spread_pairs(jnp.transpose(values, (1, 3, 0, 2, 4)).reshape(-1, ctx_rows, HD))
    squares = jnp.stack(
        [
            jnp.sum(jnp.square(projected[..., i * local_width : (i + 1) * local_width]), axis=-1)
            for i in range(2)
        ]
    )
    squares = butterfly_sum(squares, "exp")
    factors = lax.rsqrt(squares / model_width + norm_eps)
    gains = jnp.concatenate([query_gain, key_gain])[None]
    stats = jnp.stack([factors[0], factors[1]], axis=-1)
    rotated_qk = rotate_call(projected, stats, gains, cosine, half_signs(sines, -1.0, 1.0))
    qk_all = hold(spread_pairs(rotated_qk), early)
    place = lax.axis_index("ctx").astype(jnp.int32).reshape(1)
    out, out_t, lse = attend_call(place, qk_all, v_all)
    natural = jnp.stack([pick(out, place[0] ^ p) for p in range(out.shape[0])])
    natural = natural.reshape(-1, shard_len, HD)
    own = lax.all_to_all(natural, ("ctx", "exp"), split_axis=0, concat_axis=0, tiled=True)
    own = own.reshape(seq_count, local_heads, exp_count, shard_len, HD)
    own = jnp.transpose(own, (0, 3, 2, 1, 4)).reshape(seq_count * shard_len, -1)
    return (own, out), (place, qk_all, v_all, out_t, lse, projected, factors, gains)


def paired_backward(kept, grads, query_gain, key_gain, cosine, sines, model_width, early, later):
    place, qk_all, v_all, out_t, lse, projected, factors, gains = kept
    exp_count, seq_count, shard_len, width = projected.shape
    local_heads = width // 3 // HD
    grads = spread_pairs(grads, *early)
    back, sums = attend_back_call(place, qk_all, v_all, grads, out_t, lse)
    count = back.shape[0]
    parts = [flip(back[m], "ctx", m) for m in range(1, count)]
    sums = butterfly_sum(return_pairs(hold(sums, later[1])), "exp")
    during = later[0](sums)
    parts = jnp.stack([back[0]] + [hold(part, during) for part in parts])
    sums = sums.reshape(seq_count, local_heads, 2, exp_count, shard_len).sum(axis=1) / model_width
    sums = jnp.transpose(sums, (1, 2, 0, 3))
    stats = jnp.stack([factors[0], factors[1], sums[0], sums[1]], axis=-1)
    grad_qkv, gain_parts = norm_back_call(
        place, projected, stats, gains, cosine, half_signs(sines, 1.0, -1.0), parts
    )
    qgain_part, kgain_part = jnp.split(gain_parts[0], 2)
    return grad_qkv, qgain_part, kgain_part, parts


def gathered_forward(projected, query_gain, key_gain, cosine, sines, model_width, early):
    queries, keys_proj, values_low = jnp.split(projected, 3, axis=-1)
    values_low = values_low.astype(BF16)
    exp_count, seq_count, shard_len, local_width = queries.shape
    ctx_count, ctx_place = lax.axis_size("ctx"), lax.axis_index("ctx")
    local_heads = local_width // HD
    ctx_rows = exp_count * shard_len
    half_rows = ctx_rows // 2
    squares = jnp.stack(
        [jnp.sum(queries * queries, axis=-1), jnp.sum(keys_proj * keys_proj, axis=-1)]
    )
    squares = lax.psum(squares, "exp")
    factors = lax.rsqrt(squares[..., None] / model_width + norm_eps)
    query_unit = queries * factors[0]
    key_unit = keys_proj * factors[1]

    def heads(values):
        values = values.reshape(exp_count, seq_count, shard_len, local_heads, HD)
        return jnp.transpose(values, (1, 0, 2, 3, 4)).reshape(seq_count, ctx_rows, local_heads, HD)

    def rotated(values):
        values = heads(values)
        return (values * cosine[:, None, :] + turn(values) * sines[:, None, :]).astype(BF16)

    query_rot = rotated(query_unit * query_gain)
    keys_all = lax.all_gather(rotated(key_unit * key_gain), "ctx", axis=1, tiled=True)
    values_all = lax.all_gather(heads(values_low), "ctx", axis=1, tiled=True)
    tools = block_tools(half_rows, ctx_count, ctx_place)
    block_len, half_firsts, row_start, block_scores = tools
    attended_halves = []
    log_halves = []
    for half_index in range(2):
        query_half = query_rot[:, half_index * half_rows : (half_index + 1) * half_rows]
        query_first = half_firsts[half_index]
        needed_blocks = (query_first + half_rows) // block_len

        def step(counter, carried):
            running_max, running_sum, acc = carried
            key_first = counter * block_len
            start_row = row_start(key_first)
            key_block = lax.dynamic_slice_in_dim(keys_all, start_row, block_len, 1)
            value_block = lax.dynamic_slice_in_dim(values_all, start_row, block_len, 1)
            scores = block_scores(query_half, query_first, key_block, key_first)
            new_max = jnp.maximum(running_max, jnp.max(scores, axis=-1))
            fade = jnp.exp(running_max - new_max)
            probs = jnp.exp(scores - new_max[..., None])
            running_sum = running_sum * fade + jnp.sum(probs, axis=-1)
            acc = acc * jnp.transpose(fade, (0, 2, 1))[..., None] + jnp.einsum(
                "shqk,skhd->sqhd", probs.astype(BF16), value_block, preferred_element_type=F32
            )
            return (new_max, running_sum, acc)

        stat_shape = (seq_count, local_heads, half_rows)
        running_max, running_sum, acc = lax.fori_loop(
            0,
            needed_blocks,
            step,
            (
                jnp.full(stat_shape, masked_score, F32),
                jnp.zeros(stat_shape, F32),
                jnp.zeros((seq_count, half_rows, local_heads, HD), F32),
            ),
        )
        attended_halves.append(acc / jnp.transpose(running_sum, (0, 2, 1))[..., None])
        log_halves.append(running_max + jnp.log(running_sum))
    attended_float = jnp.concatenate(attended_halves, axis=1)
    attended = jnp.transpose(attended_float.astype(BF16), (0, 2, 1, 3)).reshape(-1, ctx_rows, HD)
    kept = (
        query_rot, keys_all, values_all, attended_float, log_halves, query_unit, key_unit, factors
    )
    sent = jnp.transpose(attended.reshape(-1, exp_count, shard_len, HD), (1, 0, 2, 3))
    own = lax.all_to_all(sent, "exp", split_axis=0, concat_axis=0, tiled=True)
    own = own.reshape(exp_count, seq_count, local_heads, shard_len, HD)
    own = jnp.transpose(own, (1, 3, 0, 2, 4)).reshape(seq_count * shard_len, -1)
    return (own, attended), kept


def block_tools(half_rows, ctx_count, ctx_place):
    block_len = math.gcd(half_rows, 512)
    far_first = (2 * ctx_count - 1 - ctx_place) * half_rows
    half_firsts = (ctx_place * half_rows, far_first)

    def row_start(first_pos):
        segment = first_pos // half_rows
        offset = first_pos % half_rows
        return jnp.where(
            segment < ctx_count,
            segment * 2 * half_rows + offset,
            (2 * ctx_count - 1 - segment) * 2 * half_rows + half_rows + offset,
        )

    def block_scores(query_block, query_first, key_block, key_first):
        scores = jnp.einsum("sqhd,skhd->shqk", query_block, key_block, preferred_element_type=F32)
        scores = scores * (1.0 / math.sqrt(HD))
        query_line = query_first + jnp.arange(query_block.shape[1], dtype=jnp.int32)
        key_line = key_first + jnp.arange(key_block.shape[1], dtype=jnp.int32)
        return jnp.where(key_line[None, :] <= query_line[:, None], scores, masked_score)

    return block_len, half_firsts, row_start, block_scores


def gathered_backward(
    kept, grads, query_gain, key_gain, cosine, sines, model_width, early, later
):
    query_rot, keys_all, values_all, attended_float, log_halves, query_unit, key_unit, factors = kept
    exp_count, seq_count, shard_len, local_width = query_unit.shape
    ctx_count, ctx_place = lax.axis_size("ctx"), lax.axis_index("ctx")
    local_heads = local_width // HD
    ctx_rows = exp_count * shard_len
    half_rows = ctx_rows // 2
    seq_len = keys_all.shape[1]
    score_scale = 1.0 / math.sqrt(HD)
    block_len, half_firsts, row_start, block_scores = block_tools(half_rows, ctx_count, ctx_place)
    grad_heads = jnp.transpose(
        grads.reshape(seq_count, local_heads, ctx_rows, HD), (0, 2, 1, 3)
    )
    delta_rows = jnp.transpose(jnp.sum(grad_heads.astype(F32) * attended_float, axis=-1), (0, 2, 1))
    keyval_grads = jnp.zeros((seq_count, seq_len, 2 * local_width), F32)
    query_halves = []
    for half_index in range(2):
        row_slice = slice(half_index * half_rows, (half_index + 1) * half_rows)
        query_half = query_rot[:, row_slice]
        grad_half = grad_heads[:, row_slice]
        delta_half = delta_rows[:, :, row_slice]
        log_total = log_halves[half_index]
        query_first = half_firsts[half_index]
        needed_blocks = (query_first + half_rows) // block_len

        def one_block(counter, inner):
            query_acc, keyval_acc = inner
            key_first = counter * block_len
            start_row = row_start(key_first)
            key_block = lax.dynamic_slice_in_dim(keys_all, start_row, block_len, 1)
            value_block = lax.dynamic_slice_in_dim(values_all, start_row, block_len, 1)
            scores = block_scores(query_half, query_first, key_block, key_first)
            soft_probs = jnp.exp(scores - log_total[..., None])
            grad_probs = jnp.einsum(
                "sqhd,skhd->shqk", grad_half, value_block, preferred_element_type=F32
            )
            grad_scores = (soft_probs * (grad_probs - delta_half[..., None])).astype(BF16)
            query_acc = query_acc + score_scale * jnp.einsum(
                "shqk,skhd->sqhd", grad_scores, key_block, preferred_element_type=F32
            )
            kblock_grad = score_scale * jnp.einsum(
                "shqk,sqhd->skhd", grad_scores, query_half, preferred_element_type=F32
            )
            vblock_grad = jnp.einsum(
                "shqk,sqhd->skhd", soft_probs.astype(BF16), grad_half, preferred_element_type=F32
            )
            flat = (seq_count, block_len, local_width)
            combined = jnp.concatenate([kblock_grad.reshape(flat), vblock_grad.reshape(flat)], -1)
            keyval_acc = lax.dynamic_update_slice_in_dim(
                keyval_acc,
                lax.dynamic_slice_in_dim(keyval_acc, start_row, block_len, 1) + combined,
                start_row,
                1,
            )
            return (query_acc, keyval_acc)

        query_acc, keyval_grads = lax.fori_loop(
            0,
            needed_blocks,
            one_block,
            (jnp.zeros((seq_count, half_rows, local_heads, HD), F32), keyval_grads),
        )
        query_halves.append(query_acc)
    query_back = jnp.concatenate(query_halves, axis=1)
    keyval_local = lax.psum_scatter(keyval_grads, "ctx", scatter_dimension=1, tiled=True)

    def by_row(values):
        values = values.reshape(seq_count, exp_count, shard_len, local_width)
        return jnp.transpose(values, (1, 0, 2, 3))

    def unrotated(values):
        values = values.reshape(seq_count, ctx_rows, local_heads, HD)
        return by_row(values * cosine[:, None, :] + turn_back(values) * sines[:, None, :])

    qnorm_grad = unrotated(query_back)
    knorm_grad = unrotated(keyval_local[..., :local_width])
    grad_values = by_row(keyval_local[..., local_width:].astype(BF16))
    qgain_part = jnp.sum(qnorm_grad * query_unit, axis=(0, 1, 2))
    kgain_part = jnp.sum(knorm_grad * key_unit, axis=(0, 1, 2))
    qunit_grad = qnorm_grad * query_gain
    kunit_grad = knorm_grad * key_gain
    dots = jnp.stack(
        [jnp.sum(qunit_grad * query_unit, axis=-1), jnp.sum(kunit_grad * key_unit, axis=-1)]
    )
    dots = lax.psum(dots, "exp")[..., None] / model_width
    grad_queries = (factors[0] * (qunit_grad - query_unit * dots[0])).astype(BF16)
    grad_keys = (factors[1] * (kunit_grad - key_unit * dots[1])).astype(BF16)
    later[0](grad_heads)
    grad_qkv = jnp.concatenate([grad_queries, grad_keys, grad_values], axis=-1)
    return grad_qkv, qgain_part, kgain_part, dots


NT = (((1,), (1,)), ((), ()))
TN = (((0,), (0,)), ((), ()))
EXPERT_PARAMS = pltpu.CompilerParams(vmem_limit_bytes=58 * 2**20)


def down_kernel(half_ref, rows_ref, weight_ref, out_ref):
    out_ref[0] = dot32(rows_ref[...], weight_ref[0, 0])


def down_call(rows, weights, half, width):
    count, model_width = rows.shape
    experts = weights.shape[0]
    tile, cols = math.gcd(count, 1024), math.gcd(width, 1024)
    parts = width // cols
    return pl.pallas_call(
        down_kernel,
        grid_spec=pltpu.PrefetchScalarGridSpec(
            num_scalar_prefetch=1,
            grid=(experts, parts, count // tile),
            in_specs=[
                pl.BlockSpec((tile, model_width), lambda e, f, r, h: (r, 0)),
                pl.BlockSpec(
                    (1, 1, model_width, cols), lambda e, f, r, h: (e, 2, 0, h[0] * parts + f)
                ),
            ],
            out_specs=pl.BlockSpec((1, tile, cols), lambda e, f, r, h: (e, r, f)),
        ),
        out_shape=jax.ShapeDtypeStruct((experts, count, width), F32),
        compiler_params=EXPERT_PARAMS,
        cost_estimate=SMALL,
        name="down",
    )(half, rows, weights)


def hidden_kernel(
    half_ref, rows_ref, wg_ref, wu_ref, down_ref, gate_ref, gm_ref, gg_ref, gu_ref, *dots, chunk
):
    width = wg_ref.shape[-1]

    def step(i, unused):
        at = pl.ds(pl.multiple_of(i * chunk, chunk), chunk)
        rows = rows_ref[at, :]
        pre_gate = dot32(rows, wg_ref[0, 0])
        pre_up = dot32(rows, wu_ref[0, 0])
        down, gate = down_ref[0, at, :], gate_ref[0, at, :]
        sigmoid_vals = 1.0 / (1.0 + jnp.exp(-pre_gate))
        activated = pre_gate * sigmoid_vals
        middle = activated * pre_up
        for dot_ref in dots:
            products = middle * down
            acc = products[:, :128]
            for c in range(1, width // 128):
                acc = acc + products[:, c * 128 : (c + 1) * 128]
            dot_ref[0, 0, at, :] = acc
        gm_ref[0, at, :] = (gate * middle).astype(BF16)
        grad = gate * down
        gu_ref[0, at, :] = (grad * activated).astype(BF16)
        slope = sigmoid_vals * (1.0 + pre_gate * (1.0 - sigmoid_vals))
        gg_ref[0, at, :] = (grad * pre_up * slope).astype(BF16)
        return unused

    lax.fori_loop(0, rows_ref.shape[0] // chunk, step, 0)


def hidden_call(rows, weights, down, gates, half, with_dots):
    count, model_width = rows.shape
    experts, width = weights.shape[0], down.shape[-1]
    tile, cols = math.gcd(count, 1024), math.gcd(width, 512)
    parts = width // cols
    wide = pl.BlockSpec((1, tile, cols), lambda e, f, r, h: (e, r, f))
    shape = jax.ShapeDtypeStruct((experts, count, width), BF16)
    out_specs, out_shape = [wide] * 3, [shape] * 3
    if with_dots:
        out_specs.append(pl.BlockSpec((1, 1, tile, 128), lambda e, f, r, h: (e, f, r, 0)))
        out_shape.append(jax.ShapeDtypeStruct((experts, parts, count, 128), F32))

    def weight_spec(which):
        return pl.BlockSpec(
            (1, 1, model_width, cols), lambda e, f, r, h: (e, which, 0, h[0] * parts + f)
        )

    return pl.pallas_call(
        functools.partial(hidden_kernel, chunk=math.gcd(tile, 256)),
        grid_spec=pltpu.PrefetchScalarGridSpec(
            num_scalar_prefetch=1,
            grid=(experts, parts, count // tile),
            in_specs=[
                pl.BlockSpec((tile, model_width), lambda e, f, r, h: (r, 0)),
                weight_spec(0),
                weight_spec(1),
                wide,
                pl.BlockSpec((1, tile, 1), lambda e, f, r, h: (e, r, 0)),
            ],
            out_specs=out_specs,
        ),
        out_shape=out_shape,
        compiler_params=EXPERT_PARAMS,
        cost_estimate=SMALL,
        name="hidden",
    )(half, rows, weights, weights, down, gates)


def back_kernel(*refs, count, chunk):
    a_refs, b_refs, out_ref, acc_ref = refs[:count], refs[count : 2 * count], refs[-2], refs[-1]
    turn_at = pl.program_id(2)

    def step(i, unused):
        at = pl.ds(pl.multiple_of(i * chunk, chunk), chunk)
        total = None
        for a, b in zip(a_refs, b_refs):
            term = lax.dot_general(a[0, at, :], b[0, 0], NT, preferred_element_type=F32)
            total = term if total is None else total + term

        @pl.when(turn_at == 0)
        def first():
            acc_ref[at, :] = total

        @pl.when(turn_at > 0)
        def later():
            acc_ref[at, :] += total

        return unused

    lax.fori_loop(0, out_ref.shape[0] // chunk, step, 0)

    @pl.when(turn_at == pl.num_programs(2) - 1)
    def last():
        out_ref[...] = acc_ref[...].astype(out_ref.dtype)


def back_call(parts, weights, which, kind=BF16, *after, cost=SMALL):
    experts, count, width = parts[0].shape
    model_width = weights.shape[2]
    tile, cols = math.gcd(count, 512), math.gcd(model_width, 2048)

    def weight_spec(k):
        return pl.BlockSpec((1, 1, cols, width), lambda d, r, e: (e, k, d, 0))

    return pl.pallas_call(
        functools.partial(back_kernel, count=len(parts), chunk=math.gcd(tile, 256)),
        grid=(model_width // cols, count // tile, experts),
        in_specs=[pl.BlockSpec((1, tile, width), lambda d, r, e: (e, r, 0))] * len(parts)
        + [weight_spec(k) for k in which]
        + [pl.BlockSpec(memory_space=pl.ANY)] * len(after),
        out_specs=pl.BlockSpec((tile, cols), lambda d, r, e: (r, d)),
        out_shape=jax.ShapeDtypeStruct((count, model_width), kind),
        scratch_shapes=[pltpu.VMEM((tile, cols), F32)],
        compiler_params=EXPERT_PARAMS,
        cost_estimate=cost,
        name="back",
    )(*parts, *([weights] * len(parts)), *after)


def grad_kernel(half_ref, own_rows, own_grads, near_rows, near_grads, *refs):
    total = lax.dot_general(own_rows[...], own_grads[0], TN, preferred_element_type=F32)
    total += lax.dot_general(near_rows[...], near_grads[0], TN, preferred_element_type=F32)
    refs[-1][...] = total.astype(BF16)


def grad_call(own_rows, own_grads, near_rows, near_grads, half, *after):
    count, model_width = own_rows.shape
    experts, _, width = near_grads.shape
    shards = lax.axis_size("ctx")
    cols = math.gcd(model_width // shards, 512)
    tiles = model_width // shards // cols
    row_spec = pl.BlockSpec((count, cols), lambda e, d, h: (0, d))

    def scatter_order(tile, half):
        shard = tile // tiles
        apart = jnp.where(half == 0, shard, shards - 1 - shard)
        near = apart < shards // 2
        step = jnp.where(half == 0, shard, shard - shards // 2)
        step = jnp.where(near, step, jnp.where(half == 0, shards - 1 - shard, shards // 2 - 1 - shard))
        return (2 * step + jnp.where(near, 0, 1)) * tiles + tile % tiles

    return pl.pallas_call(
        grad_kernel,
        grid_spec=pltpu.PrefetchScalarGridSpec(
            num_scalar_prefetch=1,
            grid=(experts, model_width // cols),
            in_specs=[
                row_spec,
                pl.BlockSpec((1, count, width), lambda e, d, h: (e, 0, h[0])),
                row_spec,
                pl.BlockSpec((1, count, width), lambda e, d, h: (e, 0, 0)),
            ]
            + [pl.BlockSpec(memory_space=pl.ANY)] * len(after),
            out_specs=pl.BlockSpec(
                (cols, width), lambda e, d, h: (scatter_order(d, h[0]), e)
            ),
        ),
        out_shape=jax.ShapeDtypeStruct((model_width, experts * width), BF16),
        compiler_params=EXPERT_PARAMS,
        cost_estimate=SMALL,
        name="grad",
    )(half, own_rows, own_grads, near_rows, near_grads, *after)


def scatter_rows(term):
    count = lax.axis_size("ctx")
    groups = [list(range(count // 2)), list(range(count // 2, count))]
    return lax.psum_scatter(
        term, "ctx", scatter_dimension=0, axis_index_groups=groups, tiled=True
    )


def swap_rows(term):
    size = term.shape[0] // 2
    return flip(term[size:], "ctx", lax.axis_size("ctx") - 1), term[:size]


def body(
    block_input,
    attend_gain,
    w_query,
    w_key,
    w_value,
    w_out,
    query_gain,
    key_gain,
    expert_gain,
    router,
    expert_weights,
    routes,
    cotangent,
):
    exp_count, ctx_count = lax.axis_size("exp"), lax.axis_size("ctx")
    ctx_place, exp_place = lax.axis_index("ctx"), lax.axis_index("exp")
    seq_count, shard_len, model_width = block_input.shape
    local_width = w_query.shape[1]
    local_heads = local_width // HD
    experts_all = router.shape[1]
    experts_here = expert_weights.shape[1]
    hidden_units = expert_weights.shape[3]
    rows_dev = seq_count * shard_len
    rows_all = exp_count * rows_dev
    ctx_rows = exp_count * shard_len
    half_rows = ctx_rows // 2
    pair_count = seq_count * local_heads
    paired = pair_count == ctx_count and half_rows % 128 == 0

    def gather(values):
        return lax.all_gather(values, "exp", axis=0, tiled=False)

    mirror = ctx_count - 1
    half = (ctx_place * 2 // ctx_count).astype(jnp.int32).reshape(1)
    whole = jnp.zeros((1,), jnp.int32)
    local_float = block_input.astype(F32).reshape(rows_dev, model_width)
    local_factor = rms_factor(local_float)
    local_unit = local_float * local_factor
    normed = gather((local_unit * attend_gain).astype(BF16)).reshape(rows_all, model_width)
    weights = jnp.transpose(expert_weights, (1, 2, 0, 3))
    w_qkv = jnp.concatenate([w_query, w_key, w_value], axis=1)
    own_routes = jnp.transpose(routes, (1, 0, 2)).reshape(rows_dev, TOP)
    own_grads = cotangent.reshape(rows_dev, model_width)
    grad_low = gather(own_grads).reshape(rows_all, model_width)
    full_out = gather(w_out).reshape(exp_count * local_width, model_width)
    near_low = gather(hold(flip(own_grads, "ctx", mirror), weights)).reshape(rows_all, model_width)
    all_routes = gather(own_routes).reshape(rows_all, TOP)
    near_routes = flip(all_routes, "ctx", mirror)
    w_qkv = hold(w_qkv, weights, near_routes)
    grad_down = down_call(grad_low, weights, whole, hidden_units)
    near_down = down_call(near_low, weights, half, hidden_units // 2)

    projected = dot32(normed, w_qkv).reshape(exp_count, seq_count, shard_len, 3 * local_width)
    row_ids = jnp.arange(ctx_rows, dtype=jnp.int32)
    far_first = (2 * ctx_count - 1 - ctx_place) * half_rows
    query_pos = jnp.where(
        row_ids < half_rows, ctx_place * half_rows + row_ids, far_first + row_ids - half_rows
    )
    cosine, sines = rotary_tables(query_pos, HD)
    forward, backward = (
        (paired_forward, paired_backward) if paired else (gathered_forward, gathered_backward)
    )
    (own_attended, attended), kept = forward(
        projected, query_gain, key_gain, cosine, sines, model_width, grad_down
    )

    def exchange(values):
        return lax.all_to_all(values, "exp", split_axis=0, concat_axis=0, tiled=True)

    hidden = local_float + dot32(own_attended, full_out)
    hidden_factor = rms_factor(hidden)
    unit_second = hidden * hidden_factor
    own_mixed = (unit_second * expert_gain).astype(BF16)

    expert_ids = jnp.arange(experts_all, dtype=jnp.int32)

    def chosen(table):
        return jnp.any(table[:, :, None] == expert_ids[None, None, :], axis=1)

    own_prob = jax.nn.softmax(dot32(own_mixed, router), axis=-1)

    def local_gates(rows, table):
        prob = jax.nn.softmax(dot32(rows, router), axis=-1)
        gates = jnp.where(chosen(table), prob, 0.0)
        gates = lax.dynamic_slice_in_dim(gates, exp_place * experts_here, experts_here, 1)
        return jnp.transpose(gates)[:, :, None]

    mixed = hold(gather(own_mixed).reshape(rows_all, model_width), near_down)
    near_mixed = gather(hold(flip(own_mixed, "ctx", mirror), near_down))
    gates = local_gates(mixed, all_routes)

    gated_middle, grad_gate, grad_up, dots = hidden_call(
        mixed, weights, grad_down, gates, whole, True
    )
    gate_grads = jnp.sum(dots, axis=(1, 3))
    choice_grad = exchange(
        jnp.transpose(gate_grads.reshape(experts_here, exp_count, rows_dev), (1, 0, 2))
    )
    slot_rows = back_call([grad_gate, grad_up], weights, (0, 1), BF16)
    if paired:
        attended = return_pairs(hold(attended, gated_middle))
    slot_both, slot_own = reduce_start(slot_rows.reshape(exp_count, rows_dev, model_width))
    slot_parts = reduce_send(slot_both)
    near_mixed = hold(
        near_mixed.reshape(rows_all, model_width), slot_both, choice_grad
    )
    near_gates = local_gates(near_mixed, near_routes)
    near_middle, near_grad_gate, near_grad_up = hidden_call(
        near_mixed, weights, near_down, near_gates, half, False
    )

    down_term = grad_call(
        grad_low, gated_middle, near_low, near_middle, half, attended, *slot_parts
    )
    slot_sum = reduce_total(slot_parts, slot_own)

    choice_grad = jnp.transpose(choice_grad, (2, 0, 1)).reshape(rows_dev, experts_all)
    choice_grad = jnp.where(chosen(own_routes), choice_grad, 0.0)
    logit_grad = (
        own_prob * (choice_grad - jnp.sum(own_prob * choice_grad, axis=-1, keepdims=True))
    ).astype(BF16)
    router_part = jnp.einsum("td,te->de", own_mixed, logit_grad, preferred_element_type=F32)
    mixed_grad = slot_sum + jnp.einsum(
        "te,de->td", logit_grad, router, preferred_element_type=F32
    )
    egain_part = jnp.sum(mixed_grad * unit_second, axis=0)
    usecond_grad = mixed_grad * expert_gain
    grad_rows = cotangent.astype(F32).reshape(rows_dev, model_width)
    grad_hidden = (
        hidden_factor
        * (usecond_grad - unit_second * jnp.mean(usecond_grad * unit_second, axis=-1, keepdims=True))
        + grad_rows
    )
    own_branch = grad_hidden.astype(BF16)
    early_part = jnp.concatenate([router_part, egain_part[:, None]], axis=1)
    early_part = exchange(early_part.reshape(exp_count, -1, experts_all + 1))

    grad_attended = jnp.einsum(
        "rd,hd->rh", own_branch, full_out, preferred_element_type=F32
    ).astype(BF16)
    sent = grad_attended.reshape(seq_count, shard_len, exp_count, local_heads, HD)
    sent = jnp.transpose(sent, (2, 0, 3, 1, 4)).reshape(exp_count, pair_count, shard_len, HD)
    grads = jnp.transpose(exchange(sent), (1, 0, 2, 3)).reshape(pair_count, ctx_rows, HD)
    gate_term = grad_call(mixed, grad_gate, near_mixed, near_grad_gate, half, grads)
    down_sum, gate_sum = scatter_rows(down_term), scatter_rows(gate_term)
    def place_rows(whole_grad, halves, which, *after):
        sent_rows, kept_rows = halves
        sent_rows = hold(sent_rows, *after)
        lower = jnp.where(half[0] == 0, kept_rows, sent_rows)
        upper = jnp.where(half[0] == 0, sent_rows, kept_rows)
        parts = [
            v.astype(F32).reshape(-1, experts_here, hidden_units // 2) for v in (lower, upper)
        ]
        part = jnp.concatenate(parts, axis=-1)[:, None]
        return lax.dynamic_update_slice_in_dim(whole_grad, part, which, 1)

    down_swapped = swap_rows(hold(down_sum, grads))
    branch_rows = gather(hold(own_branch, gate_term))
    late_terms = []

    def meanwhile(sums):
        up_term = grad_call(
            mixed, grad_up, near_mixed, near_grad_up, half, sums
        )
        up_sum = scatter_rows(up_term)
        cost = pl.CostEstimate(
            flops=16 * rows_all * model_width * experts_here * hidden_units,
            bytes_accessed=0,
            transcendentals=0,
        )
        expert_out = back_call([gated_middle], weights, (2,), BF16, up_term, cost=cost)
        late_terms.append((up_sum, expert_out))
        return expert_out

    grad_qkv, qgain_part, kgain_part, ended = backward(
        kept, grads, query_gain, key_gain, cosine, sines, model_width, (gate_term, early_part), (meanwhile, down_swapped[0])
    )
    attended_rows = attended.reshape(seq_count, local_heads, exp_count, shard_len, HD)
    up_sum, expert_out = late_terms[0]
    early_sum = jnp.sum(early_part, axis=0)
    gain_parts = [v[:, None] for v in (qgain_part, kgain_part)]
    sums = butterfly_sum(jnp.concatenate([early_sum] + gain_parts, axis=1), "ctx")
    gate_swapped = swap_rows(hold(gate_sum, sums))
    grad_qkv = hold(grad_qkv, gate_swapped[0], up_sum)
    branch_rows = hold(branch_rows, ended)
    branch_rows = branch_rows.reshape(exp_count, seq_count, shard_len, model_width)
    outw_part = jnp.einsum(
        "shetc,estd->dhc", attended_rows, branch_rows, preferred_element_type=F32
    ).reshape(model_width, local_width)
    qkv_part = jnp.einsum(
        "rd,rh->dh", normed, grad_qkv.reshape(rows_all, -1), preferred_element_type=F32
    )
    proj_part = jnp.concatenate([qkv_part.astype(BF16), outw_part.astype(BF16)], axis=1)
    proj_sum = lax.psum_scatter(proj_part, "ctx", scatter_dimension=0, tiled=True)

    w_qkv = jnp.concatenate([w_query, w_key, w_value], axis=1)
    grad_rows_qkv = grad_qkv.reshape(1, rows_all, -1)
    normed_back = back_call(
        [grad_rows_qkv], w_qkv[None, None], (0,), BF16, proj_part
    )
    normed_both, normed_own = reduce_start(normed_back.reshape(exp_count, rows_dev, model_width))
    normed_parts = reduce_send(normed_both)
    up_swapped = swap_rows(hold(up_sum, proj_part))
    grad_normed = reduce_total(normed_parts, normed_own, up_swapped[0])
    attend_part = jnp.sum(grad_normed * local_unit, axis=0)
    attend_sum = jnp.sum(exchange(attend_part.reshape(exp_count, -1)), axis=0)
    attend_grad = butterfly_sum(attend_sum, "ctx")
    proj_sum = hold(proj_sum, attend_grad)
    proj_grad = lax.all_gather(proj_sum, "ctx", axis=0, tiled=True)
    lunit_grad = grad_normed * attend_gain
    input_grad = grad_hidden + local_factor * (
        lunit_grad - local_unit * jnp.mean(lunit_grad * local_unit, axis=-1, keepdims=True)
    )
    expert_grad = jnp.zeros((model_width // ctx_count, 3, experts_here, hidden_units), F32)
    expert_grad = place_rows(expert_grad, down_swapped, 2, normed_both)
    expert_grad = place_rows(expert_grad, gate_swapped, 0, normed_both)
    expert_grad = place_rows(expert_grad, up_swapped, 1, grad_normed)
    produced = hold(expert_out, normed_both).reshape(exp_count, rows_dev, model_width)
    mixture = reduce_finish(*reduce_start(produced), grad_normed)
    block_output = (hidden + mixture).astype(BF16).reshape(block_input.shape)

    proj_grad = hold(proj_grad, input_grad, block_output, expert_grad).astype(F32)
    grads_of = [proj_grad[:, i * local_width : (i + 1) * local_width] for i in range(4)]
    return (
        block_output,
        input_grad.reshape(block_input.shape),
        attend_grad,
        *grads_of[:3],
        grads_of[3].T,
        sums[:, experts_all + 1],
        sums[:, experts_all + 2],
        sums[:, experts_all],
        sums[:, :experts_all],
        jnp.transpose(expert_grad, (0, 2, 1, 3)),
    )


def solution(mesh):
    placed = (
        P(None, ("ctx", "exp"), None),
        P(),
        P(None, "exp"),
        P(None, "exp"),
        P(None, "exp"),
        P("exp", None),
        P("exp"),
        P("exp"),
        P(),
        P(),
        P(None, "exp", None, None),
        P(("ctx", "exp"), None, None),
        P(None, ("ctx", "exp"), None),
    )
    return jax.shard_map(
        body,
        mesh=mesh,
        in_specs=placed,
        out_specs=(
            P(None, ("ctx", "exp"), None),
            P(None, ("ctx", "exp"), None),
            P("exp"),
            P(None, "exp"),
            P(None, "exp"),
            P(None, "exp"),
            P("exp", None),
            P("exp"),
            P("exp"),
            P("exp"),
            P("exp", None),
            P("ctx", "exp", None, None),
        ),
        check_vma=False,
    )
```

```python
import functools
import math

import jax
import jax.numpy as jnp
from jax import lax
from jax.experimental import pallas as pl
from jax.experimental.pallas import tpu as pltpu
from jax.sharding import PartitionSpec as P

HD = 128
TOP = 8


norm_eps = 1e-05
rope_base = 10000.0
masked_score = -1e30
LOG2E = 1.4426950408889634
F32 = jnp.float32
SMALL = pl.CostEstimate(flops=0, bytes_accessed=0, transcendentals=0)
BF16 = jnp.bfloat16


def rms_factor(values):
    return lax.rsqrt(jnp.mean(values * values, axis=-1, keepdims=True) + norm_eps)


def rotary_tables(positions, head_size):
    half_size = head_size // 2
    inverse_freq = rope_base ** (-(jnp.arange(half_size, dtype=F32) * 2.0) / head_size)
    angles = positions.astype(F32)[:, None] * inverse_freq[None, :]
    angles = jnp.concatenate([angles, angles], axis=1)
    return (jnp.cos(angles), jnp.sin(angles))


def turn(values):
    half_size = values.shape[-1] // 2
    return jnp.concatenate([-values[..., half_size:], values[..., :half_size]], axis=-1)


def turn_back(values):
    half_size = values.shape[-1] // 2
    return jnp.concatenate([values[..., half_size:], -values[..., :half_size]], axis=-1)


def dot32(a, b):
    return jnp.dot(a, b, preferred_element_type=F32)


def flip(values, axis, mask):
    return lax.ppermute(values, axis, [(i, i ^ mask) for i in range(lax.axis_size(axis))])


def pick(values, index, axis=0):
    return lax.dynamic_index_in_dim(values, index, axis, keepdims=False)


def hold_kernel(*refs):
    del refs


def hold(value, *after):
    return pl.pallas_call(
        hold_kernel,
        out_shape=jax.ShapeDtypeStruct(value.shape, value.dtype),
        in_specs=[pl.BlockSpec(memory_space=pl.ANY)] * (1 + len(after)),
        out_specs=pl.BlockSpec(memory_space=pl.ANY),
        input_output_aliases={0: 0},
        cost_estimate=SMALL,
        name="hold",
    )(value, *after)


def butterfly_sum(values, axis):
    mask = 1
    while mask < lax.axis_size(axis):
        values = jax.tree.map(lambda v: v + flip(v, axis, mask), values)
        mask *= 2
    return values


def reduce_start(partial):
    count = partial.shape[0]
    me = lax.axis_index("exp")
    core, chip = me % 2, me // 2
    pairs = partial.reshape((count // 2, 2) + partial.shape[1:])
    got = flip(pick(pairs, 1 - core, 1), "exp", 1)
    mine = pick(pairs, core, 1)
    both = (mine.astype(F32) + got.astype(F32)).astype(BF16)
    return both, (pick(mine, chip), pick(got, chip))


def reduce_send(both):
    chip = lax.axis_index("exp") // 2
    return [flip(pick(both, chip ^ m), "exp", 2 * m) for m in range(1, both.shape[0])]


def reduce_total(parts, own, *after):
    parts = [hold(part, *after) for part in parts] if after else parts
    total = own[0].astype(F32) + own[1].astype(F32)
    for part in parts:
        total = total + part.astype(F32)
    return total


def reduce_finish(both, own, *after):
    return reduce_total(reduce_send(both), own, *after)


def reduce_rows(partial, *after):
    return reduce_finish(*reduce_start(partial), *after)


def block_place(block, ctx_count, place):
    late = block >= ctx_count
    owner = jnp.where(late, 2 * ctx_count - 1 - block, block)
    return owner ^ place, jnp.where(late, 1, 0)


def causal_mask(rows):
    key_line = lax.broadcasted_iota(jnp.int32, (rows, rows), 0)
    query_line = lax.broadcasted_iota(jnp.int32, (rows, rows), 1)
    return key_line <= query_line


def attend_kernel(place_ref, qk_ref, v_ref, o_ref, ot_ref, lse_ref, qt_ref, vt_ref):
    ctx_count, rows = v_ref.shape[0], v_ref.shape[1] // 2
    blocks = 2 * ctx_count
    place = place_ref[0]
    scale = LOG2E / math.sqrt(HD)

    def lay(block, unused):
        slab, half = block_place(block, ctx_count, place)
        at = pl.ds(pl.multiple_of(half * rows, rows), rows)
        to = pl.ds(pl.multiple_of(block * rows, rows), rows)
        qt_ref[:, to] = qk_ref[slab, 0, at, :].T
        vt_ref[:, to] = v_ref[slab, at, :].T
        return unused

    lax.fori_loop(0, blocks, lay, 0)

    def query_block(block, unused):
        cols = pl.ds(pl.multiple_of(block * rows, rows), rows)
        query = qt_ref[:, cols]

        def part(key_block, carried, masked):
            high, total, acc = carried
            slab, half = block_place(key_block, ctx_count, place)
            at = pl.ds(pl.multiple_of(half * rows, rows), rows)
            scores = dot32(qk_ref[slab, 1, at, :], query) * scale
            if masked:
                scores = jnp.where(causal_mask(rows), scores, masked_score)
            new_high = jnp.maximum(high, jnp.max(scores, axis=0, keepdims=True))
            probs = jnp.exp2(scores - new_high)
            fade = jnp.exp2(high - new_high)
            total = total * fade + jnp.sum(probs, axis=0, keepdims=True)
            keys = pl.ds(pl.multiple_of(key_block * rows, rows), rows)
            acc = acc * fade + dot32(vt_ref[:, keys], probs.astype(BF16))
            return new_high, total, acc

        start = (
            jnp.full((1, rows), masked_score, F32),
            jnp.zeros((1, rows), F32),
            jnp.zeros((HD, rows), F32),
        )
        state = part(block, start, True)
        high, total, acc = lax.fori_loop(0, block, lambda j, c: part(j, c, False), state)
        out = acc / total
        ot_ref[:, cols] = out
        slab, half = block_place(block, ctx_count, place)
        o_ref[slab, pl.ds(pl.multiple_of(half * rows, rows), rows), :] = out.T.astype(BF16)
        lse_ref[block] = high + jnp.log2(total)
        return unused

    lax.fori_loop(0, blocks, query_block, 0)


def attend_back_kernel(
    place_ref,
    qk_ref,
    v_ref,
    do_ref,
    ot_ref,
    lse_ref,
    d_ref,
    sums_ref,
    qt_ref,
    kt_ref,
    dot_ref,
    dk_ref,
    dv_ref,
):
    ctx_count, rows = v_ref.shape[0], v_ref.shape[1] // 2
    blocks = 2 * ctx_count
    place = place_ref[0]
    score_scale = 1.0 / math.sqrt(HD)
    scale = LOG2E * score_scale

    def lay(block, unused):
        slab, half = block_place(block, ctx_count, place)
        at = pl.ds(pl.multiple_of(half * rows, rows), rows)
        to = pl.ds(pl.multiple_of(block * rows, rows), rows)
        qt_ref[:, to] = qk_ref[slab, 0, at, :].T
        kt_ref[:, to] = qk_ref[slab, 1, at, :].T
        dot_ref[:, to] = do_ref[slab, at, :].T
        dk_ref[to, :] = jnp.zeros((rows, HD), F32)
        dv_ref[to, :] = jnp.zeros((rows, HD), F32)
        return unused

    lax.fori_loop(0, blocks, lay, 0)

    def query_block(block, unused):
        cols = pl.ds(pl.multiple_of(block * rows, rows), rows)
        slab_q, half_q = block_place(block, ctx_count, place)
        at_q = pl.ds(pl.multiple_of(half_q * rows, rows), rows)
        query_t, grad_t = qt_ref[:, cols], dot_ref[:, cols]
        delta = jnp.sum(grad_t.astype(F32) * ot_ref[:, cols], axis=0, keepdims=True)
        lse = lse_ref[block]

        def part(key_block, dq, masked):
            slab, half = block_place(key_block, ctx_count, place)
            at = pl.ds(pl.multiple_of(half * rows, rows), rows)
            keys = pl.ds(pl.multiple_of(key_block * rows, rows), rows)
            probs = jnp.exp2(dot32(qk_ref[slab, 1, at, :], query_t) * scale - lse)
            if masked:
                probs = jnp.where(causal_mask(rows), probs, 0.0)
            grad_probs = dot32(v_ref[slab, at, :], grad_t)
            grad_scores = (probs * (grad_probs - delta)).astype(BF16)
            dv_ref[keys, :] += dot32(probs.astype(BF16), do_ref[slab_q, at_q, :])
            dk_ref[keys, :] += dot32(grad_scores, qk_ref[slab_q, 0, at_q, :])
            return dq + dot32(kt_ref[:, keys], grad_scores)

        dq = part(block, jnp.zeros((HD, rows), F32), True)
        dq = lax.fori_loop(0, block, lambda j, c: part(j, c, False), dq)
        dq = dq * score_scale
        d_ref[slab_q, 0, at_q, :] = dq.T.astype(BF16)
        sums = jnp.sum(dq * query_t.astype(F32), axis=0, keepdims=True)
        sums_ref[slab_q, pl.ds(half_q, 1), :] = sums
        return unused

    lax.fori_loop(0, blocks, query_block, 0)

    def give(block, unused):
        slab, half = block_place(block, ctx_count, place)
        at = pl.ds(pl.multiple_of(half * rows, rows), rows)
        to = pl.ds(pl.multiple_of(block * rows, rows), rows)
        dk = dk_ref[to, :] * score_scale
        d_ref[slab, 1, at, :] = dk.astype(BF16)
        sums = jnp.sum(dk.T * kt_ref[:, to].astype(F32), axis=0, keepdims=True)
        sums_ref[slab, pl.ds(2 + half, 1), :] = sums
        d_ref[slab, 2, at, :] = dv_ref[to, :].astype(BF16)
        return unused

    lax.fori_loop(0, blocks, give, 0)


VMEM = pl.BlockSpec(memory_space=pltpu.VMEM)
SMEM = pl.BlockSpec(memory_space=pltpu.SMEM)


def attend_call(place, qk, v):
    ctx_count, ctx_rows = v.shape[0], v.shape[1]
    length, rows = ctx_count * ctx_rows, ctx_rows // 2
    pairs = length * length // 2
    return pl.pallas_call(
        attend_kernel,
        out_shape=(
            jax.ShapeDtypeStruct(v.shape, BF16),
            jax.ShapeDtypeStruct((HD, length), F32),
            jax.ShapeDtypeStruct((2 * ctx_count, 1, rows), F32),
        ),
        in_specs=[SMEM, VMEM, VMEM],
        out_specs=(VMEM, VMEM, VMEM),
        scratch_shapes=[pltpu.VMEM((HD, length), BF16), pltpu.VMEM((HD, length), BF16)],
        compiler_params=pltpu.CompilerParams(vmem_limit_bytes=50 * 2**20),
        cost_estimate=SMALL,
        name="attend",
    )(place, qk, v)


def attend_back_call(place, qk, v, grads, out_t, lse):
    ctx_count, ctx_rows = v.shape[0], v.shape[1]
    length = ctx_count * ctx_rows
    pairs = length * length // 2
    return pl.pallas_call(
        attend_back_kernel,
        out_shape=(
            jax.ShapeDtypeStruct((ctx_count, 3, ctx_rows, HD), BF16),
            jax.ShapeDtypeStruct((ctx_count, 4, ctx_rows // 2), F32),
        ),
        in_specs=[SMEM] + [VMEM] * 5,
        out_specs=(VMEM, VMEM),
        scratch_shapes=[pltpu.VMEM((HD, length), BF16)] * 3 + [pltpu.VMEM((length, HD), F32)] * 2,
        compiler_params=pltpu.CompilerParams(vmem_limit_bytes=50 * 2**20),
        cost_estimate=pl.CostEstimate(
            flops=160 * length * length // 2 * HD, bytes_accessed=0, transcendentals=0
        ),
        name="attend_back",
    )(place, qk, v, grads, out_t, lse)


def spread_pairs(values, *after):
    count = values.shape[0]
    place = lax.axis_index("ctx")
    parts = [pick(values, place ^ m) for m in range(count)]
    parts[1:] = [flip(parts[m], "ctx", m) for m in range(1, count)]
    if after:
        parts[1:] = [hold(part, *after) for part in parts[1:]]
    return jnp.stack(parts)


def return_pairs(values):
    count = values.shape[0]
    place = lax.axis_index("ctx")
    parts = jnp.stack([values[0]] + [flip(values[m], "ctx", m) for m in range(1, count)])
    return jnp.stack([pick(parts, place ^ p) for p in range(count)])


def rotate_kernel(proj_ref, stat_ref, gain_ref, cos_ref, sin_ref, out_ref):
    heads, rows = out_ref.shape[1], proj_ref.shape[2]
    for group in range(proj_ref.shape[0]):
        line = slice(group * rows, (group + 1) * rows)
        cosine, sines = cos_ref[line, :], sin_ref[line, :]
        for which in range(2):
            factor = stat_ref[group, 0, :, which : which + 1]
            for head in range(heads):
                at = slice((which * heads + head) * HD, (which * heads + head + 1) * HD)
                unit = proj_ref[group, 0, :, at] * factor * gain_ref[:, at]
                turned = pltpu.roll(unit, HD // 2, 1)
                out_ref[0, head, which, line, :] = (unit * cosine + turned * sines).astype(BF16)


def rotate_call(projected, stats, gains, cosine, turn_sines):
    exp_count, seq_count, shard_len, width = projected.shape
    local_heads = width // 3 // HD
    group = math.gcd(exp_count, 4)
    shape = (seq_count, local_heads, 2, exp_count * shard_len, HD)
    line_spec = pl.BlockSpec((group * shard_len, HD), lambda s, e: (e, 0))
    out = pl.pallas_call(
        rotate_kernel,
        grid=(seq_count, exp_count // group),
        in_specs=[
            pl.BlockSpec((group, 1, shard_len, width), lambda s, e: (e, s, 0, 0)),
            pl.BlockSpec((group, 1, shard_len, stats.shape[-1]), lambda s, e: (e, s, 0, 0)),
            pl.BlockSpec((1, gains.shape[1]), lambda s, e: (0, 0)),
            line_spec,
            line_spec,
        ],
        out_specs=pl.BlockSpec(
            (1, local_heads, 2, group * shard_len, HD), lambda s, e: (s, 0, 0, e, 0)
        ),
        out_shape=jax.ShapeDtypeStruct(shape, BF16),
        cost_estimate=SMALL,
        name="rotate",
    )(projected, stats, gains, cosine, turn_sines)
    return out.reshape((-1,) + shape[2:])


def norm_back_kernel(place_ref, proj_ref, stat_ref, gain_ref, cos_ref, sin_ref, *refs):
    heads = len(refs) - 2
    back_refs, out_ref, sum_ref = refs[:heads], refs[heads], refs[heads + 1]
    rows = proj_ref.shape[2]

    @pl.when((pl.program_id(0) == 0) & (pl.program_id(1) == 0))
    def start():
        sum_ref[...] = jnp.zeros_like(sum_ref)

    for group in range(proj_ref.shape[0]):
        line = slice(group * rows, (group + 1) * rows)
        cosine, sines = cos_ref[line, :], sin_ref[line, :]
        for which in range(2):
            factor = stat_ref[group, 0, :, which : which + 1]
            mean = stat_ref[group, 0, :, 2 + which : 3 + which]
            for head in range(heads):
                at = slice((which * heads + head) * HD, (which * heads + head + 1) * HD)
                grad = back_refs[head][0, which, line, :].astype(F32)
                grad = grad * cosine + pltpu.roll(grad, HD // 2, 1) * sines
                unit = proj_ref[group, 0, :, at] * factor
                sum_ref[:, at] += jnp.sum(grad * unit, axis=0, keepdims=True)
                grad = factor * (grad * gain_ref[:, at] - unit * mean)
                out_ref[group, 0, :, at] = grad.astype(BF16)
        for head in range(heads):
            at = slice((2 * heads + head) * HD, (2 * heads + head + 1) * HD)
            out_ref[group, 0, :, at] = back_refs[head][0, 2, line, :]


def norm_back_call(place, projected, stats, gains, cosine, back_sines, back):
    exp_count, seq_count, shard_len, width = projected.shape
    local_heads = width // 3 // HD
    group = math.gcd(exp_count, 4)

    def back_spec(head):
        return pl.BlockSpec(
            (1, 3, group * shard_len, HD),
            lambda s, e, p: ((s * local_heads + head) ^ p[0], 0, e, 0),
        )

    wide_spec = pl.BlockSpec((group, 1, shard_len, width), lambda s, e, p: (e, s, 0, 0))
    line_spec = pl.BlockSpec((group * shard_len, HD), lambda s, e, p: (e, 0))
    gain_spec = pl.BlockSpec((1, gains.shape[1]), lambda s, e, p: (0, 0))
    return pl.pallas_call(
        norm_back_kernel,
        grid_spec=pltpu.PrefetchScalarGridSpec(
            num_scalar_prefetch=1,
            grid=(seq_count, exp_count // group),
            in_specs=[
                wide_spec,
                pl.BlockSpec(
                    (group, 1, shard_len, stats.shape[-1]), lambda s, e, p: (e, s, 0, 0)
                ),
                gain_spec,
                line_spec,
                line_spec,
            ]
            + [back_spec(head) for head in range(local_heads)],
            out_specs=(wide_spec, gain_spec),
        ),
        out_shape=(
            jax.ShapeDtypeStruct(projected.shape, BF16),
            jax.ShapeDtypeStruct(gains.shape, F32),
        ),
        cost_estimate=SMALL,
        name="norm_back",
    )(place, projected, stats, gains, cosine, back_sines, *([back] * local_heads))


def half_signs(sines, first, second):
    half_size = sines.shape[1] // 2
    return jnp.concatenate([first * sines[:, :half_size], second * sines[:, half_size:]], axis=1)


def paired_forward(projected, query_gain, key_gain, cosine, sines, model_width, early):
    exp_count, seq_count, shard_len, width = projected.shape
    local_width = width // 3
    local_heads = local_width // HD
    ctx_rows = exp_count * shard_len
    values = projected[..., 2 * local_width :].astype(BF16)
    values = values.reshape(exp_count, seq_count, shard_len, local_heads, HD)
    v_all = spread_pairs(jnp.transpose(values, (1, 3, 0, 2, 4)).reshape(-1, ctx_rows, HD))
    squares = jnp.stack(
        [
            jnp.sum(jnp.square(projected[..., i * local_width : (i + 1) * local_width]), axis=-1)
            for i in range(2)
        ]
    )
    squares = butterfly_sum(squares, "exp")
    factors = lax.rsqrt(squares / model_width + norm_eps)
    gains = jnp.concatenate([query_gain, key_gain])[None]
    stats = jnp.stack([factors[0], factors[1]], axis=-1)
    rotated_qk = rotate_call(projected, stats, gains, cosine, half_signs(sines, -1.0, 1.0))
    qk_all = hold(spread_pairs(rotated_qk), early)
    place = lax.axis_index("ctx").astype(jnp.int32).reshape(1)
    out, out_t, lse = attend_call(place, qk_all, v_all)
    natural = jnp.stack([pick(out, place[0] ^ p) for p in range(out.shape[0])])
    natural = natural.reshape(-1, shard_len, HD)
    own = lax.all_to_all(natural, ("ctx", "exp"), split_axis=0, concat_axis=0, tiled=True)
    own = own.reshape(seq_count, local_heads, exp_count, shard_len, HD)
    own = jnp.transpose(own, (0, 3, 2, 1, 4)).reshape(seq_count * shard_len, -1)
    return (own, out), (place, qk_all, v_all, out_t, lse, projected, factors, gains)


def paired_backward(kept, grads, query_gain, key_gain, cosine, sines, model_width, early, later):
    place, qk_all, v_all, out_t, lse, projected, factors, gains = kept
    exp_count, seq_count, shard_len, width = projected.shape
    local_heads = width // 3 // HD
    grads = spread_pairs(grads, *early)
    back, sums = attend_back_call(place, qk_all, v_all, grads, out_t, lse)
    count = back.shape[0]
    parts = [flip(back[m], "ctx", m) for m in range(1, count)]
    sums = butterfly_sum(return_pairs(hold(sums, later[1])), "exp")
    during = later[0](sums)
    parts = jnp.stack([back[0]] + [hold(part, during) for part in parts])
    sums = sums.reshape(seq_count, local_heads, 2, exp_count, shard_len).sum(axis=1) / model_width
    sums = jnp.transpose(sums, (1, 2, 0, 3))
    stats = jnp.stack([factors[0], factors[1], sums[0], sums[1]], axis=-1)
    grad_qkv, gain_parts = norm_back_call(
        place, projected, stats, gains, cosine, half_signs(sines, 1.0, -1.0), parts
    )
    qgain_part, kgain_part = jnp.split(gain_parts[0], 2)
    return grad_qkv, qgain_part, kgain_part, parts


def gathered_forward(projected, query_gain, key_gain, cosine, sines, model_width, early):
    queries, keys_proj, values_low = jnp.split(projected, 3, axis=-1)
    values_low = values_low.astype(BF16)
    exp_count, seq_count, shard_len, local_width = queries.shape
    ctx_count, ctx_place = lax.axis_size("ctx"), lax.axis_index("ctx")
    local_heads = local_width // HD
    ctx_rows = exp_count * shard_len
    half_rows = ctx_rows // 2
    squares = jnp.stack(
        [jnp.sum(queries * queries, axis=-1), jnp.sum(keys_proj * keys_proj, axis=-1)]
    )
    squares = lax.psum(squares, "exp")
    factors = lax.rsqrt(squares[..., None] / model_width + norm_eps)
    query_unit = queries * factors[0]
    key_unit = keys_proj * factors[1]

    def heads(values):
        values = values.reshape(exp_count, seq_count, shard_len, local_heads, HD)
        return jnp.transpose(values, (1, 0, 2, 3, 4)).reshape(seq_count, ctx_rows, local_heads, HD)

    def rotated(values):
        values = heads(values)
        return (values * cosine[:, None, :] + turn(values) * sines[:, None, :]).astype(BF16)

    query_rot = rotated(query_unit * query_gain)
    keys_all = lax.all_gather(rotated(key_unit * key_gain), "ctx", axis=1, tiled=True)
    values_all = lax.all_gather(heads(values_low), "ctx", axis=1, tiled=True)
    tools = block_tools(half_rows, ctx_count, ctx_place)
    block_len, half_firsts, row_start, block_scores = tools
    attended_halves = []
    log_halves = []
    for half_index in range(2):
        query_half = query_rot[:, half_index * half_rows : (half_index + 1) * half_rows]
        query_first = half_firsts[half_index]
        needed_blocks = (query_first + half_rows) // block_len

        def step(counter, carried):
            running_max, running_sum, acc = carried
            key_first = counter * block_len
            start_row = row_start(key_first)
            key_block = lax.dynamic_slice_in_dim(keys_all, start_row, block_len, 1)
            value_block = lax.dynamic_slice_in_dim(values_all, start_row, block_len, 1)
            scores = block_scores(query_half, query_first, key_block, key_first)
            new_max = jnp.maximum(running_max, jnp.max(scores, axis=-1))
            fade = jnp.exp(running_max - new_max)
            probs = jnp.exp(scores - new_max[..., None])
            running_sum = running_sum * fade + jnp.sum(probs, axis=-1)
            acc = acc * jnp.transpose(fade, (0, 2, 1))[..., None] + jnp.einsum(
                "shqk,skhd->sqhd", probs.astype(BF16), value_block, preferred_element_type=F32
            )
            return (new_max, running_sum, acc)

        stat_shape = (seq_count, local_heads, half_rows)
        running_max, running_sum, acc = lax.fori_loop(
            0,
            needed_blocks,
            step,
            (
                jnp.full(stat_shape, masked_score, F32),
                jnp.zeros(stat_shape, F32),
                jnp.zeros((seq_count, half_rows, local_heads, HD), F32),
            ),
        )
        attended_halves.append(acc / jnp.transpose(running_sum, (0, 2, 1))[..., None])
        log_halves.append(running_max + jnp.log(running_sum))
    attended_float = jnp.concatenate(attended_halves, axis=1)
    attended = jnp.transpose(attended_float.astype(BF16), (0, 2, 1, 3)).reshape(-1, ctx_rows, HD)
    kept = (
        query_rot, keys_all, values_all, attended_float, log_halves, query_unit, key_unit, factors
    )
    sent = jnp.transpose(attended.reshape(-1, exp_count, shard_len, HD), (1, 0, 2, 3))
    own = lax.all_to_all(sent, "exp", split_axis=0, concat_axis=0, tiled=True)
    own = own.reshape(exp_count, seq_count, local_heads, shard_len, HD)
    own = jnp.transpose(own, (1, 3, 0, 2, 4)).reshape(seq_count * shard_len, -1)
    return (own, attended), kept


def block_tools(half_rows, ctx_count, ctx_place):
    block_len = math.gcd(half_rows, 512)
    far_first = (2 * ctx_count - 1 - ctx_place) * half_rows
    half_firsts = (ctx_place * half_rows, far_first)

    def row_start(first_pos):
        segment = first_pos // half_rows
        offset = first_pos % half_rows
        return jnp.where(
            segment < ctx_count,
            segment * 2 * half_rows + offset,
            (2 * ctx_count - 1 - segment) * 2 * half_rows + half_rows + offset,
        )

    def block_scores(query_block, query_first, key_block, key_first):
        scores = jnp.einsum("sqhd,skhd->shqk", query_block, key_block, preferred_element_type=F32)
        scores = scores * (1.0 / math.sqrt(HD))
        query_line = query_first + jnp.arange(query_block.shape[1], dtype=jnp.int32)
        key_line = key_first + jnp.arange(key_block.shape[1], dtype=jnp.int32)
        return jnp.where(key_line[None, :] <= query_line[:, None], scores, masked_score)

    return block_len, half_firsts, row_start, block_scores


def gathered_backward(
    kept, grads, query_gain, key_gain, cosine, sines, model_width, early, later
):
    query_rot, keys_all, values_all, attended_float, log_halves, query_unit, key_unit, factors = kept
    exp_count, seq_count, shard_len, local_width = query_unit.shape
    ctx_count, ctx_place = lax.axis_size("ctx"), lax.axis_index("ctx")
    local_heads = local_width // HD
    ctx_rows = exp_count * shard_len
    half_rows = ctx_rows // 2
    seq_len = keys_all.shape[1]
    score_scale = 1.0 / math.sqrt(HD)
    block_len, half_firsts, row_start, block_scores = block_tools(half_rows, ctx_count, ctx_place)
    grad_heads = jnp.transpose(
        grads.reshape(seq_count, local_heads, ctx_rows, HD), (0, 2, 1, 3)
    )
    delta_rows = jnp.transpose(jnp.sum(grad_heads.astype(F32) * attended_float, axis=-1), (0, 2, 1))
    keyval_grads = jnp.zeros((seq_count, seq_len, 2 * local_width), F32)
    query_halves = []
    for half_index in range(2):
        row_slice = slice(half_index * half_rows, (half_index + 1) * half_rows)
        query_half = query_rot[:, row_slice]
        grad_half = grad_heads[:, row_slice]
        delta_half = delta_rows[:, :, row_slice]
        log_total = log_halves[half_index]
        query_first = half_firsts[half_index]
        needed_blocks = (query_first + half_rows) // block_len

        def one_block(counter, inner):
            query_acc, keyval_acc = inner
            key_first = counter * block_len
            start_row = row_start(key_first)
            key_block = lax.dynamic_slice_in_dim(keys_all, start_row, block_len, 1)
            value_block = lax.dynamic_slice_in_dim(values_all, start_row, block_len, 1)
            scores = block_scores(query_half, query_first, key_block, key_first)
            soft_probs = jnp.exp(scores - log_total[..., None])
            grad_probs = jnp.einsum(
                "sqhd,skhd->shqk", grad_half, value_block, preferred_element_type=F32
            )
            grad_scores = (soft_probs * (grad_probs - delta_half[..., None])).astype(BF16)
            query_acc = query_acc + score_scale * jnp.einsum(
                "shqk,skhd->sqhd", grad_scores, key_block, preferred_element_type=F32
            )
            kblock_grad = score_scale * jnp.einsum(
                "shqk,sqhd->skhd", grad_scores, query_half, preferred_element_type=F32
            )
            vblock_grad = jnp.einsum(
                "shqk,sqhd->skhd", soft_probs.astype(BF16), grad_half, preferred_element_type=F32
            )
            flat = (seq_count, block_len, local_width)
            combined = jnp.concatenate([kblock_grad.reshape(flat), vblock_grad.reshape(flat)], -1)
            keyval_acc = lax.dynamic_update_slice_in_dim(
                keyval_acc,
                lax.dynamic_slice_in_dim(keyval_acc, start_row, block_len, 1) + combined,
                start_row,
                1,
            )
            return (query_acc, keyval_acc)

        query_acc, keyval_grads = lax.fori_loop(
            0,
            needed_blocks,
            one_block,
            (jnp.zeros((seq_count, half_rows, local_heads, HD), F32), keyval_grads),
        )
        query_halves.append(query_acc)
    query_back = jnp.concatenate(query_halves, axis=1)
    keyval_local = lax.psum_scatter(keyval_grads, "ctx", scatter_dimension=1, tiled=True)

    def by_row(values):
        values = values.reshape(seq_count, exp_count, shard_len, local_width)
        return jnp.transpose(values, (1, 0, 2, 3))

    def unrotated(values):
        values = values.reshape(seq_count, ctx_rows, local_heads, HD)
        return by_row(values * cosine[:, None, :] + turn_back(values) * sines[:, None, :])

    qnorm_grad = unrotated(query_back)
    knorm_grad = unrotated(keyval_local[..., :local_width])
    grad_values = by_row(keyval_local[..., local_width:].astype(BF16))
    qgain_part = jnp.sum(qnorm_grad * query_unit, axis=(0, 1, 2))
    kgain_part = jnp.sum(knorm_grad * key_unit, axis=(0, 1, 2))
    qunit_grad = qnorm_grad * query_gain
    kunit_grad = knorm_grad * key_gain
    dots = jnp.stack(
        [jnp.sum(qunit_grad * query_unit, axis=-1), jnp.sum(kunit_grad * key_unit, axis=-1)]
    )
    dots = lax.psum(dots, "exp")[..., None] / model_width
    grad_queries = (factors[0] * (qunit_grad - query_unit * dots[0])).astype(BF16)
    grad_keys = (factors[1] * (kunit_grad - key_unit * dots[1])).astype(BF16)
    later[0](grad_heads)
    grad_qkv = jnp.concatenate([grad_queries, grad_keys, grad_values], axis=-1)
    return grad_qkv, qgain_part, kgain_part, dots


NT = (((1,), (1,)), ((), ()))
TN = (((0,), (0,)), ((), ()))
EXPERT_PARAMS = pltpu.CompilerParams(vmem_limit_bytes=58 * 2**20)


def down_kernel(half_ref, rows_ref, weight_ref, out_ref):
    out_ref[0] = dot32(rows_ref[...], weight_ref[0, 0])


def down_call(rows, weights, half, width):
    count, model_width = rows.shape
    experts = weights.shape[0]
    tile, cols = math.gcd(count, 1024), math.gcd(width, 1024)
    parts = width // cols
    return pl.pallas_call(
        down_kernel,
        grid_spec=pltpu.PrefetchScalarGridSpec(
            num_scalar_prefetch=1,
            grid=(experts, parts, count // tile),
            in_specs=[
                pl.BlockSpec((tile, model_width), lambda e, f, r, h: (r, 0)),
                pl.BlockSpec(
                    (1, 1, model_width, cols), lambda e, f, r, h: (e, 2, 0, h[0] * parts + f)
                ),
            ],
            out_specs=pl.BlockSpec((1, tile, cols), lambda e, f, r, h: (e, r, f)),
        ),
        out_shape=jax.ShapeDtypeStruct((experts, count, width), F32),
        compiler_params=EXPERT_PARAMS,
        cost_estimate=SMALL,
        name="down",
    )(half, rows, weights)


def hidden_kernel(
    half_ref, rows_ref, wg_ref, wu_ref, down_ref, gate_ref, gm_ref, gg_ref, gu_ref, *dots, chunk
):
    width = wg_ref.shape[-1]

    def step(i, unused):
        at = pl.ds(pl.multiple_of(i * chunk, chunk), chunk)
        rows = rows_ref[at, :]
        pre_gate = dot32(rows, wg_ref[0, 0])
        pre_up = dot32(rows, wu_ref[0, 0])
        down, gate = down_ref[0, at, :], gate_ref[0, at, :]
        sigmoid_vals = 1.0 / (1.0 + jnp.exp(-pre_gate))
        activated = pre_gate * sigmoid_vals
        middle = activated * pre_up
        for dot_ref in dots:
            products = middle * down
            acc = products[:, :128]
            for c in range(1, width // 128):
                acc = acc + products[:, c * 128 : (c + 1) * 128]
            dot_ref[0, 0, at, :] = acc
        gm_ref[0, at, :] = (gate * middle).astype(BF16)
        grad = gate * down
        gu_ref[0, at, :] = (grad * activated).astype(BF16)
        slope = sigmoid_vals * (1.0 + pre_gate * (1.0 - sigmoid_vals))
        gg_ref[0, at, :] = (grad * pre_up * slope).astype(BF16)
        return unused

    lax.fori_loop(0, rows_ref.shape[0] // chunk, step, 0)


def hidden_call(rows, weights, down, gates, half, with_dots):
    count, model_width = rows.shape
    experts, width = weights.shape[0], down.shape[-1]
    tile, cols = math.gcd(count, 1024), math.gcd(width, 512)
    parts = width // cols
    wide = pl.BlockSpec((1, tile, cols), lambda e, f, r, h: (e, r, f))
    shape = jax.ShapeDtypeStruct((experts, count, width), BF16)
    out_specs, out_shape = [wide] * 3, [shape] * 3
    if with_dots:
        out_specs.append(pl.BlockSpec((1, 1, tile, 128), lambda e, f, r, h: (e, f, r, 0)))
        out_shape.append(jax.ShapeDtypeStruct((experts, parts, count, 128), F32))

    def weight_spec(which):
        return pl.BlockSpec(
            (1, 1, model_width, cols), lambda e, f, r, h: (e, which, 0, h[0] * parts + f)
        )

    return pl.pallas_call(
        functools.partial(hidden_kernel, chunk=math.gcd(tile, 256)),
        grid_spec=pltpu.PrefetchScalarGridSpec(
            num_scalar_prefetch=1,
            grid=(experts, parts, count // tile),
            in_specs=[
                pl.BlockSpec((tile, model_width), lambda e, f, r, h: (r, 0)),
                weight_spec(0),
                weight_spec(1),
                wide,
                pl.BlockSpec((1, tile, 1), lambda e, f, r, h: (e, r, 0)),
            ],
            out_specs=out_specs,
        ),
        out_shape=out_shape,
        compiler_params=EXPERT_PARAMS,
        cost_estimate=SMALL,
        name="hidden",
    )(half, rows, weights, weights, down, gates)


def back_kernel(*refs, count, chunk):
    a_refs, b_refs, out_ref, acc_ref = refs[:count], refs[count : 2 * count], refs[-2], refs[-1]
    turn_at = pl.program_id(2)

    def step(i, unused):
        at = pl.ds(pl.multiple_of(i * chunk, chunk), chunk)
        total = None
        for a, b in zip(a_refs, b_refs):
            term = lax.dot_general(a[0, at, :], b[0, 0], NT, preferred_element_type=F32)
            total = term if total is None else total + term

        @pl.when(turn_at == 0)
        def first():
            acc_ref[at, :] = total

        @pl.when(turn_at > 0)
        def later():
            acc_ref[at, :] += total

        return unused

    lax.fori_loop(0, out_ref.shape[0] // chunk, step, 0)

    @pl.when(turn_at == pl.num_programs(2) - 1)
    def last():
        out_ref[...] = acc_ref[...].astype(out_ref.dtype)


def back_call(parts, weights, which, kind=BF16, *after, cost=SMALL):
    experts, count, width = parts[0].shape
    model_width = weights.shape[2]
    tile, cols = math.gcd(count, 512), math.gcd(model_width, 2048)

    def weight_spec(k):
        return pl.BlockSpec((1, 1, cols, width), lambda d, r, e: (e, k, d, 0))

    return pl.pallas_call(
        functools.partial(back_kernel, count=len(parts), chunk=math.gcd(tile, 256)),
        grid=(model_width // cols, count // tile, experts),
        in_specs=[pl.BlockSpec((1, tile, width), lambda d, r, e: (e, r, 0))] * len(parts)
        + [weight_spec(k) for k in which]
        + [pl.BlockSpec(memory_space=pl.ANY)] * len(after),
        out_specs=pl.BlockSpec((tile, cols), lambda d, r, e: (r, d)),
        out_shape=jax.ShapeDtypeStruct((count, model_width), kind),
        scratch_shapes=[pltpu.VMEM((tile, cols), F32)],
        compiler_params=EXPERT_PARAMS,
        cost_estimate=cost,
        name="back",
    )(*parts, *([weights] * len(parts)), *after)


def grad_kernel(half_ref, own_rows, own_grads, near_rows, near_grads, *refs):
    total = lax.dot_general(own_rows[...], own_grads[0], TN, preferred_element_type=F32)
    total += lax.dot_general(near_rows[...], near_grads[0], TN, preferred_element_type=F32)
    refs[-1][...] = total.astype(BF16)


def grad_call(own_rows, own_grads, near_rows, near_grads, half, *after):
    count, model_width = own_rows.shape
    experts, _, width = near_grads.shape
    shards = lax.axis_size("ctx")
    cols = math.gcd(model_width // shards, 512)
    tiles = model_width // shards // cols
    row_spec = pl.BlockSpec((count, cols), lambda e, d, h: (0, d))

    def scatter_order(tile, half):
        shard = tile // tiles
        apart = jnp.where(half == 0, shard, shards - 1 - shard)
        near = apart < shards // 2
        step = jnp.where(half == 0, shard, shard - shards // 2)
        step = jnp.where(near, step, jnp.where(half == 0, shards - 1 - shard, shards // 2 - 1 - shard))
        return (2 * step + jnp.where(near, 0, 1)) * tiles + tile % tiles

    return pl.pallas_call(
        grad_kernel,
        grid_spec=pltpu.PrefetchScalarGridSpec(
            num_scalar_prefetch=1,
            grid=(experts, model_width // cols),
            in_specs=[
                row_spec,
                pl.BlockSpec((1, count, width), lambda e, d, h: (e, 0, h[0])),
                row_spec,
                pl.BlockSpec((1, count, width), lambda e, d, h: (e, 0, 0)),
            ]
            + [pl.BlockSpec(memory_space=pl.ANY)] * len(after),
            out_specs=pl.BlockSpec(
                (cols, width), lambda e, d, h: (scatter_order(d, h[0]), e)
            ),
        ),
        out_shape=jax.ShapeDtypeStruct((model_width, experts * width), BF16),
        compiler_params=EXPERT_PARAMS,
        cost_estimate=SMALL,
        name="grad",
    )(half, own_rows, own_grads, near_rows, near_grads, *after)


def scatter_rows(term):
    count = lax.axis_size("ctx")
    groups = [list(range(count // 2)), list(range(count // 2, count))]
    return lax.psum_scatter(
        term, "ctx", scatter_dimension=0, axis_index_groups=groups, tiled=True
    )


def swap_rows(term):
    size = term.shape[0] // 2
    return flip(term[size:], "ctx", lax.axis_size("ctx") - 1), term[:size]


def body(
    block_input,
    attend_gain,
    w_query,
    w_key,
    w_value,
    w_out,
    query_gain,
    key_gain,
    expert_gain,
    router,
    expert_weights,
    routes,
    cotangent,
):
    exp_count, ctx_count = lax.axis_size("exp"), lax.axis_size("ctx")
    ctx_place, exp_place = lax.axis_index("ctx"), lax.axis_index("exp")
    seq_count, shard_len, model_width = block_input.shape
    local_width = w_query.shape[1]
    local_heads = local_width // HD
    experts_all = router.shape[1]
    experts_here = expert_weights.shape[1]
    hidden_units = expert_weights.shape[3]
    rows_dev = seq_count * shard_len
    rows_all = exp_count * rows_dev
    ctx_rows = exp_count * shard_len
    half_rows = ctx_rows // 2
    pair_count = seq_count * local_heads
    paired = pair_count == ctx_count and half_rows % 128 == 0

    def gather(values):
        return lax.all_gather(values, "exp", axis=0, tiled=False)

    mirror = ctx_count - 1
    half = (ctx_place * 2 // ctx_count).astype(jnp.int32).reshape(1)
    whole = jnp.zeros((1,), jnp.int32)
    local_float = block_input.astype(F32).reshape(rows_dev, model_width)
    local_factor = rms_factor(local_float)
    local_unit = local_float * local_factor
    normed = gather((local_unit * attend_gain).astype(BF16)).reshape(rows_all, model_width)
    weights = jnp.transpose(expert_weights, (1, 2, 0, 3))
    w_qkv = jnp.concatenate([w_query, w_key, w_value], axis=1)
    own_routes = jnp.transpose(routes, (1, 0, 2)).reshape(rows_dev, TOP)
    own_grads = cotangent.reshape(rows_dev, model_width)
    grad_low = gather(own_grads).reshape(rows_all, model_width)
    full_out = gather(w_out).reshape(exp_count * local_width, model_width)
    near_low = gather(hold(flip(own_grads, "ctx", mirror), weights)).reshape(rows_all, model_width)
    all_routes = gather(own_routes).reshape(rows_all, TOP)
    near_routes = flip(all_routes, "ctx", mirror)
    w_qkv = hold(w_qkv, weights, near_routes)
    grad_down = down_call(grad_low, weights, whole, hidden_units)
    near_down = down_call(near_low, weights, half, hidden_units // 2)

    projected = dot32(normed, w_qkv).reshape(exp_count, seq_count, shard_len, 3 * local_width)
    row_ids = jnp.arange(ctx_rows, dtype=jnp.int32)
    far_first = (2 * ctx_count - 1 - ctx_place) * half_rows
    query_pos = jnp.where(
        row_ids < half_rows, ctx_place * half_rows + row_ids, far_first + row_ids - half_rows
    )
    cosine, sines = rotary_tables(query_pos, HD)
    forward, backward = (
        (paired_forward, paired_backward) if paired else (gathered_forward, gathered_backward)
    )
    (own_attended, attended), kept = forward(
        projected, query_gain, key_gain, cosine, sines, model_width, grad_down
    )

    def exchange(values):
        return lax.all_to_all(values, "exp", split_axis=0, concat_axis=0, tiled=True)

    hidden = local_float + dot32(own_attended, full_out)
    hidden_factor = rms_factor(hidden)
    unit_second = hidden * hidden_factor
    own_mixed = (unit_second * expert_gain).astype(BF16)

    expert_ids = jnp.arange(experts_all, dtype=jnp.int32)

    def chosen(table):
        return jnp.any(table[:, :, None] == expert_ids[None, None, :], axis=1)

    own_prob = jax.nn.softmax(dot32(own_mixed, router), axis=-1)

    def local_gates(rows, table):
        prob = jax.nn.softmax(dot32(rows, router), axis=-1)
        gates = jnp.where(chosen(table), prob, 0.0)
        gates = lax.dynamic_slice_in_dim(gates, exp_place * experts_here, experts_here, 1)
        return jnp.transpose(gates)[:, :, None]

    mixed = hold(gather(own_mixed).reshape(rows_all, model_width), near_down)
    near_mixed = gather(hold(flip(own_mixed, "ctx", mirror), near_down))
    gates = local_gates(mixed, all_routes)

    gated_middle, grad_gate, grad_up, dots = hidden_call(
        mixed, weights, grad_down, gates, whole, True
    )
    gate_grads = jnp.sum(dots, axis=(1, 3))
    choice_grad = exchange(
        jnp.transpose(gate_grads.reshape(experts_here, exp_count, rows_dev), (1, 0, 2))
    )
    slot_rows = back_call([grad_gate, grad_up], weights, (0, 1), BF16)
    if paired:
        attended = return_pairs(hold(attended, gated_middle))
    slot_both, slot_own = reduce_start(slot_rows.reshape(exp_count, rows_dev, model_width))
    slot_parts = reduce_send(slot_both)
    near_mixed = hold(
        near_mixed.reshape(rows_all, model_width), slot_both, choice_grad
    )
    near_gates = local_gates(near_mixed, near_routes)
    near_middle, near_grad_gate, near_grad_up = hidden_call(
        near_mixed, weights, near_down, near_gates, half, False
    )

    down_term = grad_call(
        grad_low, gated_middle, near_low, near_middle, half, attended, *slot_parts
    )
    slot_sum = reduce_total(slot_parts, slot_own)

    choice_grad = jnp.transpose(choice_grad, (2, 0, 1)).reshape(rows_dev, experts_all)
    choice_grad = jnp.where(chosen(own_routes), choice_grad, 0.0)
    logit_grad = (
        own_prob * (choice_grad - jnp.sum(own_prob * choice_grad, axis=-1, keepdims=True))
    ).astype(BF16)
    router_part = jnp.einsum("td,te->de", own_mixed, logit_grad, preferred_element_type=F32)
    mixed_grad = slot_sum + jnp.einsum(
        "te,de->td", logit_grad, router, preferred_element_type=F32
    )
    egain_part = jnp.sum(mixed_grad * unit_second, axis=0)
    usecond_grad = mixed_grad * expert_gain
    grad_rows = cotangent.astype(F32).reshape(rows_dev, model_width)
    grad_hidden = (
        hidden_factor
        * (usecond_grad - unit_second * jnp.mean(usecond_grad * unit_second, axis=-1, keepdims=True))
        + grad_rows
    )
    own_branch = grad_hidden.astype(BF16)
    early_part = jnp.concatenate([router_part, egain_part[:, None]], axis=1)
    early_part = exchange(early_part.reshape(exp_count, -1, experts_all + 1))

    grad_attended = jnp.einsum(
        "rd,hd->rh", own_branch, full_out, preferred_element_type=F32
    ).astype(BF16)
    sent = grad_attended.reshape(seq_count, shard_len, exp_count, local_heads, HD)
    sent = jnp.transpose(sent, (2, 0, 3, 1, 4)).reshape(exp_count, pair_count, shard_len, HD)
    grads = jnp.transpose(exchange(sent), (1, 0, 2, 3)).reshape(pair_count, ctx_rows, HD)
    gate_term = grad_call(mixed, grad_gate, near_mixed, near_grad_gate, half, grads)
    down_sum, gate_sum = scatter_rows(down_term), scatter_rows(gate_term)
    def place_rows(whole_grad, halves, which, *after):
        sent_rows, kept_rows = halves
        sent_rows = hold(sent_rows, *after)
        lower = jnp.where(half[0] == 0, kept_rows, sent_rows)
        upper = jnp.where(half[0] == 0, sent_rows, kept_rows)
        parts = [
            v.astype(F32).reshape(-1, experts_here, hidden_units // 2) for v in (lower, upper)
        ]
        part = jnp.concatenate(parts, axis=-1)[:, None]
        return lax.dynamic_update_slice_in_dim(whole_grad, part, which, 1)

    down_swapped = swap_rows(hold(down_sum, grads))
    branch_rows = gather(hold(own_branch, gate_term))
    late_terms = []

    def meanwhile(sums):
        up_term = grad_call(
            mixed, grad_up, near_mixed, near_grad_up, half, sums
        )
        up_sum = scatter_rows(up_term)
        cost = pl.CostEstimate(
            flops=16 * rows_all * model_width * experts_here * hidden_units,
            bytes_accessed=0,
            transcendentals=0,
        )
        expert_out = back_call([gated_middle], weights, (2,), BF16, up_term, cost=cost)
        late_terms.append((up_sum, expert_out))
        return expert_out

    grad_qkv, qgain_part, kgain_part, ended = backward(
        kept, grads, query_gain, key_gain, cosine, sines, model_width, (gate_term, early_part), (meanwhile, down_swapped[0])
    )
    attended_rows = attended.reshape(seq_count, local_heads, exp_count, shard_len, HD)
    up_sum, expert_out = late_terms[0]
    early_sum = jnp.sum(early_part, axis=0)
    gain_parts = [v[:, None] for v in (qgain_part, kgain_part)]
    sums = butterfly_sum(jnp.concatenate([early_sum] + gain_parts, axis=1), "ctx")
    gate_swapped = swap_rows(hold(gate_sum, sums))
    grad_qkv = hold(grad_qkv, gate_swapped[0], up_sum)
    branch_rows = hold(branch_rows, ended)
    branch_rows = branch_rows.reshape(exp_count, seq_count, shard_len, model_width)
    outw_part = jnp.einsum(
        "shetc,estd->dhc", attended_rows, branch_rows, preferred_element_type=F32
    ).reshape(model_width, local_width)
    qkv_part = jnp.einsum(
        "rd,rh->dh", normed, grad_qkv.reshape(rows_all, -1), preferred_element_type=F32
    )
    proj_part = jnp.concatenate([qkv_part.astype(BF16), outw_part.astype(BF16)], axis=1)
    proj_sum = lax.psum_scatter(proj_part, "ctx", scatter_dimension=0, tiled=True)

    w_qkv = jnp.concatenate([w_query, w_key, w_value], axis=1)
    grad_rows_qkv = grad_qkv.reshape(1, rows_all, -1)
    normed_back = back_call(
        [grad_rows_qkv], w_qkv[None, None], (0,), BF16, proj_part
    )
    normed_both, normed_own = reduce_start(normed_back.reshape(exp_count, rows_dev, model_width))
    normed_parts = reduce_send(normed_both)
    up_swapped = swap_rows(hold(up_sum, proj_part))
    grad_normed = reduce_total(normed_parts, normed_own, up_swapped[0])
    attend_part = jnp.sum(grad_normed * local_unit, axis=0)
    attend_sum = jnp.sum(exchange(attend_part.reshape(exp_count, -1)), axis=0)
    attend_high = attend_sum.astype(BF16)
    attend_low = (attend_sum - attend_high.astype(F32)).astype(BF16)
    ends = jnp.concatenate([attend_high, attend_low])[None]
    ends = jnp.pad(ends, ((0, 15), (0, proj_sum.shape[1] - ends.shape[1])))
    proj_all = lax.all_gather(jnp.concatenate([proj_sum, ends]), "ctx", axis=0, tiled=False)
    lunit_grad = grad_normed * attend_gain
    input_grad = grad_hidden + local_factor * (
        lunit_grad - local_unit * jnp.mean(lunit_grad * local_unit, axis=-1, keepdims=True)
    )
    expert_grad = jnp.zeros((model_width // ctx_count, 3, experts_here, hidden_units), F32)
    expert_grad = place_rows(expert_grad, down_swapped, 2, normed_both)
    expert_grad = place_rows(expert_grad, gate_swapped, 0, normed_both)
    expert_grad = place_rows(expert_grad, up_swapped, 1, grad_normed)
    produced = hold(expert_out, normed_both).reshape(exp_count, rows_dev, model_width)
    mixture = reduce_finish(*reduce_start(produced), grad_normed)
    block_output = (hidden + mixture).astype(BF16).reshape(block_input.shape)

    proj_all = hold(proj_all, input_grad, block_output, expert_grad)
    shard_rows = proj_sum.shape[0]
    proj_grad = proj_all[:, :shard_rows].reshape(model_width, -1).astype(F32)
    ends = proj_all[:, shard_rows, : 2 * attend_sum.shape[0]].astype(F32)
    attend_grad = jnp.sum(ends.reshape(ctx_count, 2, -1), axis=(0, 1))
    grads_of = [proj_grad[:, i * local_width : (i + 1) * local_width] for i in range(4)]
    return (
        block_output,
        input_grad.reshape(block_input.shape),
        attend_grad,
        *grads_of[:3],
        grads_of[3].T,
        sums[:, experts_all + 1],
        sums[:, experts_all + 2],
        sums[:, experts_all],
        sums[:, :experts_all],
        jnp.transpose(expert_grad, (0, 2, 1, 3)),
    )


def solution(mesh):
    placed = (
        P(None, ("ctx", "exp"), None),
        P(),
        P(None, "exp"),
        P(None, "exp"),
        P(None, "exp"),
        P("exp", None),
        P("exp"),
        P("exp"),
        P(),
        P(),
        P(None, "exp", None, None),
        P(("ctx", "exp"), None, None),
        P(None, ("ctx", "exp"), None),
    )
    return jax.shard_map(
        body,
        mesh=mesh,
        in_specs=placed,
        out_specs=(
            P(None, ("ctx", "exp"), None),
            P(None, ("ctx", "exp"), None),
            P("exp"),
            P(None, "exp"),
            P(None, "exp"),
            P(None, "exp"),
            P("exp", None),
            P("exp"),
            P("exp"),
            P("exp"),
            P("exp", None),
            P("ctx", "exp", None, None),
        ),
        check_vma=False,
    )
```
